32 devices in a mesh: fsdp: 8 (over y, x, core), ctx: 4 (over z).
Axes of the slice: x: 2, y: 2, z: 4, core: 2. Of those that a mesh axis runs over, the one named last changes fastest.
Arguments:
- hidden_in: bfloat16 [8, 1024, 2048], P('fsdp', 'ctx'), may hold values from -6 to 6
- w_mix: bfloat16 [1, 2048, 8192], P(None, 'fsdp'), may hold values from -0.125 to 0.125
- w_dt: bfloat16 [1, 2048, 48], P(None, 'fsdp'), may hold values from -0.25 to 0.25
- w_attn_out: bfloat16 [1, 2048, 1024], P(None, 'fsdp'), may hold values from -1.5 to 1.5
- w_ssm_out: bfloat16 [1, 2048, 3072], P(None, 'fsdp'), may hold values from -0.109375 to 0.109375
- w_gate: bfloat16 [1, 2048, 4096], P(None, 'fsdp'), may hold values from -0.125 to 0.125
- w_up: bfloat16 [1, 2048, 4096], P(None, 'fsdp'), may hold values from -0.125 to 0.125
- w_down: bfloat16 [1, 2048, 4096], P(None, 'fsdp'), may hold values from -0.09375 to 0.09375
- norm_gains: float32 [1, 2, 2048], replicated, may hold values from 0.5 to 1.5
- dt_bias: float32 [1, 48], replicated, as said below
- a_log: float32 [1, 48], replicated, may hold values from -0.7 to 1.5
- skip_scale: float32 [1, 48], replicated, may hold values from 0.5 to 1.5
- cotangent: bfloat16 [8, 1024, 2048], P('fsdp', 'ctx'), may hold values from -6 to 6
Outputs:
- hidden_out: bfloat16 [8, 1024, 2048], P('fsdp', 'ctx')
- grad_hidden: float32 [8, 1024, 2048], P('fsdp', 'ctx')
- grad_w_mix: float32 [1, 2048, 8192], P(None, 'fsdp')
- grad_w_dt: float32 [1, 2048, 48], P(None, 'fsdp')
- grad_w_attn_out: float32 [1, 2048, 1024], P(None, 'fsdp')
- grad_w_ssm_out: float32 [1, 2048, 3072], P(None, 'fsdp')
- grad_w_gate: float32 [1, 2048, 4096], P(None, 'fsdp')
- grad_w_up: float32 [1, 2048, 4096], P(None, 'fsdp')
- grad_w_down: float32 [1, 2048, 4096], P(None, 'fsdp')
- grad_norm_gains: float32 [1, 2, 2048], replicated
- grad_dt_bias: float32 [1, 48], replicated
- grad_a_log: float32 [1, 48], replicated
- grad_skip_scale: float32 [1, 48], replicated
The draws below stay inside these ranges and needn't reach their ends.
Inputs may be any that keep to these rules, and one draw needn't show every extreme that they name: `dt_bias`: offsets lie between -ln(1024) - 4.5 and -ln(1024) - 0.5.
All inputs are finite; a program needn't handle non-finite values.
Results may differ from the reference program's by a relative error of at most 0.03.
Values may be sent and summed in bfloat16 or wider, within the bound.
No kernel may reach another device: no remote copies, remote signals or barrier semaphores. Data moves between devices by JAX's collectives and lax.ppermute only.
A program may use at most 704 MiB of HBM per device.

```python
import math
import jax
import jax.numpy as jnp
from jax import lax

D = 2048
FF = 4096
QUERY_HEADS = 8
KEY_VALUE_HEADS = 2
HEAD_SIZE = 128
MIXER_HEADS = 48
MIXER_HEAD_SIZE = 64
STATE_SIZE = 256
TOKEN_LENGTH = 1024
LAYERS = 1
LOC = 256
BATCH = 8
MIXW = 8192
N_CTX = 4


def draw_dt_bias(key, part):
    key = jax.random.fold_in(key, 11)
    centre = -math.log(TOKEN_LENGTH)
    return jax.random.uniform(key, (LAYERS, MIXER_HEADS), jnp.float32, centre - 4.5, centre - 0.5)


def shard_levels(own_key, shape, cuts, smallest, top_value):
    def one(axis_at, parts):
        steps = jax.random.uniform(jax.random.fold_in(jax.random.fold_in(own_key, 6), axis_at), (parts,), jnp.float32, smallest / len(cuts), top_value / len(cuts))
        return jnp.repeat(jnp.exp(steps), shape[axis_at] // parts).reshape((-1,) + (1,) * (len(shape) - axis_at - 1))

    gain = one(*cuts[0])
    for cut in cuts[1:]:
        gain = gain * one(*cut)
    return gain


def scatter_about(rng, dims, spread, bound, pieces=(), kind=jnp.bfloat16):
    drawn = spread * jax.random.normal(rng, dims, jnp.float32)
    if pieces:
        drawn = drawn * shard_levels(rng, dims, pieces, -0.22, 0.18)
    return jnp.clip(drawn, -bound, bound).astype(kind)


def setup_inputs(seed: int = 0) -> dict:
    streams_of = jax.random.split(jax.random.key(seed), 14)
    hidden_in = scatter_about(streams_of[0], (BATCH, TOKEN_LENGTH, D), 1.0, 6.0, ((0, 8), (1, 4)))
    w_mix = scatter_about(streams_of[1], (LAYERS, D, MIXW), D ** -0.5, 0.125, ((1, 8),))
    w_dt = scatter_about(streams_of[2], (LAYERS, D, MIXER_HEADS), (D // 4) ** -0.5, 0.25, ((1, 8),))
    w_attn_out = scatter_about(streams_of[3], (LAYERS, D, QUERY_HEADS * HEAD_SIZE), (QUERY_HEADS * HEAD_SIZE // 64) ** -0.5, 1.5, ((1, 8),))
    w_ssm_out = scatter_about(streams_of[4], (LAYERS, D, MIXER_HEADS * MIXER_HEAD_SIZE), (MIXER_HEADS * MIXER_HEAD_SIZE) ** -0.5, 0.109375, ((1, 8),))
    w_gate = scatter_about(streams_of[5], (LAYERS, D, FF), D ** -0.5, 0.125, ((1, 8),))
    w_up = scatter_about(streams_of[6], (LAYERS, D, FF), D ** -0.5, 0.125, ((1, 8),))
    w_down = scatter_about(streams_of[7], (LAYERS, D, FF), FF ** -0.5, 0.09375, ((1, 8),))
    norm_gains = jnp.clip(1.0 + 0.1 * jax.random.normal(streams_of[8], (LAYERS, 2, D), jnp.float32), 0.5, 1.5)
    dt_bias = draw_dt_bias(jax.random.fold_in(streams_of[13], 71), 0)
    a_log = jnp.clip(jax.random.uniform(streams_of[10], (LAYERS, MIXER_HEADS), jnp.float32, -0.7, 1.5), -0.7, 1.5)
    skip_scale = jnp.clip(jax.random.uniform(streams_of[11], (LAYERS, MIXER_HEADS), jnp.float32, 0.5, 1.5), 0.5, 1.5)
    cotangent = scatter_about(streams_of[12], (BATCH, TOKEN_LENGTH, D), 1.0, 6.0, ((0, 8), (1, 4)))
    return {"hidden_in": hidden_in, "w_mix": w_mix, "w_dt": w_dt, "w_attn_out": w_attn_out, "w_ssm_out": w_ssm_out, "w_gate": w_gate, "w_up": w_up, "w_down": w_down, "norm_gains": norm_gains, "dt_bias": dt_bias, "a_log": a_log, "skip_scale": skip_scale, "cotangent": cotangent}


EPSILON = 1e-05
THETA = 10000.0
EXACT_PRECISION = lax.Precision.HIGHEST

@jax.custom_vjp
def lower_precision(v):
    return lax.optimization_barrier(v.astype(jnp.bfloat16)).astype(jnp.float32)

@jax.custom_vjp
def lower_precision_back(v):
    return v

def low_keep(v):
    return (lower_precision(v), None)

def low_pass(kept, grad):
    return (grad,)

def back_keep(v):
    return (v, None)

def back_low(kept, grad):
    return (lower_precision(grad),)
lower_precision.defvjp(low_keep, low_pass)
lower_precision_back.defvjp(back_keep, back_low)

def rotary_embed(vectors, token_positions):
    half_dim = vectors.shape[-1] // 2
    frequency = THETA ** (-jnp.arange(half_dim, dtype=jnp.float32) / half_dim)
    angles = token_positions[:, None] * frequency[None, :]
    cosine = jnp.cos(angles)[:, None, :]
    sine_part = jnp.sin(angles)[:, None, :]
    first_half = vectors[..., :half_dim]
    second_half = vectors[..., half_dim:]
    return jnp.concatenate([first_half * cosine - second_half * sine_part, second_half * cosine + first_half * sine_part], axis=-1)

def rms_scale(vectors, gain_row):
    return vectors * lax.rsqrt(lax.optimization_barrier(jnp.mean(vectors * vectors, axis=-1, keepdims=True)) + EPSILON) * gain_row

def decay_terms(dt_raw, dt_offset, log_rate):
    step_size = jax.nn.softplus(dt_raw + dt_offset)
    level = jnp.cumsum(step_size * -jnp.exp(log_rate), axis=1)
    return (step_size, level)

def within_block(inputs, b_rows, c_rows, step_size, level):
    length_here = inputs.shape[1]
    order = jnp.arange(length_here)
    causal = (order[:, None] >= order[None, :])[None, None]
    level_head = jnp.swapaxes(level, 1, 2)
    gap_level = jnp.where(causal, level_head[:, :, :, None] - level_head[:, :, None, :], 0.0)
    fading = jnp.where(causal, jnp.exp(gap_level), 0.0)
    pairing = jnp.einsum('btn,bsn->bts', c_rows, b_rows, precision=EXACT_PRECISION)
    mixing = fading * pairing[:, None] * jnp.swapaxes(step_size, 1, 2)[:, :, None, :]
    output = jnp.einsum('bhts,bshp->bthp', mixing, inputs, precision=EXACT_PRECISION)
    weight_tail = jnp.exp(level[:, -1:, :] - level) * step_size
    fresh_state = jnp.einsum('bsh,bshp,bsn->bhpn', weight_tail, inputs, b_rows, precision=EXACT_PRECISION)
    return (output, fresh_state, jnp.exp(level[:, -1, :]))

def from_state(c_rows, level, start_state):
    return jnp.exp(level)[..., None] * jnp.einsum('btn,bhpn->bthp', c_rows, start_state, precision=EXACT_PRECISION)

def split_mixed(mixed_cols):
    shape_extents = [QUERY_HEADS * HEAD_SIZE, KEY_VALUE_HEADS * HEAD_SIZE, KEY_VALUE_HEADS * HEAD_SIZE, MIXER_HEADS * MIXER_HEAD_SIZE, MIXER_HEADS * MIXER_HEAD_SIZE, STATE_SIZE, STATE_SIZE]
    split_pieces = []
    offset = 0
    for extent in shape_extents:
        split_pieces.append(mixed_cols[..., offset:offset + extent])
        offset = offset + extent
    return split_pieces

def attend(triple):
    query_rows, rows_of_key, value_vectors = triple
    group_extent = QUERY_HEADS // KEY_VALUE_HEADS
    query_grouped = query_rows.reshape(TOKEN_LENGTH, KEY_VALUE_HEADS, group_extent, HEAD_SIZE)
    unscaled_scores = lower_precision_back(jnp.einsum('eqnw,lqw->qnel', query_grouped, rows_of_key, precision=EXACT_PRECISION))
    order = jnp.arange(TOKEN_LENGTH)
    visible = order[:, None] >= order[None, :]
    logits = jnp.where(visible, unscaled_scores / math.sqrt(HEAD_SIZE), -1e+30)
    weight_set = jax.nn.softmax(logits, axis=-1)
    mixer_output = jnp.einsum('xwvz,zxy->vxwy', lower_precision(weight_set), value_vectors, precision=EXACT_PRECISION)
    return mixer_output.reshape(TOKEN_LENGTH, QUERY_HEADS * HEAD_SIZE)

def scan_blocks(ssm_in, b_rows, c_rows, dt_raw, dt_offset, log_rate):
    batch_extent = ssm_in.shape[0]

    def to_blocks(array):
        return jnp.moveaxis(array.reshape((batch_extent, N_CTX, LOC) + array.shape[2:]), 1, 0)

    def advance(carried, split_pieces):
        x_block, b_block, c_block, dt_block = split_pieces
        step_size, level = decay_terms(dt_block, dt_offset, log_rate)
        inside, fresh_state, block_decay = within_block(x_block, b_block, c_block, step_size, level)
        output = inside + from_state(c_block, level, carried)
        return (block_decay[:, :, None, None] * carried + fresh_state, output)
    start_state = jnp.zeros((batch_extent, MIXER_HEADS, MIXER_HEAD_SIZE, STATE_SIZE), jnp.float32)
    _, outputs = lax.scan(jax.checkpoint(advance), start_state, (to_blocks(ssm_in), to_blocks(b_rows), to_blocks(c_rows), to_blocks(dt_raw)))
    return jnp.moveaxis(outputs, 0, 1).reshape(batch_extent, TOKEN_LENGTH, MIXER_HEADS, MIXER_HEAD_SIZE)

def block(state, w_mix, w_dt, w_attn_out, w_ssm_out, w_gate, w_up, w_down, gain_pair, dt_bias, a_log, skip_scale):
    batch_extent = state.shape[0]
    normed = lower_precision(rms_scale(state, gain_pair[0]))
    mixed_cols = lower_precision_back(jnp.dot(normed, w_mix, precision=EXACT_PRECISION))
    dt_raw = lower_precision_back(jnp.dot(normed, w_dt, precision=EXACT_PRECISION))
    q_part, key_piece, value_piece, z_part, x_part, b_part, c_part = split_mixed(mixed_cols)
    token_positions = jnp.arange(TOKEN_LENGTH, dtype=jnp.float32)
    query_rows = lower_precision(rotary_embed(q_part.reshape(batch_extent, TOKEN_LENGTH, QUERY_HEADS, HEAD_SIZE), token_positions))
    rows_of_key = lower_precision(rotary_embed(key_piece.reshape(batch_extent, TOKEN_LENGTH, KEY_VALUE_HEADS, HEAD_SIZE), token_positions))
    value_vectors = lower_precision(value_piece.reshape(batch_extent, TOKEN_LENGTH, KEY_VALUE_HEADS, HEAD_SIZE))
    attended = lax.map(jax.checkpoint(attend), (query_rows, rows_of_key, value_vectors))
    attended = lower_precision(lower_precision_back(attended))
    ssm_in = x_part.reshape(batch_extent, TOKEN_LENGTH, MIXER_HEADS, MIXER_HEAD_SIZE)
    ssm_y = scan_blocks(ssm_in, b_part, c_part, dt_raw, dt_bias, a_log)
    full_y = ssm_y + skip_scale[:, None] * ssm_in
    z_rows = z_part.reshape(batch_extent, TOKEN_LENGTH, MIXER_HEADS, MIXER_HEAD_SIZE)
    gated_rows = lower_precision((full_y * jax.nn.silu(z_rows)).reshape(batch_extent, TOKEN_LENGTH, MIXER_HEADS * MIXER_HEAD_SIZE))
    branch = lower_precision_back(jnp.dot(attended, w_attn_out.T, precision=EXACT_PRECISION) + jnp.dot(gated_rows, w_ssm_out.T, precision=EXACT_PRECISION))
    middle = state + branch
    normed_ffn = lower_precision(rms_scale(middle, gain_pair[1]))
    gate_rows = lower_precision_back(jnp.dot(normed_ffn, w_gate, precision=EXACT_PRECISION))
    up_rows = lower_precision_back(jnp.dot(normed_ffn, w_up, precision=EXACT_PRECISION))
    activated = lower_precision(jax.nn.silu(gate_rows) * up_rows)
    return middle + lower_precision_back(jnp.dot(activated, w_down.T, precision=EXACT_PRECISION))

def forward(state, w_mix, w_dt, w_attn_out, w_ssm_out, w_gate, w_up, w_down, norm_gains, dt_bias, a_log, skip_scale):
    for layer_no in range(LAYERS):
        state = block(state, w_mix[layer_no], w_dt[layer_no], w_attn_out[layer_no], w_ssm_out[layer_no], w_gate[layer_no], w_up[layer_no], w_down[layer_no], norm_gains[layer_no], dt_bias[layer_no], a_log[layer_no], skip_scale[layer_no])
    return state

def reference(hidden_in, w_mix, w_dt, w_attn_out, w_ssm_out, w_gate, w_up, w_down, norm_gains, dt_bias, a_log, skip_scale, cotangent):
    result, pullback = jax.vjp(forward, hidden_in.astype(jnp.float32), w_mix.astype(jnp.float32), w_dt.astype(jnp.float32), w_attn_out.astype(jnp.float32), w_ssm_out.astype(jnp.float32), w_gate.astype(jnp.float32), w_up.astype(jnp.float32), w_down.astype(jnp.float32), norm_gains.astype(jnp.float32), dt_bias.astype(jnp.float32), a_log.astype(jnp.float32), skip_scale.astype(jnp.float32))
    gradients = pullback(cotangent.astype(jnp.float32))
    return (result.astype(jnp.bfloat16), gradients[0], gradients[1], gradients[2], gradients[3], gradients[4], gradients[5], gradients[6], gradients[7], gradients[8], gradients[9], gradients[10], gradients[11])
```

```python
import math

import jax
import jax.numpy as jnp
from jax import lax
from jax.sharding import PartitionSpec as P

QUERY_HEADS = 8
KEY_VALUE_HEADS = 2
HEAD_SIZE = 128
MIXER_HEADS = 48
MIXER_HEAD_SIZE = 64
STATE_SIZE = 256
BLOCK = 256
LANES = 128

EPSILON = 1e-05
THETA = 10000.0
SCALE = 1.0 / math.sqrt(HEAD_SIZE)
BF16 = jnp.bfloat16
F32 = jnp.float32


def shift_ctx(value, hop):
    count = lax.axis_size("ctx")
    return lax.ppermute(value, "ctx", [(i, (i + hop) % count) for i in range(count)])


def swap_pair(value):
    count = lax.axis_size("ctx")
    return lax.ppermute(value, "ctx", [(i, i ^ 1) for i in range(count)])


def arrivals(value):
    return [shift_ctx(value, hop) for hop in range(1, lax.axis_size("ctx"))]


def gather_ctx(value):
    count, place = lax.axis_size("ctx"), lax.axis_index("ctx")
    rows = value.shape[0]
    parts = arrivals(value)
    out = jnp.zeros((count * rows,) + value.shape[1:], value.dtype)
    out = lax.dynamic_update_slice_in_dim(out, value, place * rows, 0)
    for hop in range(1, count):
        source = (place + count - hop) % count
        out = lax.dynamic_update_slice_in_dim(out, parts[hop - 1], source * rows, 0)
    return out


def scatter_sum_ctx(value):
    count, place = lax.axis_size("ctx"), lax.axis_index("ctx")
    rows = value.shape[0] // count
    total = lax.dynamic_slice_in_dim(value, place * rows, rows, 0)
    for hop in range(1, count):
        target = (place + hop) % count
        block = lax.dynamic_slice_in_dim(value, target * rows, rows, 0).astype(BF16)
        total = total + shift_ctx(block, hop).astype(F32)
    return total


def gather_rows(value):
    return lax.all_gather(value, "fsdp", axis=0, tiled=True)


def scatter_rows(value):
    return lax.psum_scatter(value, "fsdp", scatter_dimension=0, tiled=True)


def dot(left, right, left_dim, right_dim):
    return lax.dot_general(
        left, right, (((left_dim,), (right_dim,)), ((), ())), preferred_element_type=F32
    )


def rope(vectors, cosine, sine):
    half = vectors.shape[-1] // 2
    a, b = vectors[..., :half], vectors[..., half:]
    return jnp.concatenate([a * cosine - b * sine, b * cosine + a * sine], axis=-1)


def inverse_rms(rows):
    return lax.rsqrt(jnp.mean(rows * rows, axis=-1, keepdims=True) + EPSILON)


def rms_pull(rows, inverse, gain, grad):
    scaled = grad * gain
    return inverse * (scaled - rows * inverse * inverse * jnp.mean(rows * scaled, -1, keepdims=True))


def decay_terms(dt_raw, dt_offset, log_rate):
    step_size = jax.nn.softplus(dt_raw + dt_offset)
    level = jnp.cumsum(step_size * -jnp.exp(log_rate), axis=1)
    return (step_size, level)


def ssm(inputs, b_rows, c_rows, dt_raw, dt_offset, log_rate):
    tokens, heads, size = inputs.shape
    blocks = tokens // BLOCK
    x = inputs.reshape(blocks, BLOCK, heads, size)
    b_rows = b_rows.reshape(blocks, BLOCK, STATE_SIZE)
    c_rows = c_rows.reshape(blocks, BLOCK, STATE_SIZE)
    step_size, level = decay_terms(dt_raw.reshape(blocks, BLOCK, heads), dt_offset, log_rate)
    order = jnp.arange(BLOCK)
    causal = (order[:, None] >= order[None, :])[None, None]
    by_head = jnp.swapaxes(level, 1, 2)
    gap = jnp.where(causal, by_head[:, :, :, None] - by_head[:, :, None, :], 0.0)
    fading = jnp.where(causal, jnp.exp(gap), 0.0)
    pairing = jnp.einsum("btn,bsn->bts", c_rows, b_rows)
    mixing = fading * pairing[:, None] * jnp.swapaxes(step_size, 1, 2)[:, :, None, :]
    inside = jnp.einsum("bhts,bshp->bthp", mixing, x)
    tail = jnp.exp(level[:, -1:, :] - level) * step_size
    fresh = jnp.einsum("bshp,bsn->bhpn", tail[..., None] * x, b_rows)
    decay = jnp.exp(level[:, -1, :])
    state = jnp.zeros(fresh.shape[1:], F32)
    states = []
    for k in range(blocks):
        states.append(state)
        state = decay[k][:, None, None] * state + fresh[k]
    entered = jnp.stack(states)
    outer = jnp.exp(level)[..., None] * jnp.einsum("btn,bhpn->bthp", c_rows, entered)
    return (inside + outer).reshape(tokens, heads, size)


def attention(queries, keys, values):
    tokens = keys.shape[0]
    raw = jnp.einsum("hqd,kd->hqk", queries, keys, preferred_element_type=F32)
    order = jnp.arange(tokens)
    visible = order[:, None] >= order[None, :]
    logits = jnp.where(visible, raw * SCALE, -1e30)
    top = jnp.max(logits, axis=-1, keepdims=True)
    weights = jnp.exp(logits - top)
    total = jnp.sum(weights, axis=-1, keepdims=True)
    out = jnp.einsum("hqk,kd->hqd", weights.astype(BF16), values, preferred_element_type=F32)
    return out / total, top + jnp.log(total)


def attention_pull(queries, keys, values, out, log_total, grad_out):
    tokens = keys.shape[0]
    delta = jnp.sum(grad_out.astype(F32) * out, axis=-1, keepdims=True)
    raw = jnp.einsum("hqd,kd->hqk", queries, keys, preferred_element_type=F32)
    order = jnp.arange(tokens)
    visible = order[:, None] >= order[None, :]
    probs = jnp.exp(jnp.where(visible, raw * SCALE - log_total, -1e30))
    grad_probs = jnp.einsum("hqd,kd->hqk", grad_out, values, preferred_element_type=F32)
    grad_raw = (probs * (grad_probs - delta) * SCALE).astype(BF16)
    grad_queries = jnp.einsum("hqk,kd->hqd", grad_raw, keys, preferred_element_type=F32)
    grad_keys = jnp.einsum("hqk,hqd->kd", grad_raw, queries, preferred_element_type=F32)
    grad_values = jnp.einsum(
        "hqk,hqd->kd", probs.astype(BF16), grad_out, preferred_element_type=F32
    )
    return grad_queries, grad_keys, grad_values


def place_columns(out, block, start):
    return lax.dynamic_update_slice(out, block, (0, start))


def per_device(
    hidden_in,
    w_mix,
    w_dt,
    w_attn_out,
    w_ssm_out,
    w_gate,
    w_up,
    w_down,
    norm_gains,
    dt_bias,
    a_log,
    skip_scale,
    cotangent,
):
    w_mix, w_dt, w_attn_out, w_ssm_out = w_mix[0], w_dt[0], w_attn_out[0], w_ssm_out[0]
    w_gate, w_up, w_down = w_gate[0], w_up[0], w_down[0]
    gain_mix, gain_ffn = norm_gains[0, 0], norm_gains[0, 1]
    count, place = lax.axis_size("ctx"), lax.axis_index("ctx")
    piece, width = hidden_in.shape[1], hidden_in.shape[2]
    tokens = piece * count
    rows = w_mix.shape[0]
    hidden_units = w_gate.shape[1]
    q_heads = QUERY_HEADS // count
    group = QUERY_HEADS // KEY_VALUE_HEADS
    kv_head = (place * q_heads) // group
    heads = MIXER_HEADS // count
    q_wide, z_wide = q_heads * HEAD_SIZE, heads * MIXER_HEAD_SIZE
    key_at = QUERY_HEADS * HEAD_SIZE
    value_at = key_at + KEY_VALUE_HEADS * HEAD_SIZE
    z_at = value_at + KEY_VALUE_HEADS * HEAD_SIZE
    x_at = z_at + MIXER_HEADS * MIXER_HEAD_SIZE
    b_at = x_at + MIXER_HEADS * MIXER_HEAD_SIZE

    def columns(weight, start, size):
        return lax.dynamic_slice(weight, (0, start), (weight.shape[0], size))

    mix_own = jnp.concatenate(
        [
            columns(w_mix, place * q_wide, q_wide),
            columns(w_mix, key_at + kv_head * HEAD_SIZE, HEAD_SIZE),
            columns(w_mix, value_at + kv_head * HEAD_SIZE, HEAD_SIZE),
            columns(w_mix, z_at + place * z_wide, z_wide),
            columns(w_mix, x_at + place * z_wide, z_wide),
            w_mix[:, b_at:],
            jnp.pad(columns(w_dt, place * heads, heads), ((0, 0), (0, LANES - heads))),
            columns(w_attn_out, place * q_wide, q_wide),
            columns(w_ssm_out, place * z_wide, z_wide),
        ],
        axis=1,
    )
    mix_wide = mix_own.shape[1] - q_wide - z_wide
    half = place % 2
    half_units = hidden_units // 2
    ffn_own = jnp.concatenate(
        [columns(w, half * half_units, half_units) for w in (w_gate, w_up, w_down)], axis=1
    )
    mixer_weights = gather_rows(mix_own)
    w_in, w_out = mixer_weights[:, :mix_wide], mixer_weights[:, mix_wide:]
    ffn_weights = gather_rows(ffn_own)
    w_gate_half = ffn_weights[:, :half_units]
    w_up_half = ffn_weights[:, half_units : 2 * half_units]
    w_down_half = ffn_weights[:, 2 * half_units :]

    hidden_own = hidden_in.reshape(piece, width)
    hidden = gather_ctx(hidden_own).astype(F32)
    cot_own = cotangent.reshape(piece, width)
    cot_pair = jnp.concatenate([cot_own, swap_pair(cot_own)], axis=0)

    inverse_in = inverse_rms(hidden)
    scaled_in = hidden * inverse_in
    normed = (scaled_in * gain_mix).astype(BF16)
    mixed = dot(normed, w_in, 1, 0)
    cuts = [q_wide, HEAD_SIZE, HEAD_SIZE, z_wide, z_wide, STATE_SIZE, STATE_SIZE, LANES]
    pieces, at = [], 0
    for cut in cuts:
        pieces.append(mixed[:, at : at + cut])
        at += cut
    q_part, k_part, v_part, z_part, x_part, b_part, c_part, dt_part = pieces
    dt_part = dt_part[:, :heads]
    positions = jnp.arange(tokens, dtype=F32)
    frequency = THETA ** (-jnp.arange(HEAD_SIZE // 2, dtype=F32) / (HEAD_SIZE // 2))
    angles = positions[:, None] * frequency[None, :]
    cosine, sine = jnp.cos(angles), jnp.sin(angles)
    by_head = jnp.swapaxes(q_part.reshape(tokens, q_heads, HEAD_SIZE), 0, 1)
    queries = rope(by_head, cosine, sine).astype(BF16)
    keys = rope(k_part, cosine, sine).astype(BF16)
    values = v_part.astype(BF16)
    attended_full, log_total = attention(queries, keys, values)
    attended = jnp.swapaxes(attended_full, 0, 1).reshape(tokens, q_wide).astype(BF16)

    own_bias = lax.dynamic_slice_in_dim(dt_bias[0], place * heads, heads)
    own_rate = lax.dynamic_slice_in_dim(a_log[0], place * heads, heads)
    own_skip = lax.dynamic_slice_in_dim(skip_scale[0], place * heads, heads)
    x_heads = x_part.reshape(tokens, heads, MIXER_HEAD_SIZE)
    z_heads = z_part.reshape(tokens, heads, MIXER_HEAD_SIZE)
    ssm_y, ssm_pull = jax.vjp(ssm, x_heads, b_part, c_part, dt_part, own_bias, own_rate)
    full_y = ssm_y + own_skip[:, None] * x_heads
    gated = (full_y * jax.nn.silu(z_heads)).reshape(tokens, z_wide).astype(BF16)
    branch_in = jnp.concatenate([attended, gated], axis=1)
    branch = scatter_sum_ctx(dot(branch_in, w_out, 1, 1))
    middle = hidden_own.astype(F32) + branch

    inverse_ffn = inverse_rms(middle)
    normed_ffn = (middle * inverse_ffn * gain_ffn).astype(BF16)
    normed_pair = jnp.concatenate([normed_ffn, swap_pair(normed_ffn)], axis=0)
    gate = dot(normed_pair, w_gate_half, 1, 0)
    up = dot(normed_pair, w_up_half, 1, 0)
    sigmoid = jax.nn.sigmoid(gate)
    silu = gate * sigmoid
    activated = (silu * up).astype(BF16)
    grad_act = dot(cot_pair, w_down_half, 1, 0)
    grad_gate = (grad_act * up * (sigmoid * (1.0 + gate * (1.0 - sigmoid)))).astype(BF16)
    grad_up = (grad_act * silu).astype(BF16)
    grad_normed_pair = dot(grad_gate, w_gate_half, 1, 1) + dot(grad_up, w_up_half, 1, 1)
    grad_normed_ffn = grad_normed_pair[:piece] + swap_pair(
        grad_normed_pair[piece:].astype(BF16)
    ).astype(F32)
    out_pair = dot(activated, w_down_half, 1, 1)
    ffn_out = out_pair[:piece] + swap_pair(out_pair[piece:].astype(BF16)).astype(F32)
    hidden_out = (middle + ffn_out).astype(BF16)
    grad_w_ffn = scatter_rows(
        jnp.concatenate(
            [
                dot(normed_pair, grad_gate, 0, 0),
                dot(normed_pair, grad_up, 0, 0),
                dot(cot_pair, activated, 0, 0),
            ],
            axis=1,
        ).astype(BF16)
    )

    grad_middle = cot_own.astype(F32) + rms_pull(middle, inverse_ffn, gain_ffn, grad_normed_ffn)
    grad_gain_ffn = jnp.sum(grad_normed_ffn * middle * inverse_ffn, axis=0)
    grad_branch = gather_ctx(grad_middle.astype(BF16))
    grad_joint = dot(grad_branch, w_out, 1, 0)
    grad_attended = jnp.swapaxes(
        grad_joint[:, :q_wide].astype(BF16).reshape(tokens, q_heads, HEAD_SIZE), 0, 1
    )
    grad_w_out = scatter_rows(dot(grad_branch, branch_in, 0, 0).astype(BF16))

    grad_queries, grad_keys, grad_values = attention_pull(
        queries, keys, values, attended_full, log_total, grad_attended
    )
    grad_q = jnp.swapaxes(rope(grad_queries, cosine, -sine), 0, 1).reshape(tokens, q_wide)
    grad_k = rope(grad_keys, cosine, -sine)
    grad_gated = grad_joint[:, q_wide:].reshape(tokens, heads, MIXER_HEAD_SIZE)
    z_sigmoid = jax.nn.sigmoid(z_heads)
    grad_y = grad_gated * z_heads * z_sigmoid
    grad_z = grad_gated * full_y * (z_sigmoid * (1.0 + z_heads * (1.0 - z_sigmoid)))
    grad_skip = jnp.sum(grad_y * x_heads, axis=(0, 2))
    grad_x, grad_b, grad_c, grad_dt, grad_bias, grad_rate = ssm_pull(grad_y)
    grad_x = grad_x + own_skip[:, None] * grad_y
    grad_mixed = jnp.concatenate(
        [
            grad_q,
            grad_k,
            grad_values,
            grad_z.reshape(tokens, z_wide),
            grad_x.reshape(tokens, z_wide),
            grad_b,
            grad_c,
            jnp.pad(grad_dt, ((0, 0), (0, LANES - heads))),
        ],
        axis=1,
    ).astype(BF16)
    grad_w_in = scatter_rows(dot(normed, grad_mixed, 0, 0).astype(BF16))
    grad_normed_part = dot(grad_mixed, w_in, 1, 1)
    grad_gain_mix = jnp.sum(grad_normed_part * scaled_in, axis=0)
    grad_normed = scatter_sum_ctx(grad_normed_part)
    hidden_f32 = hidden_own.astype(F32)
    grad_hidden = grad_middle + rms_pull(
        hidden_f32, inverse_rms(hidden_f32), gain_mix, grad_normed
    )

    head_part = jnp.zeros((3, MIXER_HEADS), F32)
    head_part = lax.dynamic_update_slice(
        head_part, jnp.stack([grad_bias, grad_rate, grad_skip]), (0, place * heads)
    )
    gain_sums, head_sums = lax.psum(
        (jnp.stack([grad_gain_mix, grad_gain_ffn]), head_part), ("fsdp", "ctx")
    )

    mixer_grad = jnp.concatenate([grad_w_in, grad_w_out], axis=1)
    blocks = [mixer_grad] + arrivals(mixer_grad)
    out_mix = jnp.zeros((rows, b_at), F32)
    out_attn = jnp.zeros((rows, QUERY_HEADS * HEAD_SIZE), F32)
    out_ssm = jnp.zeros((rows, MIXER_HEADS * MIXER_HEAD_SIZE), F32)
    out_dt = jnp.zeros((rows, MIXER_HEADS), F32)
    tail = jnp.zeros((rows, 2 * STATE_SIZE), F32)
    key_value = jnp.zeros((rows, 2 * KEY_VALUE_HEADS * HEAD_SIZE), F32)
    bounds = [0]
    for cut in cuts + [q_wide, z_wide]:
        bounds.append(bounds[-1] + cut)
    for hop in range(count):
        source = (place + count - hop) % count
        wide = blocks[hop].astype(F32)
        part = [wide[:, bounds[i] : bounds[i + 1]] for i in range(len(bounds) - 1)]
        out_mix = place_columns(out_mix, part[0], source * q_wide)
        out_mix = place_columns(out_mix, part[3], z_at + source * z_wide)
        out_mix = place_columns(out_mix, part[4], x_at + source * z_wide)
        out_dt = place_columns(out_dt, part[7][:, :heads], source * heads)
        out_attn = place_columns(out_attn, part[8], source * q_wide)
        out_ssm = place_columns(out_ssm, part[9], source * z_wide)
        tail = tail + jnp.concatenate([part[5], part[6]], axis=1)
        which = (source * q_heads) // group
        spread = jnp.concatenate(
            [jnp.where(which == h, part[1], 0.0) for h in range(KEY_VALUE_HEADS)]
            + [jnp.where(which == h, part[2], 0.0) for h in range(KEY_VALUE_HEADS)],
            axis=1,
        )
        key_value = key_value + spread
    out_mix = lax.dynamic_update_slice(out_mix, key_value, (0, key_at))
    out_mix = jnp.concatenate([out_mix, tail], axis=1)

    members = count // 2
    member = place // 2
    chunk = rows // members
    total = lax.dynamic_slice_in_dim(grad_w_ffn, member * chunk, chunk, 0).astype(F32)
    for hop in range(1, members):
        target = (member + hop) % members
        block = lax.dynamic_slice_in_dim(grad_w_ffn, target * chunk, chunk, 0)
        total = total + shift_ctx(block, 2 * hop).astype(F32)
    total = total.astype(BF16)
    blocks = [total] + arrivals(total)
    outs = [jnp.zeros((rows, hidden_units), F32) for _ in range(3)]
    for hop in range(count):
        source = (place + count - hop) % count
        wide = blocks[hop].astype(F32)
        for i in range(3):
            outs[i] = lax.dynamic_update_slice(
                outs[i],
                wide[:, i * half_units : (i + 1) * half_units],
                ((source // 2) * chunk, (source % 2) * half_units),
            )
    return (
        hidden_out.reshape(hidden_in.shape),
        grad_hidden.reshape(hidden_in.shape),
        out_mix[None],
        out_dt[None],
        out_attn[None],
        out_ssm[None],
        outs[0][None],
        outs[1][None],
        outs[2][None],
        gain_sums[None],
        head_sums[0][None],
        head_sums[1][None],
        head_sums[2][None],
    )


def solution(mesh):
    split, rows = P("fsdp", "ctx", None), P(None, "fsdp", None)
    return jax.shard_map(
        per_device,
        mesh=mesh,
        in_specs=(split,) + (rows,) * 7 + (P(),) * 4 + (split,),
        out_specs=(split, split) + (rows,) * 7 + (P(),) * 4,
        check_vma=False,
    )
```

```python
import functools
import math

import jax
import jax.numpy as jnp
from jax import lax
from jax.experimental import pallas as pl
from jax.experimental.pallas import tpu as pltpu
from jax.sharding import PartitionSpec as P

QUERY_HEADS = 8
KEY_VALUE_HEADS = 2
HEAD_SIZE = 128
MIXER_HEADS = 48
MIXER_HEAD_SIZE = 64
STATE_SIZE = 256
LANES = 128

EPSILON = 1e-05
THETA = 10000.0
SCALE = 1.0 / math.sqrt(HEAD_SIZE)
VMEM_LIMIT = 56 * 1024 * 1024
BF16 = jnp.bfloat16
F32 = jnp.float32


def swap_pair(value):
    count = lax.axis_size("ctx")
    return lax.ppermute(value, "ctx", [(i, i ^ 1) for i in range(count)])


def after(value, *earlier):
    return lax.optimization_barrier((value,) + earlier)[0]


class Chain:
    def __init__(self, steps):
        self.steps, self.sends, self.result = steps, next(steps), None

    def take(self, got):
        try:
            self.sends = self.steps.send(got)
        except StopIteration as stop:
            self.sends, self.result = None, stop.value


def advance(*chains, beside=()):
    sends = [send for chain in chains for send in chain.sends]
    values = lax.optimization_barrier(tuple(value for value, _ in sends))
    got = tuple(lax.ppermute(v, "ctx", pairs) for v, (_, pairs) in zip(values, sends))
    if beside:
        sealed = lax.optimization_barrier(got + tuple(beside))
        got, beside = sealed[: len(got)], sealed[len(got) :]
    for chain in chains:
        count = len(chain.sends)
        chain.take(got[:count])
        got = got[count:]
    return beside


def finish(steps):
    chain = Chain(steps)
    while chain.sends is not None:
        advance(chain)
    return chain.result


def line_gather(value):
    count = lax.axis_size("ctx")
    up = down = value
    ups, downs = [], []
    for hop in range(1, count):
        up, down = yield [
            (up, [(i, i + 1) for i in range(hop - 1, count - 1)]),
            (down, [(i + 1, i) for i in range(count - hop)]),
        ]
        ups.append(up)
        downs.append(down)
    return ups, downs


def in_hops(value, ups, downs):
    count, place = lax.axis_size("ctx"), lax.axis_index("ctx")
    return [value] + [
        jnp.where(place >= hop, ups[hop - 1], downs[count - hop - 1]) for hop in range(1, count)
    ]


def gather_ctx(value):
    return in_hops(value, *finish(line_gather(value)))


def line_sum(parts):
    count = len(parts)
    up = down = 0.0
    for hop in range(1, count):
        up, down = yield [
            ((parts[hop] + up).astype(BF16), [(i, i + 1) for i in range(hop)]),
            (
                (parts[count - hop] + down).astype(BF16),
                [(i, i - 1) for i in range(count - hop, count)],
            ),
        ]
        up, down = up.astype(F32), down.astype(F32)
    return parts[0] + up + down


def parity_sum(grad):
    count = lax.axis_size("ctx")
    members, member = count // 2, lax.axis_index("ctx") // 2
    chunk = grad.shape[0] // members
    got = yield [
        (
            lax.dynamic_slice_in_dim(grad, ((member + hop) % members) * chunk, chunk, 0),
            [(i, (i + 2 * hop) % count) for i in range(count)],
        )
        for hop in range(1, members)
    ]
    total = lax.dynamic_slice_in_dim(grad, member * chunk, chunk, 0).astype(F32)
    for block in got:
        total = total + block.astype(F32)
    return total.astype(BF16)


def parity_gather(grad):
    total = yield from parity_sum(grad)
    ups, downs = yield from line_gather(total)
    return total, ups, downs


def gather_rows(value):
    return lax.all_gather(value, "fsdp", axis=0, tiled=True)


def scatter_rows(value):
    return lax.psum_scatter(value, "fsdp", scatter_dimension=0, tiled=True)


def dot(left, right, left_dim, right_dim):
    return lax.dot_general(
        left, right, (((left_dim,), (right_dim,)), ((), ())), preferred_element_type=F32
    )


def inverse_rms(rows):
    return lax.rsqrt(jnp.mean(rows * rows, axis=-1, keepdims=True) + EPSILON)


def rms_pull(rows, inverse, gain, grad):
    scaled = grad * gain
    return inverse * (scaled - rows * inverse * inverse * jnp.mean(rows * scaled, -1, keepdims=True))


def lanes_split(value, terms):
    parts = []
    for _ in range(terms):
        part = value.astype(BF16)
        parts.append(part)
        value = value - part.astype(F32)
    return parts


def near_exact(left, right, dims, terms, split_right):
    total = None
    for part in lanes_split(right if split_right else left, terms):
        pair = (left, part) if split_right else (part, right)
        one = lax.dot_general(*pair, (dims, ((), ())), preferred_element_type=F32)
        total = one if total is None else total + one
    return total


def mul(left, right, left_dim, right_dim):
    return lax.dot_general(
        left, right, (((left_dim,), (right_dim,)), ((), ())), preferred_element_type=F32
    )


def turn(vectors, cosine, sine):
    return vectors * cosine + pltpu.roll(vectors, HEAD_SIZE // 2, 1) * sine


def softplus(value):
    return jnp.maximum(value, 0.0) + jnp.log1p(jnp.exp(-jnp.abs(value)))


def block_terms(mixed, cuts, tri, params, spread):
    size = mixed.shape[0]
    dt_in = mixed[:, cuts["dt"] : cuts["dt"] + LANES] + params[0:1, :]
    step = softplus(dt_in)
    rate = params[1:2, :]
    level = near_exact(tri, step * rate, ((1,), (0,)), 3, True)
    last = level[size - 1 : size, :]
    enter = jnp.exp(level)
    leave = jnp.exp(last - level)
    wide = near_exact(
        jnp.concatenate([enter, step, leave * step], axis=0), spread, ((1,), (0,)), 2, False
    )
    return dict(
        dt_in=dt_in,
        step=step,
        rate=rate,
        level=level,
        last=last,
        leave=leave,
        enter_wide=wide[:size],
        step_wide=wide[size : 2 * size],
        tail_wide=wide[2 * size :],
    )


def fading_of(level, level_t, head, causal):
    gap = level[:, head : head + 1] - level_t[head : head + 1, :]
    return jnp.exp(jnp.where(causal, gap, -1e30))


def square_causal(size):
    row = lax.broadcasted_iota(jnp.int32, (size, size), 0)
    col = lax.broadcasted_iota(jnp.int32, (size, size), 1)
    return row >= col


def stacked_heads(value, at, count):
    return jnp.concatenate(
        [value[:, at + h * HEAD_SIZE : at + (h + 1) * HEAD_SIZE] for h in range(count)], axis=0
    )


def unstacked(value, count):
    size = value.shape[0] // count
    return jnp.concatenate([value[h * size : (h + 1) * size] for h in range(count)], axis=1)


def visible_keys(q_heads, size, block):
    shape = (q_heads * size, (block + 1) * size)
    row = lax.broadcasted_iota(jnp.int32, shape, 0)
    col = lax.broadcasted_iota(jnp.int32, shape, 1)
    return (row % size) + block * size >= col


def mixer_forward_kernel(
    cuts,
    q_heads,
    heads,
    blocks,
    place_ref,
    mixed_ref,
    cos_ref,
    sin_ref,
    tri_ref,
    params_ref,
    spread_ref,
    skip_ref,
    out_ref,
    state_ref,
    keys_ref,
    values_ref,
    carry,
):
    block = pl.program_id(0)
    size = mixed_ref.shape[0]
    q_wide, z_wide = q_heads * HEAD_SIZE, heads * MIXER_HEAD_SIZE

    @pl.when(block == 0)
    def _():
        carry[...] = jnp.zeros_like(carry)

    mixed = mixed_ref
    cosine, sine = cos_ref[...], sin_ref[...]
    here = pl.ds(pl.multiple_of(block * size, size), size)
    keys_ref[here, :] = turn(
        mixed[:, cuts["k"] : cuts["k"] + HEAD_SIZE], cosine, sine
    ).astype(BF16)
    values_ref[here, :] = mixed[:, cuts["v"] : cuts["v"] + HEAD_SIZE].astype(BF16)
    queries = jnp.concatenate(
        [
            turn(mixed[:, h * HEAD_SIZE : (h + 1) * HEAD_SIZE], cosine, sine)
            for h in range(q_heads)
        ],
        axis=0,
    ).astype(BF16)

    for at in range(blocks):

        @pl.when(block == at)
        def _(at=at):
            span = (at + 1) * size
            raw = mul(queries, keys_ref[:span, :], 1, 1) * SCALE
            logits = jnp.where(visible_keys(q_heads, size, at), raw, -1e30)
            weights = jnp.exp(logits - jnp.max(logits, axis=-1, keepdims=True))
            total = jnp.sum(weights, axis=-1, keepdims=True)
            attended = mul(weights.astype(BF16), values_ref[:span, :], 1, 0) / total
            out_ref[:, :q_wide] = unstacked(attended, q_heads).astype(BF16)

    terms = block_terms(mixed, cuts, tri_ref[...], params_ref, spread_ref[...])
    x = mixed[:, cuts["x"] : cuts["x"] + z_wide]
    b_rows = mixed[:, cuts["b"] : cuts["b"] + STATE_SIZE].astype(BF16)
    c_rows = mixed[:, cuts["c"] : cuts["c"] + STATE_SIZE].astype(BF16)
    causal = square_causal(size)
    pairing = mul(c_rows, b_rows, 1, 1)
    level = terms["level"]
    level_t = level.T
    x_step = (x * terms["step_wide"]).astype(BF16)
    first = lax.broadcasted_iota(jnp.int32, (size, LANES), 1) < MIXER_HEAD_SIZE
    inside = []
    for pair in range(heads // 2):
        both = x_step[:, pair * LANES : (pair + 1) * LANES]
        sides = []
        for head in (2 * pair, 2 * pair + 1):
            mixing = (fading_of(level, level_t, head, causal) * pairing).astype(BF16)
            sides.append(mul(mixing, both, 1, 0))
        inside.append(jnp.where(first, sides[0], sides[1]))
    state = carry[...]
    state_ref[0] = state
    full = (
        jnp.concatenate(inside, axis=1)
        + terms["enter_wide"] * mul(c_rows, state.astype(BF16), 1, 0)
        + skip_ref[...] * x
    )
    z = mixed[:, cuts["z"] : cuts["z"] + z_wide]
    out_ref[:, q_wide:] = (full * z * jax.nn.sigmoid(z)).astype(BF16)
    fresh = mul(b_rows, (x * terms["tail_wide"]).astype(BF16), 0, 0)
    carry[...] = terms["enter_wide"][size - 1 : size, :] * state + fresh


def mixer_backward_kernel(
    cuts,
    q_heads,
    heads,
    blocks,
    place_ref,
    mixed_ref,
    joint_ref,
    state_ref,
    keys_ref,
    values_ref,
    cos_ref,
    sin_ref,
    tri_ref,
    params_ref,
    spread_ref,
    skip_ref,
    out_ref,
    head_ref,
    grad_keys,
    grad_values,
    carry,
):
    block = blocks - 1 - pl.program_id(0)
    size = mixed_ref.shape[0]
    q_wide, z_wide = q_heads * HEAD_SIZE, heads * MIXER_HEAD_SIZE

    @pl.when(block == blocks - 1)
    def _():
        carry[...] = jnp.zeros_like(carry)
        grad_keys[...] = jnp.zeros_like(grad_keys)
        grad_values[...] = jnp.zeros_like(grad_values)
        head_ref[...] = jnp.zeros_like(head_ref)

    mixed, joint = mixed_ref, joint_ref
    cosine, sine = cos_ref[...], sin_ref[...]
    queries = jnp.concatenate(
        [
            turn(mixed[:, h * HEAD_SIZE : (h + 1) * HEAD_SIZE], cosine, sine)
            for h in range(q_heads)
        ],
        axis=0,
    ).astype(BF16)
    grad_out = stacked_heads(joint, 0, q_heads).astype(BF16)

    for at in range(blocks):

        @pl.when(block == at)
        def _(at=at):
            span = (at + 1) * size
            keys, values = keys_ref[:span, :], values_ref[:span, :]
            raw = mul(queries, keys, 1, 1) * SCALE
            logits = jnp.where(visible_keys(q_heads, size, at), raw, -1e30)
            weights = jnp.exp(logits - jnp.max(logits, axis=-1, keepdims=True))
            probs = weights / jnp.sum(weights, axis=-1, keepdims=True)
            grad_probs = mul(grad_out, values, 1, 1)
            delta = jnp.sum(probs * grad_probs, axis=-1, keepdims=True)
            grad_raw = (probs * (grad_probs - delta) * SCALE).astype(BF16)
            grad_queries = mul(grad_raw, keys, 1, 0)
            for h in range(q_heads):
                out_ref[:, h * HEAD_SIZE : (h + 1) * HEAD_SIZE] = turn(
                    grad_queries[h * size : (h + 1) * size], cosine, -sine
                ).astype(BF16)
            grad_keys[:span, :] += mul(grad_raw, queries, 0, 0)
            grad_values[:span, :] += mul(probs.astype(BF16), grad_out, 0, 0)

    here = pl.ds(pl.multiple_of(block * size, size), size)
    out_ref[:, cuts["k"] : cuts["k"] + HEAD_SIZE] = turn(
        grad_keys[here, :], cosine, -sine
    ).astype(BF16)
    out_ref[:, cuts["v"] : cuts["v"] + HEAD_SIZE] = grad_values[here, :].astype(BF16)

    tri, spread = tri_ref[...], spread_ref[...]
    terms = block_terms(mixed, cuts, tri, params_ref, spread)
    x = mixed[:, cuts["x"] : cuts["x"] + z_wide]
    z = mixed[:, cuts["z"] : cuts["z"] + z_wide]
    b_rows = mixed[:, cuts["b"] : cuts["b"] + STATE_SIZE].astype(BF16)
    c_rows = mixed[:, cuts["c"] : cuts["c"] + STATE_SIZE].astype(BF16)
    skip = skip_ref[...]
    causal = square_causal(size)
    pairing = mul(c_rows, b_rows, 1, 1)
    level = terms["level"]
    level_t = level.T
    enter_wide, step_wide, tail_wide = (
        terms["enter_wide"],
        terms["step_wide"],
        terms["tail_wide"],
    )
    x_step = (x * step_wide).astype(BF16)
    grad_gated = joint[:, q_wide:]
    sigmoid = jax.nn.sigmoid(z)
    grad_y = grad_gated * z * sigmoid
    grad_y16 = grad_y.astype(BF16)
    first = lax.broadcasted_iota(jnp.int32, (size, LANES), 1) < MIXER_HEAD_SIZE
    inside, grad_x_step = [], []
    grad_pairing = jnp.zeros((size, size), F32)
    none = jnp.zeros((size, LANES), BF16)
    for pair in range(heads // 2):
        lanes = slice(pair * LANES, (pair + 1) * LANES)
        both, grad_both = x_step[:, lanes], grad_y16[:, lanes]
        ys, xs = [], []
        for side, head in enumerate((2 * pair, 2 * pair + 1)):
            fading = fading_of(level, level_t, head, causal)
            mixing = (fading * pairing).astype(BF16)
            ys.append(mul(mixing, both, 1, 0))
            xs.append(mul(mixing, grad_both, 0, 0))
            alone = jnp.where(first == (side == 0), grad_both, none)
            grad_pairing = grad_pairing + fading * mul(alone, both, 1, 1)
        inside.append(jnp.where(first, ys[0], ys[1]))
        grad_x_step.append(jnp.where(first, xs[0], xs[1]))
    inside = jnp.concatenate(inside, axis=1)
    grad_x_step = jnp.concatenate(grad_x_step, axis=1)
    state = state_ref[0]
    state16 = state.astype(BF16)
    adjoint = carry[...]
    adjoint16 = adjoint.astype(BF16)
    outer = enter_wide * mul(c_rows, state16, 1, 0)
    full = inside + outer + skip * x
    grad_z = grad_gated * full * (sigmoid * (1.0 + z * (1.0 - sigmoid)))
    out_ref[:, cuts["z"] : cuts["z"] + z_wide] = grad_z.astype(BF16)
    entered = (enter_wide * grad_y).astype(BF16)
    pairing16 = grad_pairing.astype(BF16)
    grad_c = mul(entered, state16, 1, 1) + mul(pairing16, b_rows, 1, 0)
    grad_b = mul((x * tail_wide).astype(BF16), adjoint16, 1, 1) + mul(pairing16, c_rows, 0, 0)
    out_ref[:, cuts["b"] : cuts["b"] + STATE_SIZE] = grad_b.astype(BF16)
    out_ref[:, cuts["c"] : cuts["c"] + STATE_SIZE] = grad_c.astype(BF16)
    pushed = mul(b_rows, adjoint16, 1, 0)
    grad_x = step_wide * grad_x_step + tail_wide * pushed + skip * grad_y
    out_ref[:, cuts["x"] : cuts["x"] + z_wide] = grad_x.astype(BF16)

    def by_head(value):
        return near_exact(value, spread, ((1,), (1,)), 2, False)

    row_part = by_head(grad_y16.astype(F32) * inside + grad_y * outer)
    col_part = by_head(x_step.astype(F32) * grad_x_step)
    step_part = by_head(x * grad_x_step)
    tail_part = by_head(x * pushed)
    sums = jnp.concatenate(
        [
            jnp.sum(state * adjoint, axis=0, keepdims=True),
            jnp.sum(grad_y * x, axis=0, keepdims=True),
            jnp.zeros((6, z_wide), F32),
        ],
        axis=0,
    )
    sums = by_head(sums)
    step, leave, last = terms["step"], terms["leave"], terms["last"]
    moved = leave * step * tail_part
    grad_level = row_part - col_part - moved
    at_last = jnp.sum(moved, axis=0, keepdims=True) + jnp.exp(last) * sums[0:1, :]
    row = lax.broadcasted_iota(jnp.int32, (size, LANES), 0)
    grad_level = grad_level + jnp.where(row == size - 1, at_last, 0.0)
    grad_log = near_exact(tri, grad_level, ((0,), (0,)), 3, True)
    grad_step = step_part + leave * tail_part + grad_log * terms["rate"]
    grad_dt = grad_step * jax.nn.sigmoid(terms["dt_in"])
    lane = lax.broadcasted_iota(jnp.int32, (size, LANES), 1)
    grad_dt = jnp.where(lane < heads, grad_dt, 0.0)
    out_ref[:, cuts["dt"] : cuts["dt"] + LANES] = grad_dt.astype(BF16)
    head_ref[...] += jnp.concatenate(
        [
            jnp.sum(grad_dt, axis=0, keepdims=True),
            jnp.sum(grad_log * step, axis=0, keepdims=True) * terms["rate"],
            sums[1:2, :],
            jnp.zeros((5, LANES), F32),
        ],
        axis=0,
    )
    carry[...] = enter_wide[size - 1 : size, :] * adjoint + mul(c_rows, entered, 0, 0)


def mixer_tables(tokens, size, heads, bias, log_rate, skip):
    half = HEAD_SIZE // 2
    positions = jnp.arange(tokens, dtype=F32)
    frequency = THETA ** (-jnp.arange(half, dtype=F32) / half)
    angles = positions[:, None] * frequency[None, :]
    cosine, sine = jnp.cos(angles), jnp.sin(angles)
    order = jnp.arange(size)
    tri = (order[:, None] >= order[None, :]).astype(BF16)
    z_wide = heads * MIXER_HEAD_SIZE
    owner = jnp.arange(z_wide) // MIXER_HEAD_SIZE
    spread = (jnp.arange(LANES)[:, None] == owner[None, :]).astype(BF16)
    params = jnp.zeros((8, LANES), F32)
    params = params.at[0, :heads].set(bias).at[1, :heads].set(-jnp.exp(log_rate))
    return (
        jnp.concatenate([cosine, cosine], axis=1),
        jnp.concatenate([-sine, sine], axis=1),
        tri,
        params,
        spread,
        jnp.repeat(skip, MIXER_HEAD_SIZE)[None, :],
    )


def whole(shape):
    return pl.BlockSpec(shape, lambda i, place: (0,) * len(shape))


def mixer_forward(place, mixed, tables, cuts, q_heads, heads, blocks):
    tokens, wide = mixed.shape
    size = tokens // blocks
    cosine, sine, tri, params, spread, skip = tables
    z_wide = heads * MIXER_HEAD_SIZE
    out_wide = q_heads * HEAD_SIZE + z_wide

    def by_hop(width):
        return pl.BlockSpec(
            (size, width), lambda i, place: (lax.rem(place[0] - i + blocks, blocks), 0)
        )

    in_order = pl.BlockSpec((size, HEAD_SIZE), lambda i, place: (i, 0))
    return pl.pallas_call(
        functools.partial(mixer_forward_kernel, cuts, q_heads, heads, blocks),
        grid_spec=pltpu.PrefetchScalarGridSpec(
            num_scalar_prefetch=1,
            grid=(blocks,),
            in_specs=[
                by_hop(wide),
                in_order,
                in_order,
                whole(tri.shape),
                whole(params.shape),
                whole(spread.shape),
                whole(skip.shape),
            ],
            out_specs=[
                by_hop(out_wide),
                pl.BlockSpec((1, STATE_SIZE, z_wide), lambda i, place: (i, 0, 0)),
                whole((tokens, HEAD_SIZE)),
                whole((tokens, HEAD_SIZE)),
            ],
            scratch_shapes=[pltpu.VMEM((STATE_SIZE, z_wide), F32)],
        ),
        out_shape=[
            jax.ShapeDtypeStruct((tokens, out_wide), BF16),
            jax.ShapeDtypeStruct((blocks, STATE_SIZE, z_wide), F32),
            jax.ShapeDtypeStruct((tokens, HEAD_SIZE), BF16),
            jax.ShapeDtypeStruct((tokens, HEAD_SIZE), BF16),
        ],
        compiler_params=pltpu.CompilerParams(vmem_limit_bytes=VMEM_LIMIT),
        cost_estimate=pl.CostEstimate(
            flops=8_000_000_000, bytes_accessed=20_000_000, transcendentals=0
        ),
        name="mixer_forward",
    )(place, mixed, cosine, sine, tri, params, spread, skip)


def mixer_backward(place, mixed, joint, states, keys, values, tables, cuts, q_heads, heads, blocks):
    tokens, wide = mixed.shape
    size = tokens // blocks
    cosine, sine, tri, params, spread, skip = tables
    z_wide = heads * MIXER_HEAD_SIZE

    def by_hop(width):
        return pl.BlockSpec(
            (size, width), lambda i, place: (lax.rem(place[0] + i + 1, blocks), 0)
        )

    in_order = pl.BlockSpec((size, HEAD_SIZE), lambda i, place: (blocks - 1 - i, 0))
    return pl.pallas_call(
        functools.partial(mixer_backward_kernel, cuts, q_heads, heads, blocks),
        grid_spec=pltpu.PrefetchScalarGridSpec(
            num_scalar_prefetch=1,
            grid=(blocks,),
            in_specs=[
                by_hop(wide),
                by_hop(joint.shape[1]),
                pl.BlockSpec((1, STATE_SIZE, z_wide), lambda i, place: (blocks - 1 - i, 0, 0)),
                whole(keys.shape),
                whole(values.shape),
                in_order,
                in_order,
                whole(tri.shape),
                whole(params.shape),
                whole(spread.shape),
                whole(skip.shape),
            ],
            out_specs=[by_hop(wide), whole((8, LANES))],
            scratch_shapes=[
                pltpu.VMEM((tokens, HEAD_SIZE), F32),
                pltpu.VMEM((tokens, HEAD_SIZE), F32),
                pltpu.VMEM((STATE_SIZE, z_wide), F32),
            ],
        ),
        out_shape=[
            jax.ShapeDtypeStruct((tokens, wide), BF16),
            jax.ShapeDtypeStruct((8, LANES), F32),
        ],
        compiler_params=pltpu.CompilerParams(vmem_limit_bytes=VMEM_LIMIT),
        cost_estimate=pl.CostEstimate(
            flops=20_000_000_000, bytes_accessed=30_000_000, transcendentals=0
        ),
        name="mixer_backward",
    )(place, mixed, joint, states, keys, values, cosine, sine, tri, params, spread, skip)


def pack_kernel(cuts, starts_ref, *refs):
    sources = refs[: max(c[0] for out in cuts for c in out) + 1]
    outs = refs[len(sources) : len(sources) + len(cuts)]
    semaphores = refs[-1]
    copies, at = [], 0
    for out, ref in zip(cuts, outs):
        column = 0
        for source, wide in out:
            start = pl.multiple_of(starts_ref[at], LANES)
            copies.append(
                pltpu.make_async_copy(
                    sources[source].at[:, pl.ds(start, wide)],
                    ref.at[:, pl.ds(column, wide)],
                    semaphores.at[at],
                )
            )
            column += wide
            at += 1
    for copy in copies:
        copy.start()
    for copy in copies:
        copy.wait()


def pack_columns(sources, cuts):
    starts = jnp.stack([start for out in cuts for _, start, _ in out]).astype(jnp.int32)
    rows = sources[0].shape[0]
    anywhere = pl.BlockSpec(memory_space=pl.ANY)
    return pl.pallas_call(
        functools.partial(pack_kernel, [[(s, w) for s, _, w in out] for out in cuts]),
        grid_spec=pltpu.PrefetchScalarGridSpec(
            num_scalar_prefetch=1,
            grid=(1,),
            in_specs=[anywhere] * len(sources),
            out_specs=[
                pl.BlockSpec((rows, sum(w for _, _, w in out)), lambda i, starts: (0, 0))
                for out in cuts
            ],
            scratch_shapes=[pltpu.SemaphoreType.DMA((starts.shape[0],))],
        ),
        out_shape=[
            jax.ShapeDtypeStruct((rows, sum(w for _, _, w in out)), BF16) for out in cuts
        ],
        compiler_params=pltpu.CompilerParams(vmem_limit_bytes=VMEM_LIMIT),
        cost_estimate=pl.CostEstimate(
            flops=0, bytes_accessed=20_000_000, transcendentals=0
        ),
        name="pack_columns",
    )(starts, *sources)


def dense_cost(flops, *arrays):
    return pl.CostEstimate(
        flops=flops,
        bytes_accessed=sum(math.prod(a.shape) * a.dtype.itemsize for a in arrays),
        transcendentals=0,
    )


def mixer_in_kernel(count, place_ref, gain_ref, w_ref, *refs):
    parts = refs[: 2 * count - 1]
    out_ref, normed_ref, scaled_ref = refs[2 * count - 1 :]
    size = parts[0].shape[0]

    @pl.when(pl.program_id(0) == 0)
    def _():
        for hop in range(count):
            if hop == 0:
                rows = parts[0][...].astype(F32)
            else:
                rows = jnp.where(
                    place_ref[0] >= hop,
                    parts[hop][...].astype(F32),
                    parts[2 * count - 1 - hop][...].astype(F32),
                )
            scaled = rows * lax.rsqrt(jnp.mean(rows * rows, axis=-1, keepdims=True) + EPSILON)
            scaled_ref[hop * size : (hop + 1) * size, :] = scaled.astype(BF16)
            normed_ref[hop * size : (hop + 1) * size, :] = (scaled * gain_ref[...]).astype(BF16)

    out_ref[...] = mul(normed_ref[...], w_ref[...], 1, 0)


def mixer_in(place, own, ups, downs, gain, weight, wide):
    size, depth = own.shape
    count = len(ups) + 1
    tokens = size * count
    tile = max(t for t in range(LANES, 1025, LANES) if wide % t == 0)

    def fixed(shape):
        return pl.BlockSpec(shape, lambda j, place: (0, 0))

    outs = [
        jax.ShapeDtypeStruct((tokens, wide), F32),
        jax.ShapeDtypeStruct((tokens, depth), BF16),
        jax.ShapeDtypeStruct((tokens, depth), BF16),
    ]
    return pl.pallas_call(
        functools.partial(mixer_in_kernel, count),
        grid_spec=pltpu.PrefetchScalarGridSpec(
            num_scalar_prefetch=1,
            grid=(wide // tile,),
            in_specs=[
                fixed((1, depth)),
                pl.BlockSpec((depth, tile), lambda j, place: (0, j)),
            ]
            + [fixed((size, depth))] * (2 * count - 1),
            out_specs=[
                pl.BlockSpec((tokens, tile), lambda j, place: (0, j)),
                fixed((tokens, depth)),
                fixed((tokens, depth)),
            ],
        ),
        out_shape=outs,
        compiler_params=pltpu.CompilerParams(vmem_limit_bytes=VMEM_LIMIT),
        cost_estimate=dense_cost(2 * tokens * depth * wide, weight, *outs),
        name="mixer_in",
    )(place, gain, weight, own, *ups, *downs)


def ffn_kernel(x_ref, act_grad_ref, gate_ref, up_ref, activated_ref, grad_gate_ref, grad_up_ref):
    rows = x_ref[...]
    gate = mul(rows, gate_ref[...], 1, 0)
    up = mul(rows, up_ref[...], 1, 0)
    grad = act_grad_ref[...]
    sigmoid = jax.nn.sigmoid(gate)
    silu = gate * sigmoid
    activated_ref[...] = (silu * up).astype(BF16)
    grad_gate_ref[...] = (grad * up * (sigmoid * (1.0 + gate * (1.0 - sigmoid)))).astype(BF16)
    grad_up_ref[...] = (grad * silu).astype(BF16)


def ffn_inner(x, act_grad, weights):
    tokens, depth = x.shape
    units = act_grad.shape[1]
    tile = 256
    tiles = units // tile
    out = jax.ShapeDtypeStruct((tokens, units), BF16)
    by_unit = pl.BlockSpec((tokens, tile), lambda j: (0, j))
    return pl.pallas_call(
        ffn_kernel,
        grid=(tiles,),
        in_specs=[
            pl.BlockSpec((tokens, depth), lambda j: (0, 0)),
            by_unit,
            pl.BlockSpec((depth, tile), lambda j: (0, tiles + j)),
            pl.BlockSpec((depth, tile), lambda j: (0, 2 * tiles + j)),
        ],
        out_specs=[by_unit] * 3,
        out_shape=[out] * 3,
        compiler_params=pltpu.CompilerParams(vmem_limit_bytes=VMEM_LIMIT),
        cost_estimate=dense_cost(4 * tokens * depth * units, weights, out, out, out),
        name="ffn_inner",
    )(x, act_grad, weights, weights)


def ffn_back_kernel(grad_gate_ref, grad_up_ref, gate_ref, up_ref, own_ref, other_ref):
    total = mul(grad_gate_ref[...], gate_ref[...], 1, 1) + mul(grad_up_ref[...], up_ref[...], 1, 1)
    half = total.shape[0] // 2
    own_ref[...] = total[:half]
    other_ref[...] = total[half:].astype(BF16)


def ffn_back(grad_gate, grad_up, weights):
    tokens, units = grad_gate.shape
    depth = weights.shape[0]
    tile = 256
    whole_rows = pl.BlockSpec((tokens, units), lambda j: (0, 0))
    half = pl.BlockSpec((tokens // 2, tile), lambda j: (0, j))
    return pl.pallas_call(
        ffn_back_kernel,
        grid=(depth // tile,),
        in_specs=[
            whole_rows,
            whole_rows,
            pl.BlockSpec((tile, units), lambda j: (j, 1)),
            pl.BlockSpec((tile, units), lambda j: (j, 2)),
        ],
        out_specs=[half, half],
        out_shape=[
            jax.ShapeDtypeStruct((tokens // 2, depth), F32),
            jax.ShapeDtypeStruct((tokens // 2, depth), BF16),
        ],
        compiler_params=pltpu.CompilerParams(vmem_limit_bytes=VMEM_LIMIT),
        cost_estimate=dense_cost(4 * tokens * depth * units, weights),
        name="ffn_back",
    )(grad_gate, grad_up, weights, weights)


def outer_kernel(pairs, rider_at, *refs):
    out_ref = refs[-1]
    at = 0
    for left, right, start, wide in pairs:
        value = mul(refs[left][...], refs[right][:, start : start + wide], 0, 0)
        out_ref[:, at : at + wide] = value.astype(BF16)
        at += wide
    if rider_at is not None:
        riders = refs[-2][...]
        rows = riders.shape[0]
        for k in range(out_ref.shape[0] // rows):
            block = out_ref[k * rows : (k + 1) * rows, rider_at : rider_at + LANES]
            out_ref[k * rows : (k + 1) * rows, rider_at : rider_at + LANES] = block + riders


def weight_grads(pairs, riders=None, rider_at=None):
    operands = []

    def position(array):
        for i, held in enumerate(operands):
            if held is array:
                return i
        operands.append(array)
        return len(operands) - 1

    lefts = [position(left) for left, _, _, _ in pairs]
    n_left = len(operands)
    rights = [position(right) for _, right, _, _ in pairs]
    plan = [(l, r, p[2], p[3]) for l, r, p in zip(lefts, rights, pairs)]
    tokens, depth = operands[0].shape
    wide = sum(p[3] for p in pairs)
    tile = 256
    operands += [] if riders is None else [riders]
    specs = [pl.BlockSpec((a.shape[0], tile), lambda j: (0, j)) for a in operands[:n_left]] + [
        pl.BlockSpec(a.shape, lambda j: (0, 0)) for a in operands[n_left:]
    ]
    out = jax.ShapeDtypeStruct((depth, wide), BF16)
    return pl.pallas_call(
        functools.partial(outer_kernel, plan, rider_at),
        grid=(depth // tile,),
        in_specs=specs,
        out_specs=pl.BlockSpec((tile, wide), lambda j: (j, 0)),
        out_shape=out,
        compiler_params=pltpu.CompilerParams(vmem_limit_bytes=VMEM_LIMIT),
        cost_estimate=dense_cost(2 * tokens * depth * wide, out, *operands),
        name="weight_grads",
    )(*operands)


def unpack_kernel(cuts, out_at, q_heads, heads, gain_columns, count, place_ref, *refs):
    parts = refs[: 2 * count - 1]
    mix_ref, attn_ref, ssm_ref, extra_ref = refs[2 * count - 1 :]
    place = place_ref[0]
    q_wide, z_wide = q_heads * HEAD_SIZE, heads * MIXER_HEAD_SIZE
    group = QUERY_HEADS // KEY_VALUE_HEADS
    key_at = QUERY_HEADS * HEAD_SIZE
    kv_wide = KEY_VALUE_HEADS * HEAD_SIZE
    z_at = key_at + 2 * kv_wide
    x_at = z_at + MIXER_HEADS * MIXER_HEAD_SIZE
    b_at = x_at + MIXER_HEADS * MIXER_HEAD_SIZE
    step = mix_ref.shape[0]
    lane = lax.broadcasted_iota(jnp.int32, (step, LANES), 1)
    head_lane = heads + gain_columns
    head_at = MIXER_HEADS + gain_columns
    shared = jnp.zeros((step, 2 * STATE_SIZE), F32)
    extra = jnp.zeros((step, LANES), F32)
    mix_ref[:, key_at : key_at + 2 * kv_wide] = jnp.zeros((step, 2 * kv_wide), F32)

    for hop in range(count):
        source = lax.rem(place - hop + count, count)

        def of(start, wide, hop=hop):
            if hop == 0:
                return parts[0][:, start : start + wide].astype(F32)
            up = parts[hop][:, start : start + wide].astype(F32)
            down = parts[2 * count - 1 - hop][:, start : start + wide].astype(F32)
            return jnp.where(place >= hop, up, down)

        def put(ref, start, value):
            ref[:, pl.ds(pl.multiple_of(start, LANES), value.shape[1])] = value

        put(mix_ref, source * q_wide, of(cuts["q"], q_wide))
        put(mix_ref, z_at + source * z_wide, of(cuts["z"], z_wide))
        put(mix_ref, x_at + source * z_wide, of(cuts["x"], z_wide))
        put(attn_ref, source * q_wide, of(out_at, q_wide))
        put(ssm_ref, source * z_wide, of(out_at + q_wide, z_wide))
        shared = shared + of(cuts["b"], 2 * STATE_SIZE)
        which = lax.div(source * q_heads, group)
        for name, base in (("k", key_at), ("v", key_at + kv_wide)):
            at = pl.ds(pl.multiple_of(base + which * HEAD_SIZE, LANES), HEAD_SIZE)
            mix_ref[:, at] += of(cuts[name], HEAD_SIZE)
        small = of(cuts["dt"], LANES)
        own = jnp.where(lane < heads, small, 0.0)
        gains = jnp.where((lane >= heads) & (lane < head_lane), small, 0.0)
        column = jnp.where(lane == head_lane, small, 0.0)
        extra = (
            extra
            + pltpu.roll(own, source * heads, 1)
            + pltpu.roll(gains, MIXER_HEADS - heads, 1)
            + pltpu.roll(column, head_at - head_lane + source, 1)
        )
    mix_ref[:, b_at:] = shared
    extra_ref[...] = extra


def unpack_mixer(place, own, ups, downs, cuts, out_at, q_heads, heads, gain_columns):
    rows, wide = own.shape
    count = len(ups) + 1
    step = min(rows, 64)
    widths = (
        QUERY_HEADS * HEAD_SIZE
        + 2 * KEY_VALUE_HEADS * HEAD_SIZE
        + 2 * MIXER_HEADS * MIXER_HEAD_SIZE
        + 2 * STATE_SIZE,
        QUERY_HEADS * HEAD_SIZE,
        MIXER_HEADS * MIXER_HEAD_SIZE,
        LANES,
    )

    def spec(columns):
        return pl.BlockSpec((step, columns), lambda i, place: (i, 0))

    return pl.pallas_call(
        functools.partial(unpack_kernel, cuts, out_at, q_heads, heads, gain_columns, count),
        grid_spec=pltpu.PrefetchScalarGridSpec(
            num_scalar_prefetch=1,
            grid=(rows // step,),
            in_specs=[spec(wide)] * (2 * count - 1),
            out_specs=[spec(w) for w in widths],
        ),
        out_shape=[jax.ShapeDtypeStruct((rows, w), F32) for w in widths],
        compiler_params=pltpu.CompilerParams(vmem_limit_bytes=VMEM_LIMIT),
        cost_estimate=pl.CostEstimate(
            flops=100_000_000, bytes_accessed=26_000_000, transcendentals=0
        ),
        name="unpack_mixer",
    )(place, own, *ups, *downs)


def per_device(
    hidden_in,
    w_mix,
    w_dt,
    w_attn_out,
    w_ssm_out,
    w_gate,
    w_up,
    w_down,
    norm_gains,
    dt_bias,
    a_log,
    skip_scale,
    cotangent,
):
    w_mix, w_dt, w_attn_out, w_ssm_out = w_mix[0], w_dt[0], w_attn_out[0], w_ssm_out[0]
    w_gate, w_up, w_down = w_gate[0], w_up[0], w_down[0]
    gain_mix, gain_ffn = norm_gains[0, 0], norm_gains[0, 1]
    count, place = lax.axis_size("ctx"), lax.axis_index("ctx")
    piece, width = hidden_in.shape[1], hidden_in.shape[2]
    tokens = piece * count
    rows = w_mix.shape[0]
    hidden_units = w_gate.shape[1]
    q_heads = QUERY_HEADS // count
    group = QUERY_HEADS // KEY_VALUE_HEADS
    kv_head = (place * q_heads) // group
    heads = MIXER_HEADS // count
    q_wide, z_wide = q_heads * HEAD_SIZE, heads * MIXER_HEAD_SIZE
    key_at = QUERY_HEADS * HEAD_SIZE
    value_at = key_at + KEY_VALUE_HEADS * HEAD_SIZE
    z_at = value_at + KEY_VALUE_HEADS * HEAD_SIZE
    x_at = z_at + MIXER_HEADS * MIXER_HEAD_SIZE
    b_at = x_at + MIXER_HEADS * MIXER_HEAD_SIZE
    names = ("q", "k", "v", "z", "x", "b", "c", "dt")
    sizes = (q_wide, HEAD_SIZE, HEAD_SIZE, z_wide, z_wide, STATE_SIZE, STATE_SIZE, LANES)
    cuts, mix_wide = {}, 0
    for name, size in zip(names, sizes):
        cuts[name] = mix_wide
        mix_wide += size

    half = place % 2
    half_units = hidden_units // 2
    own_dt = lax.dynamic_slice(w_dt, (0, place * heads), (rows, heads))
    own_dt = jnp.pad(own_dt, ((0, 0), (0, LANES - heads)))
    here = jnp.reshape(place, (1,)).astype(jnp.int32)
    mix_starts = (
        (place * q_wide, q_wide),
        (key_at + kv_head * HEAD_SIZE, HEAD_SIZE),
        (value_at + kv_head * HEAD_SIZE, HEAD_SIZE),
        (z_at + place * z_wide, z_wide),
        (x_at + place * z_wide, z_wide),
        (b_at + 0 * place, 2 * STATE_SIZE),
    )
    from_half = (half * half_units, half_units)
    mixer_own, ffn_own = pack_columns(
        (w_mix, own_dt, w_attn_out, w_ssm_out, w_gate, w_up, w_down),
        (
            [(0,) + cut for cut in mix_starts]
            + [(1, 0 * place, LANES), (2, place * q_wide, q_wide), (3, place * z_wide, z_wide)],
            [(6,) + from_half, (4,) + from_half, (5,) + from_half],
        ),
    )
    w_mixer = gather_rows(mixer_own)
    w_in, w_out = w_mixer[:, :mix_wide], w_mixer[:, mix_wide:]
    w_ffn = gather_rows(ffn_own)
    w_down_half = w_ffn[:, :half_units]

    blocks = tokens // piece

    hidden_own = hidden_in.reshape(piece, width)
    hidden_ups, hidden_downs = finish(line_gather(hidden_own))
    mixed, normed, scaled_in = mixer_in(
        here, hidden_own, hidden_ups, hidden_downs, gain_mix[None, :], w_mixer, mix_wide
    )
    own = [lax.dynamic_slice_in_dim(p[0], place * heads, heads) for p in (dt_bias, a_log, skip_scale)]
    tables = mixer_tables(tokens, piece, heads, *own)
    branch_in, states, keys, values = mixer_forward(
        here, mixed, tables, cuts, q_heads, heads, blocks
    )
    cot_own = cotangent.reshape(piece, width)
    cot_swap = swap_pair(after(cot_own, *hidden_ups))
    branch_in, cot_swap = lax.optimization_barrier((branch_in, cot_swap))
    cot_pair = jnp.concatenate([cot_own, cot_swap], axis=0)
    branch = finish(
        line_sum([dot(branch_in[s * piece : (s + 1) * piece], w_out, 1, 1) for s in range(count)])
    )
    middle = hidden_own.astype(F32) + branch
    grad_act = dot(cot_pair, w_down_half, 1, 0)

    inverse_ffn = inverse_rms(middle)
    normed_ffn = (middle * inverse_ffn * gain_ffn).astype(BF16)
    normed_swap, grad_act = lax.optimization_barrier((swap_pair(normed_ffn), grad_act))
    normed_pair = jnp.concatenate([normed_ffn, normed_swap], axis=0)
    activated, grad_gate, grad_up = ffn_inner(normed_pair, grad_act, w_ffn)
    grad_normed_own, grad_normed_other = ffn_back(grad_gate, grad_up, w_ffn)
    grad_swap = swap_pair(grad_normed_other)
    activated, grad_gate, grad_up = lax.optimization_barrier(
        (activated, grad_gate, grad_up, grad_normed_other)
    )[:3]
    quarter = half_units // 2
    grad_w_first = weight_grads(
        ((normed_pair, grad_gate, 0, half_units), (normed_pair, grad_up, 0, quarter))
    )
    grad_w_second = weight_grads(
        (
            (normed_pair, grad_up, quarter, quarter),
            (cot_pair, after(activated, grad_w_first), 0, half_units),
        )
    )
    grad_swap, grad_w_second = lax.optimization_barrier((grad_swap, grad_w_second))
    grad_w_first = scatter_rows(grad_w_first)
    grad_normed_ffn = grad_normed_own + grad_swap.astype(F32)

    grad_middle = cot_own.astype(F32) + rms_pull(middle, inverse_ffn, gain_ffn, grad_normed_ffn)
    grad_gain_ffn = jnp.sum(grad_normed_ffn * middle * inverse_ffn, axis=0)
    branch_own = grad_middle.astype(BF16)
    activated = after(activated, branch_own)
    out_pair = dot(activated, w_down_half, 1, 1)
    grad_branch = jnp.concatenate(gather_ctx(branch_own), axis=0)
    grad_joint = dot(grad_branch, w_out, 1, 0)
    out_swap = swap_pair(after(out_pair[piece:].astype(BF16), grad_branch))
    grad_w_second = scatter_rows(after(grad_w_second, grad_w_first, grad_branch))
    first = Chain(parity_gather(grad_w_first))

    grad_mixed, head_part = mixer_backward(
        here, mixed, grad_joint, states, keys, values, tables, cuts, q_heads, heads, blocks
    )
    grad_mixed, head_part, out_swap = advance(first, beside=(grad_mixed, head_part, out_swap))
    ffn_out = out_pair[:piece] + out_swap.astype(F32)
    hidden_out = (middle + ffn_out).astype(BF16)
    grad_normed_part = dot(grad_mixed, w_in, 1, 1)
    grad_gain_mix = jnp.sum(grad_normed_part * scaled_in, axis=0)
    grad_normed_part, grad_gain_mix = advance(first, beside=(grad_normed_part, grad_gain_mix))

    gain_columns = 2 * width // rows
    riders = jnp.concatenate(
        [
            jnp.zeros((rows, heads), F32),
            jnp.stack([grad_gain_mix, grad_gain_ffn]).reshape(rows, gain_columns),
            jnp.pad(head_part[:3, :heads].reshape(3 * heads), (0, rows - 3 * heads))[:, None],
            jnp.zeros((rows, LANES - heads - gain_columns - 1), F32),
        ],
        axis=1,
    )
    grad_w_mixer = weight_grads(
        ((normed, grad_mixed, 0, mix_wide), (grad_branch, branch_in, 0, q_wide + z_wide)),
        riders.astype(BF16),
        cuts["dt"],
    )
    normed_sum = Chain(
        line_sum([grad_normed_part[s * piece : (s + 1) * piece] for s in range(count)])
    )
    (grad_w_mixer,) = advance(first, normed_sum, beside=(grad_w_mixer,))
    grad_w_mixer = scatter_rows(after(grad_w_mixer, grad_w_second))
    second = Chain(parity_gather(grad_w_second))
    chains = [first, normed_sum, second]
    while normed_sum.sends is not None:
        advance(*[chain for chain in chains if chain.sends is not None])
    mixer = Chain(line_gather(grad_w_mixer))
    chains = [first, second, mixer]
    while mixer.sends is not None:
        advance(*[chain for chain in chains if chain.sends is not None])
    while second.sends is not None:
        advance(*[chain for chain in chains if chain.sends is not None])
    grad_normed = normed_sum.result
    hidden_f32 = hidden_own.astype(F32)
    grad_hidden = grad_middle + rms_pull(
        hidden_f32, inverse_rms(hidden_f32), gain_mix, grad_normed
    )

    chunk = rows // (count // 2)

    outs = [jnp.zeros((rows, hidden_units), F32) for _ in range(3)]
    first, second = in_hops(*first.result), in_hops(*second.result)
    for hop in range(count):
        source = (place + count - hop) % count
        row, column = (source // 2) * chunk, (source % 2) * half_units
        for i, block, start, size, offset in (
            (0, first, 0, half_units, 0),
            (1, first, half_units, quarter, 0),
            (1, second, 0, quarter, quarter),
            (2, second, quarter, half_units, 0),
        ):
            outs[i] = lax.dynamic_update_slice(
                outs[i],
                block[hop][:, start : start + size].astype(F32),
                (row, column + offset),
            )
    out_gate, out_up, out_down = outs

    out_mix, out_attn, out_ssm, extra = unpack_mixer(
        here, grad_w_mixer, *mixer.result, cuts, mix_wide, q_heads, heads, gain_columns
    )
    head_at = MIXER_HEADS + gain_columns
    gain_sums = extra[:, MIXER_HEADS:head_at].reshape(norm_gains.shape)
    head_sums = extra[: 3 * heads, head_at : head_at + count].reshape(3, heads, count)
    head_sums = jnp.swapaxes(head_sums, 1, 2).reshape(3, MIXER_HEADS)

    return (
        hidden_out.reshape(hidden_in.shape),
        grad_hidden.reshape(hidden_in.shape),
        out_mix[None],
        extra[None, :, :MIXER_HEADS],
        out_attn[None],
        out_ssm[None],
        out_gate[None],
        out_up[None],
        out_down[None],
        gain_sums,
        head_sums[0][None],
        head_sums[1][None],
        head_sums[2][None],
    )


def solution(mesh):
    split, rows = P("fsdp", "ctx", None), P(None, "fsdp", None)
    return jax.shard_map(
        per_device,
        mesh=mesh,
        in_specs=(split,) + (rows,) * 7 + (P(),) * 4 + (split,),
        out_specs=(split, split) + (rows,) * 7 + (P(),) * 4,
        check_vma=False,
    )
```

```python
import functools
import math

import jax
import jax.numpy as jnp
from jax import lax
from jax.experimental import pallas as pl
from jax.experimental.pallas import tpu as pltpu
from jax.sharding import PartitionSpec as P

QUERY_HEADS = 8
KEY_VALUE_HEADS = 2
HEAD_SIZE = 128
MIXER_HEADS = 48
MIXER_HEAD_SIZE = 64
STATE_SIZE = 256
LANES = 128

EPSILON = 1e-05
THETA = 10000.0
SCALE = 1.0 / math.sqrt(HEAD_SIZE)
VMEM_LIMIT = 56 * 1024 * 1024
BF16 = jnp.bfloat16
F32 = jnp.float32


def swap_pair(value):
    count = lax.axis_size("ctx")
    return lax.ppermute(value, "ctx", [(i, i ^ 1) for i in range(count)])


def after(value, *earlier):
    return lax.optimization_barrier((value,) + earlier)[0]


class Chain:
    def __init__(self, steps):
        self.steps, self.sends, self.result = steps, next(steps), None

    def take(self, got):
        try:
            self.sends = self.steps.send(got)
        except StopIteration as stop:
            self.sends, self.result = None, stop.value


class Flight:
    def __init__(self, *chains):
        self.chains = chains
        sends = [send for chain in chains for send in chain.sends]
        self.values = lax.optimization_barrier(tuple(value for value, _ in sends))
        self.got = tuple(
            lax.ppermute(v, "ctx", pairs) for v, (_, pairs) in zip(self.values, sends)
        )

    def land(self, beside=()):
        sealed = lax.optimization_barrier(self.got + tuple(beside))
        got = sealed[: len(self.got)]
        for chain in self.chains:
            count = len(chain.sends)
            chain.take(got[:count])
            got = got[count:]
        return sealed[len(self.got) :]


def advance(*chains, beside=()):
    return Flight(*chains).land(beside)


def live(*chains):
    return [chain for chain in chains if chain.sends is not None]


def finish(steps):
    chain = Chain(steps)
    while chain.sends is not None:
        advance(chain)
    return chain.result


def line_gather(value):
    count = lax.axis_size("ctx")
    up = down = value
    ups, downs = [], []
    for hop in range(1, count):
        up, down = yield [
            (up, [(i, i + 1) for i in range(hop - 1, count - 1)]),
            (down, [(i + 1, i) for i in range(count - hop)]),
        ]
        ups.append(up)
        downs.append(down)
    return ups, downs


def in_hops(value, ups, downs):
    count, place = lax.axis_size("ctx"), lax.axis_index("ctx")
    return [value] + [
        jnp.where(place >= hop, ups[hop - 1], downs[count - hop - 1]) for hop in range(1, count)
    ]


def gather_ctx(value):
    return in_hops(value, *finish(line_gather(value)))


def line_sum(parts):
    count = len(parts)
    up = down = 0.0
    for hop in range(1, count):
        up, down = yield [
            ((parts[hop] + up).astype(BF16), [(i, i + 1) for i in range(hop)]),
            (
                (parts[count - hop] + down).astype(BF16),
                [(i, i - 1) for i in range(count - hop, count)],
            ),
        ]
        up, down = up.astype(F32), down.astype(F32)
    return parts[0] + up + down


def parity_sum(grad):
    count = lax.axis_size("ctx")
    members, member = count // 2, lax.axis_index("ctx") // 2
    chunk = grad.shape[0] // members
    got = yield [
        (
            lax.dynamic_slice_in_dim(grad, ((member + hop) % members) * chunk, chunk, 0),
            [(i, (i + 2 * hop) % count) for i in range(count)],
        )
        for hop in range(1, members)
    ]
    total = lax.dynamic_slice_in_dim(grad, member * chunk, chunk, 0).astype(F32)
    for block in got:
        total = total + block.astype(F32)
    return total.astype(BF16)


def parity_gather(grad):
    total = yield from parity_sum(grad)
    ups, downs = yield from line_gather(total)
    return total, ups, downs


def gather_rows(value):
    return lax.all_gather(value, "fsdp", axis=0, tiled=True)


def scatter_rows(value):
    return lax.psum_scatter(value, "fsdp", scatter_dimension=0, tiled=True)


def dot(left, right, left_dim, right_dim):
    return lax.dot_general(
        left, right, (((left_dim,), (right_dim,)), ((), ())), preferred_element_type=F32
    )


def inverse_rms(rows):
    return lax.rsqrt(jnp.mean(rows * rows, axis=-1, keepdims=True) + EPSILON)


def rms_pull(rows, inverse, gain, grad):
    scaled = grad * gain
    return inverse * (scaled - rows * inverse * inverse * jnp.mean(rows * scaled, -1, keepdims=True))


def lanes_split(value, terms):
    parts = []
    for _ in range(terms):
        part = value.astype(BF16)
        parts.append(part)
        value = value - part.astype(F32)
    return parts


def near_exact(left, right, dims, terms, split_right):
    total = None
    for part in lanes_split(right if split_right else left, terms):
        pair = (left, part) if split_right else (part, right)
        one = lax.dot_general(*pair, (dims, ((), ())), preferred_element_type=F32)
        total = one if total is None else total + one
    return total


def mul(left, right, left_dim, right_dim):
    return lax.dot_general(
        left, right, (((left_dim,), (right_dim,)), ((), ())), preferred_element_type=F32
    )


def turn(vectors, cosine, sine):
    return vectors * cosine + pltpu.roll(vectors, HEAD_SIZE // 2, 1) * sine


def softplus(value):
    return jnp.maximum(value, 0.0) + jnp.log1p(jnp.exp(-jnp.abs(value)))


def block_terms(mixed, cuts, tri, params, spread):
    size = mixed.shape[0]
    dt_in = mixed[:, cuts["dt"] : cuts["dt"] + LANES] + params[0:1, :]
    step = softplus(dt_in)
    rate = params[1:2, :]
    level = near_exact(tri, step * rate, ((1,), (0,)), 3, True)
    last = level[size - 1 : size, :]
    enter = jnp.exp(level)
    leave = jnp.exp(last - level)
    wide = near_exact(
        jnp.concatenate([enter, step, leave * step], axis=0), spread, ((1,), (0,)), 2, False
    )
    return dict(
        dt_in=dt_in,
        step=step,
        rate=rate,
        level=level,
        last=last,
        leave=leave,
        enter_wide=wide[:size],
        step_wide=wide[size : 2 * size],
        tail_wide=wide[2 * size :],
    )


def fading_of(level, level_t, head, causal):
    gap = level[:, head : head + 1] - level_t[head : head + 1, :]
    return jnp.exp(jnp.where(causal, gap, -1e30))


def square_causal(size):
    row = lax.broadcasted_iota(jnp.int32, (size, size), 0)
    col = lax.broadcasted_iota(jnp.int32, (size, size), 1)
    return row >= col


def stacked_heads(value, at, count):
    return jnp.concatenate(
        [value[:, at + h * HEAD_SIZE : at + (h + 1) * HEAD_SIZE] for h in range(count)], axis=0
    )


def unstacked(value, count):
    size = value.shape[0] // count
    return jnp.concatenate([value[h * size : (h + 1) * size] for h in range(count)], axis=1)


def visible_keys(q_heads, size, block):
    shape = (q_heads * size, (block + 1) * size)
    row = lax.broadcasted_iota(jnp.int32, shape, 0)
    col = lax.broadcasted_iota(jnp.int32, shape, 1)
    return (row % size) + block * size >= col


def mixer_forward_kernel(
    cuts,
    q_heads,
    heads,
    blocks,
    place_ref,
    mixed_ref,
    cos_ref,
    sin_ref,
    tri_ref,
    params_ref,
    spread_ref,
    skip_ref,
    out_ref,
    state_ref,
    keys_ref,
    values_ref,
    carry,
):
    block = pl.program_id(0)
    size = mixed_ref.shape[0]
    q_wide, z_wide = q_heads * HEAD_SIZE, heads * MIXER_HEAD_SIZE

    @pl.when(block == 0)
    def _():
        carry[...] = jnp.zeros_like(carry)

    mixed = mixed_ref
    cosine, sine = cos_ref[...], sin_ref[...]
    here = pl.ds(pl.multiple_of(block * size, size), size)
    keys_ref[here, :] = turn(
        mixed[:, cuts["k"] : cuts["k"] + HEAD_SIZE], cosine, sine
    ).astype(BF16)
    values_ref[here, :] = mixed[:, cuts["v"] : cuts["v"] + HEAD_SIZE].astype(BF16)
    queries = jnp.concatenate(
        [
            turn(mixed[:, h * HEAD_SIZE : (h + 1) * HEAD_SIZE], cosine, sine)
            for h in range(q_heads)
        ],
        axis=0,
    ).astype(BF16)

    for at in range(blocks):

        @pl.when(block == at)
        def _(at=at):
            span = (at + 1) * size
            raw = mul(queries, keys_ref[:span, :], 1, 1) * SCALE
            logits = jnp.where(visible_keys(q_heads, size, at), raw, -1e30)
            weights = jnp.exp(logits - jnp.max(logits, axis=-1, keepdims=True))
            total = jnp.sum(weights, axis=-1, keepdims=True)
            attended = mul(weights.astype(BF16), values_ref[:span, :], 1, 0) / total
            out_ref[:, :q_wide] = unstacked(attended, q_heads).astype(BF16)

    terms = block_terms(mixed, cuts, tri_ref[...], params_ref, spread_ref[...])
    x = mixed[:, cuts["x"] : cuts["x"] + z_wide]
    b_rows = mixed[:, cuts["b"] : cuts["b"] + STATE_SIZE].astype(BF16)
    c_rows = mixed[:, cuts["c"] : cuts["c"] + STATE_SIZE].astype(BF16)
    causal = square_causal(size)
    pairing = mul(c_rows, b_rows, 1, 1)
    level = terms["level"]
    level_t = level.T
    x_step = (x * terms["step_wide"]).astype(BF16)
    first = lax.broadcasted_iota(jnp.int32, (size, LANES), 1) < MIXER_HEAD_SIZE
    inside = []
    for pair in range(heads // 2):
        both = x_step[:, pair * LANES : (pair + 1) * LANES]
        sides = []
        for head in (2 * pair, 2 * pair + 1):
            mixing = (fading_of(level, level_t, head, causal) * pairing).astype(BF16)
            sides.append(mul(mixing, both, 1, 0))
        inside.append(jnp.where(first, sides[0], sides[1]))
    state = carry[...]
    state_ref[0] = state
    full = (
        jnp.concatenate(inside, axis=1)
        + terms["enter_wide"] * mul(c_rows, state.astype(BF16), 1, 0)
        + skip_ref[...] * x
    )
    z = mixed[:, cuts["z"] : cuts["z"] + z_wide]
    out_ref[:, q_wide:] = (full * z * jax.nn.sigmoid(z)).astype(BF16)
    fresh = mul(b_rows, (x * terms["tail_wide"]).astype(BF16), 0, 0)
    carry[...] = terms["enter_wide"][size - 1 : size, :] * state + fresh


def mixer_backward_kernel(
    cuts,
    q_heads,
    heads,
    blocks,
    place_ref,
    mixed_ref,
    joint_ref,
    state_ref,
    keys_ref,
    values_ref,
    cos_ref,
    sin_ref,
    tri_ref,
    params_ref,
    spread_ref,
    skip_ref,
    out_ref,
    head_ref,
    grad_keys,
    grad_values,
    carry,
):
    block = blocks - 1 - pl.program_id(0)
    size = mixed_ref.shape[0]
    q_wide, z_wide = q_heads * HEAD_SIZE, heads * MIXER_HEAD_SIZE

    @pl.when(block == blocks - 1)
    def _():
        carry[...] = jnp.zeros_like(carry)
        grad_keys[...] = jnp.zeros_like(grad_keys)
        grad_values[...] = jnp.zeros_like(grad_values)
        head_ref[...] = jnp.zeros_like(head_ref)

    mixed, joint = mixed_ref, joint_ref
    cosine, sine = cos_ref[...], sin_ref[...]
    queries = jnp.concatenate(
        [
            turn(mixed[:, h * HEAD_SIZE : (h + 1) * HEAD_SIZE], cosine, sine)
            for h in range(q_heads)
        ],
        axis=0,
    ).astype(BF16)
    grad_out = stacked_heads(joint, 0, q_heads).astype(BF16)

    for at in range(blocks):

        @pl.when(block == at)
        def _(at=at):
            span = (at + 1) * size
            keys, values = keys_ref[:span, :], values_ref[:span, :]
            raw = mul(queries, keys, 1, 1) * SCALE
            logits = jnp.where(visible_keys(q_heads, size, at), raw, -1e30)
            weights = jnp.exp(logits - jnp.max(logits, axis=-1, keepdims=True))
            probs = weights / jnp.sum(weights, axis=-1, keepdims=True)
            grad_probs = mul(grad_out, values, 1, 1)
            delta = jnp.sum(probs * grad_probs, axis=-1, keepdims=True)
            grad_raw = (probs * (grad_probs - delta) * SCALE).astype(BF16)
            grad_queries = mul(grad_raw, keys, 1, 0)
            for h in range(q_heads):
                out_ref[:, h * HEAD_SIZE : (h + 1) * HEAD_SIZE] = turn(
                    grad_queries[h * size : (h + 1) * size], cosine, -sine
                ).astype(BF16)
            grad_keys[:span, :] += mul(grad_raw, queries, 0, 0)
            grad_values[:span, :] += mul(probs.astype(BF16), grad_out, 0, 0)

    here = pl.ds(pl.multiple_of(block * size, size), size)
    out_ref[:, cuts["k"] : cuts["k"] + HEAD_SIZE] = turn(
        grad_keys[here, :], cosine, -sine
    ).astype(BF16)
    out_ref[:, cuts["v"] : cuts["v"] + HEAD_SIZE] = grad_values[here, :].astype(BF16)

    tri, spread = tri_ref[...], spread_ref[...]
    terms = block_terms(mixed, cuts, tri, params_ref, spread)
    x = mixed[:, cuts["x"] : cuts["x"] + z_wide]
    z = mixed[:, cuts["z"] : cuts["z"] + z_wide]
    b_rows = mixed[:, cuts["b"] : cuts["b"] + STATE_SIZE].astype(BF16)
    c_rows = mixed[:, cuts["c"] : cuts["c"] + STATE_SIZE].astype(BF16)
    skip = skip_ref[...]
    causal = square_causal(size)
    pairing = mul(c_rows, b_rows, 1, 1)
    level = terms["level"]
    level_t = level.T
    enter_wide, step_wide, tail_wide = (
        terms["enter_wide"],
        terms["step_wide"],
        terms["tail_wide"],
    )
    x_step = (x * step_wide).astype(BF16)
    grad_gated = joint[:, q_wide:]
    sigmoid = jax.nn.sigmoid(z)
    grad_y = grad_gated * z * sigmoid
    grad_y16 = grad_y.astype(BF16)
    first = lax.broadcasted_iota(jnp.int32, (size, LANES), 1) < MIXER_HEAD_SIZE
    inside, grad_x_step = [], []
    grad_pairing = jnp.zeros((size, size), F32)
    none = jnp.zeros((size, LANES), BF16)
    for pair in range(heads // 2):
        lanes = slice(pair * LANES, (pair + 1) * LANES)
        both, grad_both = x_step[:, lanes], grad_y16[:, lanes]
        ys, xs = [], []
        for side, head in enumerate((2 * pair, 2 * pair + 1)):
            fading = fading_of(level, level_t, head, causal)
            mixing = (fading * pairing).astype(BF16)
            ys.append(mul(mixing, both, 1, 0))
            xs.append(mul(mixing, grad_both, 0, 0))
            alone = jnp.where(first == (side == 0), grad_both, none)
            grad_pairing = grad_pairing + fading * mul(alone, both, 1, 1)
        inside.append(jnp.where(first, ys[0], ys[1]))
        grad_x_step.append(jnp.where(first, xs[0], xs[1]))
    inside = jnp.concatenate(inside, axis=1)
    grad_x_step = jnp.concatenate(grad_x_step, axis=1)
    state = state_ref[0]
    state16 = state.astype(BF16)
    adjoint = carry[...]
    adjoint16 = adjoint.astype(BF16)
    outer = enter_wide * mul(c_rows, state16, 1, 0)
    full = inside + outer + skip * x
    grad_z = grad_gated * full * (sigmoid * (1.0 + z * (1.0 - sigmoid)))
    out_ref[:, cuts["z"] : cuts["z"] + z_wide] = grad_z.astype(BF16)
    entered = (enter_wide * grad_y).astype(BF16)
    pairing16 = grad_pairing.astype(BF16)
    grad_c = mul(entered, state16, 1, 1) + mul(pairing16, b_rows, 1, 0)
    grad_b = mul((x * tail_wide).astype(BF16), adjoint16, 1, 1) + mul(pairing16, c_rows, 0, 0)
    out_ref[:, cuts["b"] : cuts["b"] + STATE_SIZE] = grad_b.astype(BF16)
    out_ref[:, cuts["c"] : cuts["c"] + STATE_SIZE] = grad_c.astype(BF16)
    pushed = mul(b_rows, adjoint16, 1, 0)
    grad_x = step_wide * grad_x_step + tail_wide * pushed + skip * grad_y
    out_ref[:, cuts["x"] : cuts["x"] + z_wide] = grad_x.astype(BF16)

    def by_head(value):
        return near_exact(value, spread, ((1,), (1,)), 2, False)

    row_part = by_head(grad_y16.astype(F32) * inside + grad_y * outer)
    col_part = by_head(x_step.astype(F32) * grad_x_step)
    step_part = by_head(x * grad_x_step)
    tail_part = by_head(x * pushed)
    sums = jnp.concatenate(
        [
            jnp.sum(state * adjoint, axis=0, keepdims=True),
            jnp.sum(grad_y * x, axis=0, keepdims=True),
            jnp.zeros((6, z_wide), F32),
        ],
        axis=0,
    )
    sums = by_head(sums)
    step, leave, last = terms["step"], terms["leave"], terms["last"]
    moved = leave * step * tail_part
    grad_level = row_part - col_part - moved
    at_last = jnp.sum(moved, axis=0, keepdims=True) + jnp.exp(last) * sums[0:1, :]
    row = lax.broadcasted_iota(jnp.int32, (size, LANES), 0)
    grad_level = grad_level + jnp.where(row == size - 1, at_last, 0.0)
    grad_log = near_exact(tri, grad_level, ((0,), (0,)), 3, True)
    grad_step = step_part + leave * tail_part + grad_log * terms["rate"]
    grad_dt = grad_step * jax.nn.sigmoid(terms["dt_in"])
    lane = lax.broadcasted_iota(jnp.int32, (size, LANES), 1)
    grad_dt = jnp.where(lane < heads, grad_dt, 0.0)
    out_ref[:, cuts["dt"] : cuts["dt"] + LANES] = grad_dt.astype(BF16)
    head_ref[...] += jnp.concatenate(
        [
            jnp.sum(grad_dt, axis=0, keepdims=True),
            jnp.sum(grad_log * step, axis=0, keepdims=True) * terms["rate"],
            sums[1:2, :],
            jnp.zeros((5, LANES), F32),
        ],
        axis=0,
    )
    carry[...] = enter_wide[size - 1 : size, :] * adjoint + mul(c_rows, entered, 0, 0)


def mixer_tables(tokens, size, heads, bias, log_rate, skip):
    half = HEAD_SIZE // 2
    positions = jnp.arange(tokens, dtype=F32)
    frequency = THETA ** (-jnp.arange(half, dtype=F32) / half)
    angles = positions[:, None] * frequency[None, :]
    cosine, sine = jnp.cos(angles), jnp.sin(angles)
    order = jnp.arange(size)
    tri = (order[:, None] >= order[None, :]).astype(BF16)
    z_wide = heads * MIXER_HEAD_SIZE
    owner = jnp.arange(z_wide) // MIXER_HEAD_SIZE
    spread = (jnp.arange(LANES)[:, None] == owner[None, :]).astype(BF16)
    params = jnp.zeros((8, LANES), F32)
    params = params.at[0, :heads].set(bias).at[1, :heads].set(-jnp.exp(log_rate))
    return (
        jnp.concatenate([cosine, cosine], axis=1),
        jnp.concatenate([-sine, sine], axis=1),
        tri,
        params,
        spread,
        jnp.repeat(skip, MIXER_HEAD_SIZE)[None, :],
    )


def whole(shape):
    return pl.BlockSpec(shape, lambda i, place: (0,) * len(shape))


def mixer_forward(place, mixed, tables, cuts, q_heads, heads, blocks):
    tokens, wide = mixed.shape
    size = tokens // blocks
    cosine, sine, tri, params, spread, skip = tables
    z_wide = heads * MIXER_HEAD_SIZE
    out_wide = q_heads * HEAD_SIZE + z_wide

    def by_hop(width):
        return pl.BlockSpec(
            (size, width), lambda i, place: (lax.rem(place[0] - i + blocks, blocks), 0)
        )

    in_order = pl.BlockSpec((size, HEAD_SIZE), lambda i, place: (i, 0))
    return pl.pallas_call(
        functools.partial(mixer_forward_kernel, cuts, q_heads, heads, blocks),
        grid_spec=pltpu.PrefetchScalarGridSpec(
            num_scalar_prefetch=1,
            grid=(blocks,),
            in_specs=[
                by_hop(wide),
                in_order,
                in_order,
                whole(tri.shape),
                whole(params.shape),
                whole(spread.shape),
                whole(skip.shape),
            ],
            out_specs=[
                by_hop(out_wide),
                pl.BlockSpec((1, STATE_SIZE, z_wide), lambda i, place: (i, 0, 0)),
                whole((tokens, HEAD_SIZE)),
                whole((tokens, HEAD_SIZE)),
            ],
            scratch_shapes=[pltpu.VMEM((STATE_SIZE, z_wide), F32)],
        ),
        out_shape=[
            jax.ShapeDtypeStruct((tokens, out_wide), BF16),
            jax.ShapeDtypeStruct((blocks, STATE_SIZE, z_wide), F32),
            jax.ShapeDtypeStruct((tokens, HEAD_SIZE), BF16),
            jax.ShapeDtypeStruct((tokens, HEAD_SIZE), BF16),
        ],
        compiler_params=pltpu.CompilerParams(vmem_limit_bytes=VMEM_LIMIT),
        cost_estimate=pl.CostEstimate(
            flops=8_000_000_000, bytes_accessed=20_000_000, transcendentals=0
        ),
        name="mixer_forward",
    )(place, mixed, cosine, sine, tri, params, spread, skip)


def mixer_backward(place, mixed, joint, states, keys, values, tables, cuts, q_heads, heads, blocks):
    tokens, wide = mixed.shape
    size = tokens // blocks
    cosine, sine, tri, params, spread, skip = tables
    z_wide = heads * MIXER_HEAD_SIZE

    def by_hop(width):
        return pl.BlockSpec(
            (size, width), lambda i, place: (lax.rem(place[0] + i + 1, blocks), 0)
        )

    in_order = pl.BlockSpec((size, HEAD_SIZE), lambda i, place: (blocks - 1 - i, 0))
    return pl.pallas_call(
        functools.partial(mixer_backward_kernel, cuts, q_heads, heads, blocks),
        grid_spec=pltpu.PrefetchScalarGridSpec(
            num_scalar_prefetch=1,
            grid=(blocks,),
            in_specs=[
                by_hop(wide),
                by_hop(joint.shape[1]),
                pl.BlockSpec((1, STATE_SIZE, z_wide), lambda i, place: (blocks - 1 - i, 0, 0)),
                whole(keys.shape),
                whole(values.shape),
                in_order,
                in_order,
                whole(tri.shape),
                whole(params.shape),
                whole(spread.shape),
                whole(skip.shape),
            ],
            out_specs=[by_hop(wide), whole((8, LANES))],
            scratch_shapes=[
                pltpu.VMEM((tokens, HEAD_SIZE), F32),
                pltpu.VMEM((tokens, HEAD_SIZE), F32),
                pltpu.VMEM((STATE_SIZE, z_wide), F32),
            ],
        ),
        out_shape=[
            jax.ShapeDtypeStruct((tokens, wide), BF16),
            jax.ShapeDtypeStruct((8, LANES), F32),
        ],
        compiler_params=pltpu.CompilerParams(vmem_limit_bytes=VMEM_LIMIT),
        cost_estimate=pl.CostEstimate(
            flops=20_000_000_000, bytes_accessed=30_000_000, transcendentals=0
        ),
        name="mixer_backward",
    )(place, mixed, joint, states, keys, values, cosine, sine, tri, params, spread, skip)


def pack_kernel(cuts, starts_ref, *refs):
    sources = refs[: max(c[0] for out in cuts for c in out) + 1]
    outs = refs[len(sources) : len(sources) + len(cuts)]
    semaphores = refs[-1]
    copies, at = [], 0
    for out, ref in zip(cuts, outs):
        column = 0
        for source, wide in out:
            start = pl.multiple_of(starts_ref[at], LANES)
            copies.append(
                pltpu.make_async_copy(
                    sources[source].at[:, pl.ds(start, wide)],
                    ref.at[:, pl.ds(column, wide)],
                    semaphores.at[at],
                )
            )
            column += wide
            at += 1
    for copy in copies:
        copy.start()
    for copy in copies:
        copy.wait()


def pack_columns(sources, cuts):
    starts = jnp.stack([start for out in cuts for _, start, _ in out]).astype(jnp.int32)
    rows = sources[0].shape[0]
    anywhere = pl.BlockSpec(memory_space=pl.ANY)
    return pl.pallas_call(
        functools.partial(pack_kernel, [[(s, w) for s, _, w in out] for out in cuts]),
        grid_spec=pltpu.PrefetchScalarGridSpec(
            num_scalar_prefetch=1,
            grid=(1,),
            in_specs=[anywhere] * len(sources),
            out_specs=[
                pl.BlockSpec((rows, sum(w for _, _, w in out)), lambda i, starts: (0, 0))
                for out in cuts
            ],
            scratch_shapes=[pltpu.SemaphoreType.DMA((starts.shape[0],))],
        ),
        out_shape=[
            jax.ShapeDtypeStruct((rows, sum(w for _, _, w in out)), BF16) for out in cuts
        ],
        compiler_params=pltpu.CompilerParams(vmem_limit_bytes=VMEM_LIMIT),
        cost_estimate=pl.CostEstimate(
            flops=0, bytes_accessed=20_000_000, transcendentals=0
        ),
        name="pack_columns",
    )(starts, *sources)


def dense_cost(flops, *arrays):
    return pl.CostEstimate(
        flops=flops,
        bytes_accessed=sum(math.prod(a.shape) * a.dtype.itemsize for a in arrays),
        transcendentals=0,
    )


def mixer_in_kernel(count, place_ref, gain_ref, w_ref, *refs):
    parts = refs[: 2 * count - 1]
    out_ref, normed_ref, scaled_ref = refs[2 * count - 1 :]
    size = parts[0].shape[0]

    @pl.when(pl.program_id(0) == 0)
    def _():
        for hop in range(count):
            if hop == 0:
                rows = parts[0][...].astype(F32)
            else:
                rows = jnp.where(
                    place_ref[0] >= hop,
                    parts[hop][...].astype(F32),
                    parts[2 * count - 1 - hop][...].astype(F32),
                )
            scaled = rows * lax.rsqrt(jnp.mean(rows * rows, axis=-1, keepdims=True) + EPSILON)
            scaled_ref[hop * size : (hop + 1) * size, :] = scaled.astype(BF16)
            normed_ref[hop * size : (hop + 1) * size, :] = (scaled * gain_ref[...]).astype(BF16)

    out_ref[...] = mul(normed_ref[...], w_ref[...], 1, 0)


def mixer_in(place, own, ups, downs, gain, weight, wide):
    size, depth = own.shape
    count = len(ups) + 1
    tokens = size * count
    tile = max(t for t in range(LANES, 1025, LANES) if wide % t == 0)

    def fixed(shape):
        return pl.BlockSpec(shape, lambda j, place: (0, 0))

    outs = [
        jax.ShapeDtypeStruct((tokens, wide), F32),
        jax.ShapeDtypeStruct((tokens, depth), BF16),
        jax.ShapeDtypeStruct((tokens, depth), BF16),
    ]
    return pl.pallas_call(
        functools.partial(mixer_in_kernel, count),
        grid_spec=pltpu.PrefetchScalarGridSpec(
            num_scalar_prefetch=1,
            grid=(wide // tile,),
            in_specs=[
                fixed((1, depth)),
                pl.BlockSpec((depth, tile), lambda j, place: (0, j)),
            ]
            + [fixed((size, depth))] * (2 * count - 1),
            out_specs=[
                pl.BlockSpec((tokens, tile), lambda j, place: (0, j)),
                fixed((tokens, depth)),
                fixed((tokens, depth)),
            ],
        ),
        out_shape=outs,
        compiler_params=pltpu.CompilerParams(vmem_limit_bytes=VMEM_LIMIT),
        cost_estimate=dense_cost(2 * tokens * depth * wide, weight, *outs),
        name="mixer_in",
    )(place, gain, weight, own, *ups, *downs)


def ffn_kernel(
    own_ref,
    other_ref,
    act_grad_ref,
    gate_ref,
    up_ref,
    activated_ref,
    grad_gate_ref,
    grad_up_ref,
    rows_ref,
):
    @pl.when(pl.program_id(0) == 0)
    def _():
        rows_ref[: own_ref.shape[0], :] = own_ref[...]
        rows_ref[own_ref.shape[0] :, :] = other_ref[...]

    rows = rows_ref[...]
    gate = mul(rows, gate_ref[...], 1, 0)
    up = mul(rows, up_ref[...], 1, 0)
    grad = act_grad_ref[...]
    sigmoid = jax.nn.sigmoid(gate)
    silu = gate * sigmoid
    activated_ref[...] = (silu * up).astype(BF16)
    grad_gate_ref[...] = (grad * up * (sigmoid * (1.0 + gate * (1.0 - sigmoid)))).astype(BF16)
    grad_up_ref[...] = (grad * silu).astype(BF16)


def ffn_inner(own, other, act_grad, weights):
    tokens, depth = 2 * own.shape[0], own.shape[1]
    units = act_grad.shape[1]
    tile = 256
    tiles = units // tile
    out = jax.ShapeDtypeStruct((tokens, units), BF16)
    by_unit = pl.BlockSpec((tokens, tile), lambda j: (0, j))
    return pl.pallas_call(
        ffn_kernel,
        grid=(tiles,),
        in_specs=[
            pl.BlockSpec(own.shape, lambda j: (0, 0)),
            pl.BlockSpec(own.shape, lambda j: (0, 0)),
            by_unit,
            pl.BlockSpec((depth, tile), lambda j: (0, tiles + j)),
            pl.BlockSpec((depth, tile), lambda j: (0, 2 * tiles + j)),
        ],
        out_specs=[by_unit] * 3 + [pl.BlockSpec((tokens, depth), lambda j: (0, 0))],
        out_shape=[out] * 3 + [jax.ShapeDtypeStruct((tokens, depth), BF16)],
        compiler_params=pltpu.CompilerParams(vmem_limit_bytes=VMEM_LIMIT),
        cost_estimate=dense_cost(4 * tokens * depth * units, weights, out, out, out),
        name="ffn_inner",
    )(own, other, act_grad, weights, weights)


def ffn_back_kernel(count, *refs):
    own_ref, other_ref = refs[-2:]
    total = mul(refs[0][...], refs[count][...], 1, 1)
    for i in range(1, count):
        total = total + mul(refs[i][...], refs[count + i][...], 1, 1)
    half = total.shape[0] // 2
    own_ref[...] = total[:half]
    other_ref[...] = total[half:].astype(BF16)


def ffn_back(grads, weights, columns):
    tokens, units = grads[0].shape
    depth = weights.shape[0]
    tile = 256
    half = pl.BlockSpec((tokens // 2, tile), lambda j: (0, j))
    return pl.pallas_call(
        functools.partial(ffn_back_kernel, len(grads)),
        grid=(depth // tile,),
        in_specs=[pl.BlockSpec((tokens, units), lambda j: (0, 0)) for _ in grads]
        + [pl.BlockSpec((tile, units), lambda j, c=c: (j, c)) for c in columns],
        out_specs=[half, half],
        out_shape=[
            jax.ShapeDtypeStruct((tokens // 2, depth), F32),
            jax.ShapeDtypeStruct((tokens // 2, depth), BF16),
        ],
        compiler_params=pltpu.CompilerParams(vmem_limit_bytes=VMEM_LIMIT),
        cost_estimate=dense_cost(2 * len(grads) * tokens * depth * units, weights),
        name="ffn_back",
    )(*grads, *[weights for _ in columns])


def joint_kernel(count, place_ref, w_ref, *refs):
    parts = refs[: 2 * count - 1]
    out_ref, rows_ref = refs[2 * count - 1 :]
    size = parts[0].shape[0]

    @pl.when(pl.program_id(0) == 0)
    def _():
        rows_ref[:size, :] = parts[0][...]
        for hop in range(1, count):
            rows_ref[hop * size : (hop + 1) * size, :] = jnp.where(
                place_ref[0] >= hop,
                parts[hop][...].astype(F32),
                parts[2 * count - 1 - hop][...].astype(F32),
            ).astype(BF16)

    out_ref[...] = mul(rows_ref[...], w_ref[...], 1, 0)


def joint(place, own, ups, downs, weight):
    size, depth = own.shape
    count = len(ups) + 1
    tokens, wide = size * count, weight.shape[1]
    tile = min(wide, 512)

    def fixed(shape):
        return pl.BlockSpec(shape, lambda j, place: (0, 0))

    outs = [
        jax.ShapeDtypeStruct((tokens, wide), F32),
        jax.ShapeDtypeStruct((tokens, depth), BF16),
    ]
    return pl.pallas_call(
        functools.partial(joint_kernel, count),
        grid_spec=pltpu.PrefetchScalarGridSpec(
            num_scalar_prefetch=1,
            grid=(wide // tile,),
            in_specs=[pl.BlockSpec((depth, tile), lambda j, place: (0, j))]
            + [fixed((size, depth))] * (2 * count - 1),
            out_specs=[
                pl.BlockSpec((tokens, tile), lambda j, place: (0, j)),
                fixed((tokens, depth)),
            ],
        ),
        out_shape=outs,
        compiler_params=pltpu.CompilerParams(vmem_limit_bytes=VMEM_LIMIT),
        cost_estimate=dense_cost(2 * tokens * depth * wide, weight, *outs),
        name="joint",
    )(place, weight, own, *ups, *downs)


def mixer_out_kernel(grad_ref, w_ref, scaled_ref, gain_ref, own_ref, *other_refs):
    total = mul(grad_ref[...], w_ref[:, : grad_ref.shape[1]], 1, 1)
    size = own_ref.shape[0]
    own_ref[...] = total[:size]
    for hop, ref in enumerate(other_refs, 1):
        ref[...] = total[hop * size : (hop + 1) * size].astype(BF16)
    sums = jnp.sum(total * scaled_ref[...].astype(F32), axis=0, keepdims=True)
    gain_ref[...] = jnp.broadcast_to(sums, gain_ref.shape)


def mixer_out(grad, weights, scaled, size):
    tokens, wide = grad.shape
    depth = weights.shape[0]
    tile = 256
    outs = [jax.ShapeDtypeStruct((8, depth), F32), jax.ShapeDtypeStruct((size, depth), F32)]
    outs += [jax.ShapeDtypeStruct((size, depth), BF16)] * (tokens // size - 1)
    return pl.pallas_call(
        mixer_out_kernel,
        grid=(depth // tile,),
        in_specs=[
            pl.BlockSpec((tokens, wide), lambda j: (0, 0)),
            pl.BlockSpec((tile, weights.shape[1]), lambda j: (j, 0)),
            pl.BlockSpec((tokens, tile), lambda j: (0, j)),
        ],
        out_specs=[pl.BlockSpec((o.shape[0], tile), lambda j: (0, j)) for o in outs],
        out_shape=outs,
        compiler_params=pltpu.CompilerParams(vmem_limit_bytes=VMEM_LIMIT),
        cost_estimate=dense_cost(2 * tokens * depth * wide, grad, weights, scaled, *outs),
        name="mixer_out",
    )(grad, weights, scaled)


def outer_kernel(pairs, rider_at, *refs):
    out_ref = refs[-1]
    at = 0
    for left, right, start, wide in pairs:
        value = mul(refs[left][...], refs[right][:, start : start + wide], 0, 0)
        out_ref[:, at : at + wide] = value.astype(BF16)
        at += wide
    if rider_at is not None:
        riders = refs[-2][...]
        rows = riders.shape[0]
        for k in range(out_ref.shape[0] // rows):
            block = out_ref[k * rows : (k + 1) * rows, rider_at : rider_at + LANES]
            out_ref[k * rows : (k + 1) * rows, rider_at : rider_at + LANES] = block + riders


def weight_grads(pairs, riders=None, rider_at=None):
    operands = []

    def position(array):
        for i, held in enumerate(operands):
            if held is array:
                return i
        operands.append(array)
        return len(operands) - 1

    lefts = [position(left) for left, _, _, _ in pairs]
    n_left = len(operands)
    rights = [position(right) for _, right, _, _ in pairs]
    plan = [(l, r, p[2], p[3]) for l, r, p in zip(lefts, rights, pairs)]
    tokens, depth = operands[0].shape
    wide = sum(p[3] for p in pairs)
    tile = 256
    operands += [] if riders is None else [riders]
    specs = [pl.BlockSpec((a.shape[0], tile), lambda j: (0, j)) for a in operands[:n_left]] + [
        pl.BlockSpec(a.shape, lambda j: (0, 0)) for a in operands[n_left:]
    ]
    out = jax.ShapeDtypeStruct((depth, wide), BF16)
    return pl.pallas_call(
        functools.partial(outer_kernel, plan, rider_at),
        grid=(depth // tile,),
        in_specs=specs,
        out_specs=pl.BlockSpec((tile, wide), lambda j: (j, 0)),
        out_shape=out,
        compiler_params=pltpu.CompilerParams(vmem_limit_bytes=VMEM_LIMIT),
        cost_estimate=dense_cost(2 * tokens * depth * wide, out, *operands),
        name="weight_grads",
    )(*operands)


def unpack_kernel(places, q_heads, heads, gain_columns, count, place_ref, *refs):
    arrays = 2 * count - 1
    groups = [refs[i : i + arrays] for i in range(0, len(refs) - 4, arrays)]
    mix_ref, attn_ref, ssm_ref, extra_ref = refs[-4:]
    place = place_ref[0]
    q_wide, z_wide = q_heads * HEAD_SIZE, heads * MIXER_HEAD_SIZE
    group = QUERY_HEADS // KEY_VALUE_HEADS
    key_at = QUERY_HEADS * HEAD_SIZE
    kv_wide = KEY_VALUE_HEADS * HEAD_SIZE
    z_at = key_at + 2 * kv_wide
    x_at = z_at + MIXER_HEADS * MIXER_HEAD_SIZE
    b_at = x_at + MIXER_HEADS * MIXER_HEAD_SIZE
    step = mix_ref.shape[0]
    lane = lax.broadcasted_iota(jnp.int32, (step, LANES), 1)
    head_lane = heads + gain_columns
    head_at = MIXER_HEADS + gain_columns
    shared = jnp.zeros((step, 2 * STATE_SIZE), F32)
    extra = jnp.zeros((step, LANES), F32)
    mix_ref[:, key_at : key_at + 2 * kv_wide] = jnp.zeros((step, 2 * kv_wide), F32)

    for hop in range(count):
        source = lax.rem(place - hop + count, count)

        def of(name, hop=hop):
            group, start, wide = places[name]
            parts = groups[group]
            if hop == 0:
                return parts[0][:, start : start + wide].astype(F32)
            up = parts[hop][:, start : start + wide].astype(F32)
            down = parts[2 * count - 1 - hop][:, start : start + wide].astype(F32)
            return jnp.where(place >= hop, up, down)

        def put(ref, start, value):
            ref[:, pl.ds(pl.multiple_of(start, LANES), value.shape[1])] = value

        put(mix_ref, source * q_wide, of("q"))
        put(mix_ref, z_at + source * z_wide, of("z"))
        put(mix_ref, x_at + source * z_wide, of("x"))
        put(attn_ref, source * q_wide, of("attn"))
        put(ssm_ref, source * z_wide, of("ssm"))
        shared = shared + of("bc")
        which = lax.div(source * q_heads, group)
        for name, base in (("k", key_at), ("v", key_at + kv_wide)):
            at = pl.ds(pl.multiple_of(base + which * HEAD_SIZE, LANES), HEAD_SIZE)
            mix_ref[:, at] += of(name)
        small = of("dt")
        own = jnp.where(lane < heads, small, 0.0)
        gains = jnp.where((lane >= heads) & (lane < head_lane), small, 0.0)
        column = jnp.where(lane == head_lane, small, 0.0)
        extra = (
            extra
            + pltpu.roll(own, source * heads, 1)
            + pltpu.roll(gains, MIXER_HEADS - heads, 1)
            + pltpu.roll(column, head_at - head_lane + source, 1)
        )
    mix_ref[:, b_at:] = shared
    extra_ref[...] = extra


def unpack_mixer(place, groups, places, q_heads, heads, gain_columns):
    count = len(groups[0][1]) + 1
    rows = groups[0][0].shape[0]
    step = min(rows, 64)
    widths = (
        QUERY_HEADS * HEAD_SIZE
        + 2 * KEY_VALUE_HEADS * HEAD_SIZE
        + 2 * MIXER_HEADS * MIXER_HEAD_SIZE
        + 2 * STATE_SIZE,
        QUERY_HEADS * HEAD_SIZE,
        MIXER_HEADS * MIXER_HEAD_SIZE,
        LANES,
    )
    operands = [part for own, ups, downs in groups for part in (own, *ups, *downs)]

    def spec(columns):
        return pl.BlockSpec((step, columns), lambda i, place: (i, 0))

    return pl.pallas_call(
        functools.partial(unpack_kernel, places, q_heads, heads, gain_columns, count),
        grid_spec=pltpu.PrefetchScalarGridSpec(
            num_scalar_prefetch=1,
            grid=(rows // step,),
            in_specs=[spec(o.shape[1]) for o in operands],
            out_specs=[spec(w) for w in widths],
        ),
        out_shape=[jax.ShapeDtypeStruct((rows, w), F32) for w in widths],
        compiler_params=pltpu.CompilerParams(vmem_limit_bytes=VMEM_LIMIT),
        cost_estimate=pl.CostEstimate(
            flops=100_000_000, bytes_accessed=26_000_000, transcendentals=0
        ),
        name="unpack_mixer",
    )(place, *operands)


def unpack_ffn_kernel(count, place_ref, *refs):
    arrays = 2 * count - 1
    groups = (refs[:arrays], refs[arrays : 2 * arrays])
    outs = refs[2 * arrays :]
    place = place_ref[0]
    chunk = groups[0][0].shape[0]
    half = outs[0].shape[1] // 2
    quarter = half // 2
    pieces = (
        (0, 0, 0, half, 0),
        (1, 0, half, quarter, 0),
        (1, 1, 0, quarter, quarter),
        (2, 1, quarter, half, 0),
    )
    for hop in range(count):
        source = lax.rem(place - hop + count, count)
        row = pl.multiple_of(lax.div(source, 2) * chunk, chunk)
        side = lax.rem(source, 2) * half
        for out, group, start, wide, offset in pieces:
            parts = groups[group]
            value = parts[0][:, start : start + wide] if hop == 0 else None
            if hop:
                up = parts[hop][:, start : start + wide]
                down = parts[arrays - hop][:, start : start + wide]
                value = jnp.where(place >= hop, up.astype(F32), down.astype(F32))
            column = pl.multiple_of(side + offset, LANES)
            outs[out][pl.ds(row, chunk), pl.ds(column, wide)] = value.astype(F32)


def unpack_ffn(place, groups, units):
    count = len(groups[0][1]) + 1
    rows = groups[0][0].shape[0] * (count // 2)
    operands = [part for own, ups, downs in groups for part in (own, *ups, *downs)]

    def fixed(shape):
        return pl.BlockSpec(shape, lambda i, place: (0, 0))

    return pl.pallas_call(
        functools.partial(unpack_ffn_kernel, count),
        grid_spec=pltpu.PrefetchScalarGridSpec(
            num_scalar_prefetch=1,
            grid=(1,),
            in_specs=[fixed(o.shape) for o in operands],
            out_specs=[fixed((rows, units))] * 3,
        ),
        out_shape=[jax.ShapeDtypeStruct((rows, units), F32)] * 3,
        compiler_params=pltpu.CompilerParams(vmem_limit_bytes=VMEM_LIMIT),
        cost_estimate=pl.CostEstimate(
            flops=100_000_000, bytes_accessed=22_000_000, transcendentals=0
        ),
        name="unpack_ffn",
    )(place, *operands)


def per_device(
    hidden_in,
    w_mix,
    w_dt,
    w_attn_out,
    w_ssm_out,
    w_gate,
    w_up,
    w_down,
    norm_gains,
    dt_bias,
    a_log,
    skip_scale,
    cotangent,
):
    w_mix, w_dt, w_attn_out, w_ssm_out = w_mix[0], w_dt[0], w_attn_out[0], w_ssm_out[0]
    w_gate, w_up, w_down = w_gate[0], w_up[0], w_down[0]
    gain_mix, gain_ffn = norm_gains[0, 0], norm_gains[0, 1]
    count, place = lax.axis_size("ctx"), lax.axis_index("ctx")
    piece, width = hidden_in.shape[1], hidden_in.shape[2]
    tokens = piece * count
    rows = w_mix.shape[0]
    hidden_units = w_gate.shape[1]
    q_heads = QUERY_HEADS // count
    group = QUERY_HEADS // KEY_VALUE_HEADS
    kv_head = (place * q_heads) // group
    heads = MIXER_HEADS // count
    q_wide, z_wide = q_heads * HEAD_SIZE, heads * MIXER_HEAD_SIZE
    key_at = QUERY_HEADS * HEAD_SIZE
    value_at = key_at + KEY_VALUE_HEADS * HEAD_SIZE
    z_at = value_at + KEY_VALUE_HEADS * HEAD_SIZE
    x_at = z_at + MIXER_HEADS * MIXER_HEAD_SIZE
    b_at = x_at + MIXER_HEADS * MIXER_HEAD_SIZE
    names = ("q", "k", "v", "z", "x", "b", "c", "dt")
    sizes = (q_wide, HEAD_SIZE, HEAD_SIZE, z_wide, z_wide, STATE_SIZE, STATE_SIZE, LANES)
    cuts, mix_wide = {}, 0
    for name, size in zip(names, sizes):
        cuts[name] = mix_wide
        mix_wide += size

    half = place % 2
    half_units = hidden_units // 2
    own_dt = lax.dynamic_slice(w_dt, (0, place * heads), (rows, heads))
    own_dt = jnp.pad(own_dt, ((0, 0), (0, LANES - heads)))
    here = jnp.reshape(place, (1,)).astype(jnp.int32)
    mix_starts = (
        (place * q_wide, q_wide),
        (key_at + kv_head * HEAD_SIZE, HEAD_SIZE),
        (value_at + kv_head * HEAD_SIZE, HEAD_SIZE),
        (z_at + place * z_wide, z_wide),
        (x_at + place * z_wide, z_wide),
        (b_at + 0 * place, 2 * STATE_SIZE),
    )
    from_half = (half * half_units, half_units)
    (mixer_own,) = pack_columns(
        (w_mix, own_dt, w_attn_out, w_ssm_out),
        (
            [(0,) + cut for cut in mix_starts]
            + [(1, 0 * place, LANES), (2, place * q_wide, q_wide), (3, place * z_wide, z_wide)],
        ),
    )
    (ffn_own,) = pack_columns(
        (w_gate, w_up, w_down), ([(2,) + from_half, (0,) + from_half, (1,) + from_half],)
    )
    w_mixer, w_ffn = gather_rows(mixer_own), gather_rows(ffn_own)
    w_out = w_mixer[:, mix_wide:]
    w_down_half = w_ffn[:, :half_units]

    blocks = tokens // piece

    hidden_own = hidden_in.reshape(piece, width)
    hidden_ups, hidden_downs = finish(line_gather(hidden_own))
    mixed, normed, scaled_in = mixer_in(
        here, hidden_own, hidden_ups, hidden_downs, gain_mix[None, :], w_mixer, mix_wide
    )
    own = [lax.dynamic_slice_in_dim(p[0], place * heads, heads) for p in (dt_bias, a_log, skip_scale)]
    tables = mixer_tables(tokens, piece, heads, *own)
    branch_in, states, keys, values = mixer_forward(
        here, mixed, tables, cuts, q_heads, heads, blocks
    )
    cot_own = cotangent.reshape(piece, width)
    cot_swap = swap_pair(after(cot_own, mixed))
    branch_in, cot_swap = lax.optimization_barrier((branch_in, cot_swap))
    cot_pair = jnp.concatenate([cot_own, cot_swap], axis=0)
    halves = []
    for half_rows in (w_out[: width // 2], w_out[width // 2 :]):
        terms = [None] * count

        def branch_term(rows_in, hop, half_rows=half_rows):
            return dot(rows_in[hop * piece : (hop + 1) * piece], half_rows, 1, 1)

        for hop in (1, count - 1):
            terms[hop] = branch_term(branch_in, hop)
        branch_line = Chain(line_sum(terms))
        flight = Flight(branch_line)
        late_in = after(branch_in, *flight.values)
        for hop in range(count):
            if terms[hop] is None:
                terms[hop] = branch_term(late_in, hop)
        halves.append((branch_line, flight))
    for branch_line, flight in halves:
        flight.land()
    for branch_line, _ in halves:
        while live(branch_line):
            advance(branch_line)
    branch = jnp.concatenate([branch_line.result for branch_line, _ in halves], axis=1)
    middle = hidden_own.astype(F32) + branch
    grad_act = dot(cot_pair, w_down_half, 1, 0)

    inverse_ffn = inverse_rms(middle)
    normed_ffn = (middle * inverse_ffn * gain_ffn).astype(BF16)
    normed_swap, grad_act = lax.optimization_barrier((swap_pair(normed_ffn), grad_act))
    activated, grad_gate, grad_up, normed_pair = ffn_inner(
        normed_ffn, normed_swap, grad_act, w_ffn
    )
    grad_normed_own, grad_normed_other = ffn_back((grad_gate, grad_up), w_ffn, (1, 2))
    grad_swap = swap_pair(grad_normed_other)
    activated, grad_gate, grad_up = lax.optimization_barrier(
        (activated, grad_gate, grad_up, grad_normed_other)
    )[:3]
    quarter = half_units // 2
    grad_w_first = weight_grads(
        ((normed_pair, grad_gate, 0, half_units), (normed_pair, grad_up, 0, quarter))
    )
    grad_swap, grad_w_first = lax.optimization_barrier((grad_swap, grad_w_first))
    grad_w_first = scatter_rows(grad_w_first)
    grad_normed_ffn = grad_normed_own + grad_swap.astype(F32)

    grad_middle = cot_own.astype(F32) + rms_pull(middle, inverse_ffn, gain_ffn, grad_normed_ffn)
    grad_gain_ffn = jnp.sum(grad_normed_ffn * middle * inverse_ffn, axis=0)
    branch_own = grad_middle.astype(BF16)
    branch_line = Chain(line_gather(branch_own))
    late_activated, late_up = lax.optimization_barrier((activated, grad_up, branch_own))[:2]
    grad_w_second = weight_grads(
        ((normed_pair, late_up, quarter, quarter), (cot_pair, late_activated, 0, half_units))
    )
    (grad_w_second,) = advance(branch_line, beside=(grad_w_second,))
    out_half, out_other = ffn_back((after(activated, grad_w_second),), w_ffn, (0,))
    out_half, out_other = advance(branch_line, beside=(out_half, out_other))
    while branch_line.sends is not None:
        advance(branch_line)
    grad_joint, grad_branch = joint(here, branch_own, *branch_line.result, w_out)
    out_swap = swap_pair(after(out_other, *branch_line.result[0]))
    first = Chain(parity_gather(grad_w_first))
    grad_w_second = scatter_rows(after(grad_w_second, grad_w_first, grad_joint))

    grad_mixed, head_part = mixer_backward(
        here, mixed, grad_joint, states, keys, values, tables, cuts, q_heads, heads, blocks
    )
    grad_mixed, head_part, out_swap = advance(first, beside=(grad_mixed, head_part, out_swap))
    gain_rows, *dn_parts = mixer_out(grad_mixed, w_mixer, scaled_in, piece)
    gain_rows, *dn_parts = advance(first, beside=(gain_rows, *dn_parts))

    gain_columns = 2 * width // rows
    riders = jnp.concatenate(
        [
            jnp.zeros((rows, heads), F32),
            jnp.stack([gain_rows[0], grad_gain_ffn]).reshape(rows, gain_columns),
            jnp.pad(head_part[:3, :heads].reshape(3 * heads), (0, rows - 3 * heads))[:, None],
            jnp.zeros((rows, LANES - heads - gain_columns - 1), F32),
        ],
        axis=1,
    )
    grad_w_mixer = weight_grads(
        ((normed, grad_mixed, 0, mix_wide), (grad_branch, branch_in, 0, q_wide + z_wide)),
        riders.astype(BF16),
        cuts["dt"],
    )
    normed_sum = Chain(line_sum(dn_parts))
    (grad_w_mixer,) = advance(first, normed_sum, beside=(grad_w_mixer,))
    grad_w_mixer = scatter_rows(after(grad_w_mixer, grad_w_second))
    second = Chain(parity_gather(grad_w_second))
    advance(*live(second, first))
    while live(normed_sum):
        advance(*live(second, first, normed_sum))
    mixer = Chain(line_gather(after(grad_w_mixer, normed_sum.result)))
    while live(second, first):
        advance(*live(mixer, second, first))

    sealed = lax.optimization_barrier(
        (first.result, second.result, tuple(value for value, _ in mixer.sends))
    )
    outs = tuple(unpack_ffn(here, sealed[:2], hidden_units))
    outs = advance(*live(mixer), beside=outs)
    sealed = lax.optimization_barrier(
        (normed_sum.result, out_swap, tuple(value for value, _ in mixer.sends))
    )
    hidden_out = (middle + (out_half + sealed[1].astype(F32))).astype(BF16)
    hidden_f32 = hidden_own.astype(F32)
    grad_hidden = grad_middle + rms_pull(
        hidden_f32, inverse_rms(hidden_f32), gain_mix, sealed[0]
    )
    hidden_out, grad_hidden = advance(mixer, beside=(hidden_out, grad_hidden))
    while live(mixer):
        advance(mixer)
    out_gate, out_up, out_down = outs

    places = {name: (0, cuts[name], size) for name, size in zip(names, sizes)}
    places["bc"] = (0, cuts["b"], 2 * STATE_SIZE)
    places["attn"] = (0, mix_wide, q_wide)
    places["ssm"] = (0, mix_wide + q_wide, z_wide)
    out_mix, out_attn, out_ssm, extra = unpack_mixer(
        here, ((grad_w_mixer,) + mixer.result,), places, q_heads, heads, gain_columns
    )
    head_at = MIXER_HEADS + gain_columns
    gain_sums = extra[:, MIXER_HEADS:head_at].reshape(norm_gains.shape)
    head_sums = extra[: 3 * heads, head_at : head_at + count].reshape(3, heads, count)
    head_sums = jnp.swapaxes(head_sums, 1, 2).reshape(3, MIXER_HEADS)

    return (
        hidden_out.reshape(hidden_in.shape),
        grad_hidden.reshape(hidden_in.shape),
        out_mix[None],
        extra[None, :, :MIXER_HEADS],
        out_attn[None],
        out_ssm[None],
        out_gate[None],
        out_up[None],
        out_down[None],
        gain_sums,
        head_sums[0][None],
        head_sums[1][None],
        head_sums[2][None],
    )


def solution(mesh):
    split, rows = P("fsdp", "ctx", None), P(None, "fsdp", None)
    return jax.shard_map(
        per_device,
        mesh=mesh,
        in_specs=(split,) + (rows,) * 7 + (P(),) * 4 + (split,),
        out_specs=(split, split) + (rows,) * 7 + (P(),) * 4,
        check_vma=False,
    )
```

```python
import functools
import math

import jax
import jax.numpy as jnp
from jax import lax
from jax.experimental import pallas as pl
from jax.experimental.pallas import tpu as pltpu
from jax.sharding import PartitionSpec as P

QUERY_HEADS = 8
KEY_VALUE_HEADS = 2
HEAD_SIZE = 128
MIXER_HEADS = 48
MIXER_HEAD_SIZE = 64
STATE_SIZE = 256
LANES = 128

EPSILON = 1e-05
THETA = 10000.0
SCALE = 1.0 / math.sqrt(HEAD_SIZE)
VMEM_LIMIT = 56 * 1024 * 1024
BF16 = jnp.bfloat16
F32 = jnp.float32


def swap_pair(value):
    count = lax.axis_size("ctx")
    return lax.ppermute(value, "ctx", [(i, i ^ 1) for i in range(count)])


def after(value, *earlier):
    return lax.optimization_barrier((value,) + earlier)[0]


class Chain:
    def __init__(self, steps):
        self.steps, self.sends, self.result = steps, next(steps), None

    def take(self, got):
        try:
            self.sends = self.steps.send(got)
        except StopIteration as stop:
            self.sends, self.result = None, stop.value


class Flight:
    def __init__(self, *chains):
        self.chains = chains
        sends = [send for chain in chains for send in chain.sends]
        self.values = lax.optimization_barrier(tuple(value for value, _ in sends))
        self.got = tuple(
            lax.ppermute(v, "ctx", pairs) for v, (_, pairs) in zip(self.values, sends)
        )

    def land(self, beside=()):
        sealed = lax.optimization_barrier(self.got + tuple(beside))
        got = sealed[: len(self.got)]
        for chain in self.chains:
            count = len(chain.sends)
            chain.take(got[:count])
            got = got[count:]
        return sealed[len(self.got) :]


def advance(*chains, beside=()):
    return Flight(*chains).land(beside)


def live(*chains):
    return [chain for chain in chains if chain.sends is not None]


def finish(steps):
    chain = Chain(steps)
    while chain.sends is not None:
        advance(chain)
    return chain.result


def line_gather(value):
    count = lax.axis_size("ctx")
    up = down = value
    ups, downs = [], []
    for hop in range(1, count):
        up, down = yield [
            (up, [(i, i + 1) for i in range(hop - 1, count - 1)]),
            (down, [(i + 1, i) for i in range(count - hop)]),
        ]
        ups.append(up)
        downs.append(down)
    return ups, downs


def in_hops(value, ups, downs):
    count, place = lax.axis_size("ctx"), lax.axis_index("ctx")
    return [value] + [
        jnp.where(place >= hop, ups[hop - 1], downs[count - hop - 1]) for hop in range(1, count)
    ]


def gather_ctx(value):
    return in_hops(value, *finish(line_gather(value)))


def line_sum(parts):
    count = len(parts)
    up = down = 0.0
    for hop in range(1, count):
        up, down = yield [
            ((parts[hop] + up).astype(BF16), [(i, i + 1) for i in range(hop)]),
            (
                (parts[count - hop] + down).astype(BF16),
                [(i, i - 1) for i in range(count - hop, count)],
            ),
        ]
        up, down = up.astype(F32), down.astype(F32)
    return parts[0] + up + down


def parity_sum(grad):
    count = lax.axis_size("ctx")
    members, member = count // 2, lax.axis_index("ctx") // 2
    chunk = grad.shape[0] // members
    got = yield [
        (
            lax.dynamic_slice_in_dim(grad, ((member + hop) % members) * chunk, chunk, 0),
            [(i, (i + 2 * hop) % count) for i in range(count)],
        )
        for hop in range(1, members)
    ]
    total = lax.dynamic_slice_in_dim(grad, member * chunk, chunk, 0).astype(F32)
    for block in got:
        total = total + block.astype(F32)
    return total.astype(BF16)


def parity_gather(grad):
    total = yield from parity_sum(grad)
    ups, downs = yield from line_gather(total)
    return total, ups, downs


def gather_rows(value):
    return lax.all_gather(value, "fsdp", axis=0, tiled=True)


def scatter_rows(value):
    return lax.psum_scatter(value, "fsdp", scatter_dimension=0, tiled=True)


def dot(left, right, left_dim, right_dim):
    return lax.dot_general(
        left, right, (((left_dim,), (right_dim,)), ((), ())), preferred_element_type=F32
    )


def inverse_rms(rows):
    return lax.rsqrt(jnp.mean(rows * rows, axis=-1, keepdims=True) + EPSILON)


def rms_pull(rows, inverse, gain, grad):
    scaled = grad * gain
    return inverse * (scaled - rows * inverse * inverse * jnp.mean(rows * scaled, -1, keepdims=True))


def lanes_split(value, terms):
    parts = []
    for _ in range(terms):
        part = value.astype(BF16)
        parts.append(part)
        value = value - part.astype(F32)
    return parts


def near_exact(left, right, dims, terms, split_right):
    total = None
    for part in lanes_split(right if split_right else left, terms):
        pair = (left, part) if split_right else (part, right)
        one = lax.dot_general(*pair, (dims, ((), ())), preferred_element_type=F32)
        total = one if total is None else total + one
    return total


def mul(left, right, left_dim, right_dim):
    return lax.dot_general(
        left, right, (((left_dim,), (right_dim,)), ((), ())), preferred_element_type=F32
    )


def turn(vectors, cosine, sine):
    return vectors * cosine + pltpu.roll(vectors, HEAD_SIZE // 2, 1) * sine


def softplus(value):
    return jnp.maximum(value, 0.0) + jnp.log1p(jnp.exp(-jnp.abs(value)))


def block_terms(mixed, cuts, tri, params, spread):
    size = mixed.shape[0]
    dt_in = mixed[:, cuts["dt"] : cuts["dt"] + LANES] + params[0:1, :]
    step = softplus(dt_in)
    rate = params[1:2, :]
    level = near_exact(tri, step * rate, ((1,), (0,)), 3, True)
    last = level[size - 1 : size, :]
    enter = jnp.exp(level)
    leave = jnp.exp(last - level)
    wide = near_exact(
        jnp.concatenate([enter, step, leave * step], axis=0), spread, ((1,), (0,)), 2, False
    )
    return dict(
        dt_in=dt_in,
        step=step,
        rate=rate,
        level=level,
        last=last,
        leave=leave,
        enter_wide=wide[:size],
        step_wide=wide[size : 2 * size],
        tail_wide=wide[2 * size :],
    )


def fading_of(level, level_t, head, causal):
    gap = level[:, head : head + 1] - level_t[head : head + 1, :]
    return jnp.exp(jnp.where(causal, gap, -1e30))


def square_causal(size):
    row = lax.broadcasted_iota(jnp.int32, (size, size), 0)
    col = lax.broadcasted_iota(jnp.int32, (size, size), 1)
    return row >= col


def stacked_heads(value, at, count):
    return jnp.concatenate(
        [value[:, at + h * HEAD_SIZE : at + (h + 1) * HEAD_SIZE] for h in range(count)], axis=0
    )


def unstacked(value, count):
    size = value.shape[0] // count
    return jnp.concatenate([value[h * size : (h + 1) * size] for h in range(count)], axis=1)


def visible_keys(q_heads, size, block):
    shape = (q_heads * size, (block + 1) * size)
    row = lax.broadcasted_iota(jnp.int32, shape, 0)
    col = lax.broadcasted_iota(jnp.int32, shape, 1)
    return (row % size) + block * size >= col


def mixer_forward_kernel(
    cuts,
    q_heads,
    heads,
    blocks,
    place_ref,
    mixed_ref,
    cos_ref,
    sin_ref,
    tri_ref,
    params_ref,
    spread_ref,
    skip_ref,
    out_ref,
    state_ref,
    keys_ref,
    values_ref,
    carry,
):
    block = pl.program_id(0)
    size = mixed_ref.shape[0]
    q_wide, z_wide = q_heads * HEAD_SIZE, heads * MIXER_HEAD_SIZE

    @pl.when(block == 0)
    def _():
        carry[...] = jnp.zeros_like(carry)

    mixed = mixed_ref
    cosine, sine = cos_ref[...], sin_ref[...]
    here = pl.ds(pl.multiple_of(block * size, size), size)
    keys_ref[here, :] = turn(
        mixed[:, cuts["k"] : cuts["k"] + HEAD_SIZE], cosine, sine
    ).astype(BF16)
    values_ref[here, :] = mixed[:, cuts["v"] : cuts["v"] + HEAD_SIZE].astype(BF16)
    queries = jnp.concatenate(
        [
            turn(mixed[:, h * HEAD_SIZE : (h + 1) * HEAD_SIZE], cosine, sine)
            for h in range(q_heads)
        ],
        axis=0,
    ).astype(BF16)

    for at in range(blocks):

        @pl.when(block == at)
        def _(at=at):
            span = (at + 1) * size
            raw = mul(queries, keys_ref[:span, :], 1, 1) * SCALE
            logits = jnp.where(visible_keys(q_heads, size, at), raw, -1e30)
            weights = jnp.exp(logits - jnp.max(logits, axis=-1, keepdims=True))
            total = jnp.sum(weights, axis=-1, keepdims=True)
            attended = mul(weights.astype(BF16), values_ref[:span, :], 1, 0) / total
            out_ref[:, :q_wide] = unstacked(attended, q_heads).astype(BF16)

    terms = block_terms(mixed, cuts, tri_ref[...], params_ref, spread_ref[...])
    x = mixed[:, cuts["x"] : cuts["x"] + z_wide]
    b_rows = mixed[:, cuts["b"] : cuts["b"] + STATE_SIZE].astype(BF16)
    c_rows = mixed[:, cuts["c"] : cuts["c"] + STATE_SIZE].astype(BF16)
    causal = square_causal(size)
    pairing = mul(c_rows, b_rows, 1, 1)
    level = terms["level"]
    level_t = level.T
    x_step = (x * terms["step_wide"]).astype(BF16)
    first = lax.broadcasted_iota(jnp.int32, (size, LANES), 1) < MIXER_HEAD_SIZE
    inside = []
    for pair in range(heads // 2):
        both = x_step[:, pair * LANES : (pair + 1) * LANES]
        sides = []
        for head in (2 * pair, 2 * pair + 1):
            mixing = (fading_of(level, level_t, head, causal) * pairing).astype(BF16)
            sides.append(mul(mixing, both, 1, 0))
        inside.append(jnp.where(first, sides[0], sides[1]))
    state = carry[...]
    state_ref[0] = state
    full = (
        jnp.concatenate(inside, axis=1)
        + terms["enter_wide"] * mul(c_rows, state.astype(BF16), 1, 0)
        + skip_ref[...] * x
    )
    z = mixed[:, cuts["z"] : cuts["z"] + z_wide]
    out_ref[:, q_wide:] = (full * z * jax.nn.sigmoid(z)).astype(BF16)
    fresh = mul(b_rows, (x * terms["tail_wide"]).astype(BF16), 0, 0)
    carry[...] = terms["enter_wide"][size - 1 : size, :] * state + fresh


def mixer_backward_kernel(
    cuts,
    q_heads,
    heads,
    blocks,
    place_ref,
    mixed_ref,
    joint_ref,
    state_ref,
    keys_ref,
    values_ref,
    cos_ref,
    sin_ref,
    tri_ref,
    params_ref,
    spread_ref,
    skip_ref,
    out_ref,
    head_ref,
    grad_keys,
    grad_values,
    carry,
):
    block = blocks - 1 - pl.program_id(0)
    size = mixed_ref.shape[0]
    q_wide, z_wide = q_heads * HEAD_SIZE, heads * MIXER_HEAD_SIZE

    @pl.when(block == blocks - 1)
    def _():
        carry[...] = jnp.zeros_like(carry)
        grad_keys[...] = jnp.zeros_like(grad_keys)
        grad_values[...] = jnp.zeros_like(grad_values)
        head_ref[...] = jnp.zeros_like(head_ref)

    mixed, joint = mixed_ref, joint_ref
    cosine, sine = cos_ref[...], sin_ref[...]
    queries = jnp.concatenate(
        [
            turn(mixed[:, h * HEAD_SIZE : (h + 1) * HEAD_SIZE], cosine, sine)
            for h in range(q_heads)
        ],
        axis=0,
    ).astype(BF16)
    grad_out = stacked_heads(joint, 0, q_heads).astype(BF16)

    for at in range(blocks):

        @pl.when(block == at)
        def _(at=at):
            span = (at + 1) * size
            keys, values = keys_ref[:span, :], values_ref[:span, :]
            raw = mul(queries, keys, 1, 1) * SCALE
            logits = jnp.where(visible_keys(q_heads, size, at), raw, -1e30)
            weights = jnp.exp(logits - jnp.max(logits, axis=-1, keepdims=True))
            probs = weights / jnp.sum(weights, axis=-1, keepdims=True)
            grad_probs = mul(grad_out, values, 1, 1)
            delta = jnp.sum(probs * grad_probs, axis=-1, keepdims=True)
            grad_raw = (probs * (grad_probs - delta) * SCALE).astype(BF16)
            grad_queries = mul(grad_raw, keys, 1, 0)
            for h in range(q_heads):
                out_ref[:, h * HEAD_SIZE : (h + 1) * HEAD_SIZE] = turn(
                    grad_queries[h * size : (h + 1) * size], cosine, -sine
                ).astype(BF16)
            grad_keys[:span, :] += mul(grad_raw, queries, 0, 0)
            grad_values[:span, :] += mul(probs.astype(BF16), grad_out, 0, 0)

    here = pl.ds(pl.multiple_of(block * size, size), size)
    out_ref[:, cuts["k"] : cuts["k"] + HEAD_SIZE] = turn(
        grad_keys[here, :], cosine, -sine
    ).astype(BF16)
    out_ref[:, cuts["v"] : cuts["v"] + HEAD_SIZE] = grad_values[here, :].astype(BF16)

    tri, spread = tri_ref[...], spread_ref[...]
    terms = block_terms(mixed, cuts, tri, params_ref, spread)
    x = mixed[:, cuts["x"] : cuts["x"] + z_wide]
    z = mixed[:, cuts["z"] : cuts["z"] + z_wide]
    b_rows = mixed[:, cuts["b"] : cuts["b"] + STATE_SIZE].astype(BF16)
    c_rows = mixed[:, cuts["c"] : cuts["c"] + STATE_SIZE].astype(BF16)
    skip = skip_ref[...]
    causal = square_causal(size)
    pairing = mul(c_rows, b_rows, 1, 1)
    level = terms["level"]
    level_t = level.T
    enter_wide, step_wide, tail_wide = (
        terms["enter_wide"],
        terms["step_wide"],
        terms["tail_wide"],
    )
    x_step = (x * step_wide).astype(BF16)
    grad_gated = joint[:, q_wide:]
    sigmoid = jax.nn.sigmoid(z)
    grad_y = grad_gated * z * sigmoid
    grad_y16 = grad_y.astype(BF16)
    first = lax.broadcasted_iota(jnp.int32, (size, LANES), 1) < MIXER_HEAD_SIZE
    inside, grad_x_step = [], []
    grad_pairing = jnp.zeros((size, size), F32)
    none = jnp.zeros((size, LANES), BF16)
    for pair in range(heads // 2):
        lanes = slice(pair * LANES, (pair + 1) * LANES)
        both, grad_both = x_step[:, lanes], grad_y16[:, lanes]
        ys, xs = [], []
        for side, head in enumerate((2 * pair, 2 * pair + 1)):
            fading = fading_of(level, level_t, head, causal)
            mixing = (fading * pairing).astype(BF16)
            ys.append(mul(mixing, both, 1, 0))
            xs.append(mul(mixing, grad_both, 0, 0))
            alone = jnp.where(first == (side == 0), grad_both, none)
            grad_pairing = grad_pairing + fading * mul(alone, both, 1, 1)
        inside.append(jnp.where(first, ys[0], ys[1]))
        grad_x_step.append(jnp.where(first, xs[0], xs[1]))
    inside = jnp.concatenate(inside, axis=1)
    grad_x_step = jnp.concatenate(grad_x_step, axis=1)
    state = state_ref[0]
    state16 = state.astype(BF16)
    adjoint = carry[...]
    adjoint16 = adjoint.astype(BF16)
    outer = enter_wide * mul(c_rows, state16, 1, 0)
    full = inside + outer + skip * x
    grad_z = grad_gated * full * (sigmoid * (1.0 + z * (1.0 - sigmoid)))
    out_ref[:, cuts["z"] : cuts["z"] + z_wide] = grad_z.astype(BF16)
    entered = (enter_wide * grad_y).astype(BF16)
    pairing16 = grad_pairing.astype(BF16)
    grad_c = mul(entered, state16, 1, 1) + mul(pairing16, b_rows, 1, 0)
    grad_b = mul((x * tail_wide).astype(BF16), adjoint16, 1, 1) + mul(pairing16, c_rows, 0, 0)
    out_ref[:, cuts["b"] : cuts["b"] + STATE_SIZE] = grad_b.astype(BF16)
    out_ref[:, cuts["c"] : cuts["c"] + STATE_SIZE] = grad_c.astype(BF16)
    pushed = mul(b_rows, adjoint16, 1, 0)
    grad_x = step_wide * grad_x_step + tail_wide * pushed + skip * grad_y
    out_ref[:, cuts["x"] : cuts["x"] + z_wide] = grad_x.astype(BF16)

    def by_head(value):
        return near_exact(value, spread, ((1,), (1,)), 2, False)

    row_part = by_head(grad_y16.astype(F32) * inside + grad_y * outer)
    col_part = by_head(x_step.astype(F32) * grad_x_step)
    step_part = by_head(x * grad_x_step)
    tail_part = by_head(x * pushed)
    sums = jnp.concatenate(
        [
            jnp.sum(state * adjoint, axis=0, keepdims=True),
            jnp.sum(grad_y * x, axis=0, keepdims=True),
            jnp.zeros((6, z_wide), F32),
        ],
        axis=0,
    )
    sums = by_head(sums)
    step, leave, last = terms["step"], terms["leave"], terms["last"]
    moved = leave * step * tail_part
    grad_level = row_part - col_part - moved
    at_last = jnp.sum(moved, axis=0, keepdims=True) + jnp.exp(last) * sums[0:1, :]
    row = lax.broadcasted_iota(jnp.int32, (size, LANES), 0)
    grad_level = grad_level + jnp.where(row == size - 1, at_last, 0.0)
    grad_log = near_exact(tri, grad_level, ((0,), (0,)), 3, True)
    grad_step = step_part + leave * tail_part + grad_log * terms["rate"]
    grad_dt = grad_step * jax.nn.sigmoid(terms["dt_in"])
    lane = lax.broadcasted_iota(jnp.int32, (size, LANES), 1)
    grad_dt = jnp.where(lane < heads, grad_dt, 0.0)
    out_ref[:, cuts["dt"] : cuts["dt"] + LANES] = grad_dt.astype(BF16)
    head_ref[...] += jnp.concatenate(
        [
            jnp.sum(grad_dt, axis=0, keepdims=True),
            jnp.sum(grad_log * step, axis=0, keepdims=True) * terms["rate"],
            sums[1:2, :],
            jnp.zeros((5, LANES), F32),
        ],
        axis=0,
    )
    carry[...] = enter_wide[size - 1 : size, :] * adjoint + mul(c_rows, entered, 0, 0)


def mixer_tables(tokens, size, heads, bias, log_rate, skip):
    half = HEAD_SIZE // 2
    positions = jnp.arange(tokens, dtype=F32)
    frequency = THETA ** (-jnp.arange(half, dtype=F32) / half)
    angles = positions[:, None] * frequency[None, :]
    cosine, sine = jnp.cos(angles), jnp.sin(angles)
    order = jnp.arange(size)
    tri = (order[:, None] >= order[None, :]).astype(BF16)
    z_wide = heads * MIXER_HEAD_SIZE
    owner = jnp.arange(z_wide) // MIXER_HEAD_SIZE
    spread = (jnp.arange(LANES)[:, None] == owner[None, :]).astype(BF16)
    params = jnp.zeros((8, LANES), F32)
    params = params.at[0, :heads].set(bias).at[1, :heads].set(-jnp.exp(log_rate))
    return (
        jnp.concatenate([cosine, cosine], axis=1),
        jnp.concatenate([-sine, sine], axis=1),
        tri,
        params,
        spread,
        jnp.repeat(skip, MIXER_HEAD_SIZE)[None, :],
    )


def whole(shape):
    return pl.BlockSpec(shape, lambda i, place: (0,) * len(shape))


def mixer_forward(place, mixed, tables, cuts, q_heads, heads, blocks):
    tokens, wide = mixed.shape
    size = tokens // blocks
    cosine, sine, tri, params, spread, skip = tables
    z_wide = heads * MIXER_HEAD_SIZE
    out_wide = q_heads * HEAD_SIZE + z_wide

    def by_hop(width):
        return pl.BlockSpec(
            (size, width), lambda i, place: (lax.rem(place[0] - i + blocks, blocks), 0)
        )

    in_order = pl.BlockSpec((size, HEAD_SIZE), lambda i, place: (i, 0))
    return pl.pallas_call(
        functools.partial(mixer_forward_kernel, cuts, q_heads, heads, blocks),
        grid_spec=pltpu.PrefetchScalarGridSpec(
            num_scalar_prefetch=1,
            grid=(blocks,),
            in_specs=[
                by_hop(wide),
                in_order,
                in_order,
                whole(tri.shape),
                whole(params.shape),
                whole(spread.shape),
                whole(skip.shape),
            ],
            out_specs=[
                by_hop(out_wide),
                pl.BlockSpec((1, STATE_SIZE, z_wide), lambda i, place: (i, 0, 0)),
                whole((tokens, HEAD_SIZE)),
                whole((tokens, HEAD_SIZE)),
            ],
            scratch_shapes=[pltpu.VMEM((STATE_SIZE, z_wide), F32)],
        ),
        out_shape=[
            jax.ShapeDtypeStruct((tokens, out_wide), BF16),
            jax.ShapeDtypeStruct((blocks, STATE_SIZE, z_wide), F32),
            jax.ShapeDtypeStruct((tokens, HEAD_SIZE), BF16),
            jax.ShapeDtypeStruct((tokens, HEAD_SIZE), BF16),
        ],
        compiler_params=pltpu.CompilerParams(vmem_limit_bytes=VMEM_LIMIT),
        cost_estimate=pl.CostEstimate(
            flops=8_000_000_000, bytes_accessed=20_000_000, transcendentals=0
        ),
        name="mixer_forward",
    )(place, mixed, cosine, sine, tri, params, spread, skip)


def mixer_backward(place, mixed, joint, states, keys, values, tables, cuts, q_heads, heads, blocks):
    tokens, wide = mixed.shape
    size = tokens // blocks
    cosine, sine, tri, params, spread, skip = tables
    z_wide = heads * MIXER_HEAD_SIZE

    def by_hop(width):
        return pl.BlockSpec(
            (size, width), lambda i, place: (lax.rem(place[0] + i + 1, blocks), 0)
        )

    in_order = pl.BlockSpec((size, HEAD_SIZE), lambda i, place: (blocks - 1 - i, 0))
    return pl.pallas_call(
        functools.partial(mixer_backward_kernel, cuts, q_heads, heads, blocks),
        grid_spec=pltpu.PrefetchScalarGridSpec(
            num_scalar_prefetch=1,
            grid=(blocks,),
            in_specs=[
                by_hop(wide),
                by_hop(joint.shape[1]),
                pl.BlockSpec((1, STATE_SIZE, z_wide), lambda i, place: (blocks - 1 - i, 0, 0)),
                whole(keys.shape),
                whole(values.shape),
                in_order,
                in_order,
                whole(tri.shape),
                whole(params.shape),
                whole(spread.shape),
                whole(skip.shape),
            ],
            out_specs=[by_hop(wide), whole((8, LANES))],
            scratch_shapes=[
                pltpu.VMEM((tokens, HEAD_SIZE), F32),
                pltpu.VMEM((tokens, HEAD_SIZE), F32),
                pltpu.VMEM((STATE_SIZE, z_wide), F32),
            ],
        ),
        out_shape=[
            jax.ShapeDtypeStruct((tokens, wide), BF16),
            jax.ShapeDtypeStruct((8, LANES), F32),
        ],
        compiler_params=pltpu.CompilerParams(vmem_limit_bytes=VMEM_LIMIT),
        cost_estimate=pl.CostEstimate(
            flops=20_000_000_000, bytes_accessed=30_000_000, transcendentals=0
        ),
        name="mixer_backward",
    )(place, mixed, joint, states, keys, values, cosine, sine, tri, params, spread, skip)


def pack_kernel(cuts, starts_ref, *refs):
    sources = refs[: max(c[0] for out in cuts for c in out) + 1]
    outs = refs[len(sources) : len(sources) + len(cuts)]
    semaphores = refs[-1]
    copies, at = [], 0
    for out, ref in zip(cuts, outs):
        column = 0
        for source, wide in out:
            start = pl.multiple_of(starts_ref[at], LANES)
            copies.append(
                pltpu.make_async_copy(
                    sources[source].at[:, pl.ds(start, wide)],
                    ref.at[:, pl.ds(column, wide)],
                    semaphores.at[at],
                )
            )
            column += wide
            at += 1
    for copy in copies:
        copy.start()
    for copy in copies:
        copy.wait()


def pack_columns(sources, cuts):
    starts = jnp.stack([start for out in cuts for _, start, _ in out]).astype(jnp.int32)
    rows = sources[0].shape[0]
    anywhere = pl.BlockSpec(memory_space=pl.ANY)
    return pl.pallas_call(
        functools.partial(pack_kernel, [[(s, w) for s, _, w in out] for out in cuts]),
        grid_spec=pltpu.PrefetchScalarGridSpec(
            num_scalar_prefetch=1,
            grid=(1,),
            in_specs=[anywhere] * len(sources),
            out_specs=[
                pl.BlockSpec((rows, sum(w for _, _, w in out)), lambda i, starts: (0, 0))
                for out in cuts
            ],
            scratch_shapes=[pltpu.SemaphoreType.DMA((starts.shape[0],))],
        ),
        out_shape=[
            jax.ShapeDtypeStruct((rows, sum(w for _, _, w in out)), BF16) for out in cuts
        ],
        compiler_params=pltpu.CompilerParams(vmem_limit_bytes=VMEM_LIMIT),
        cost_estimate=pl.CostEstimate(
            flops=0, bytes_accessed=20_000_000, transcendentals=0
        ),
        name="pack_columns",
    )(starts, *sources)


def dense_cost(flops, *arrays):
    return pl.CostEstimate(
        flops=flops,
        bytes_accessed=sum(math.prod(a.shape) * a.dtype.itemsize for a in arrays),
        transcendentals=0,
    )


def fetch_hops(count, place, parts, target, semaphores):
    size = parts[0].shape[0]

    def copy(source, hop):
        return pltpu.make_async_copy(
            source, target.at[hop * size : (hop + 1) * size, :], semaphores.at[hop]
        )

    copy(parts[0], 0).start()
    for hop in range(1, count):

        @pl.when(place >= hop)
        def _(hop=hop):
            copy(parts[hop], hop).start()

        @pl.when(place < hop)
        def _(hop=hop):
            copy(parts[2 * count - 1 - hop], hop).start()

    for hop in range(count):
        copy(parts[0], hop).wait()


def mixer_in_kernel(count, place_ref, gain_ref, w_ref, *refs):
    parts = refs[: 2 * count - 1]
    out_ref, normed_ref, raw, semaphores = refs[2 * count - 1 :]
    size = parts[0].shape[0]

    @pl.when(pl.program_id(0) == 0)
    def _():
        fetch_hops(count, place_ref[0], parts, raw, semaphores)
        for hop in range(count):
            at = slice(hop * size, (hop + 1) * size)
            rows = raw[at, :].astype(F32)
            scaled = rows * lax.rsqrt(jnp.mean(rows * rows, axis=-1, keepdims=True) + EPSILON)
            normed_ref[at, :] = (scaled * gain_ref[...]).astype(BF16)

    out_ref[...] = mul(normed_ref[...], w_ref[...], 1, 0)


def mixer_in(place, own, ups, downs, gain, weight, wide):
    size, depth = own.shape
    count = len(ups) + 1
    tokens = size * count
    tile = max(t for t in range(LANES, 1025, LANES) if wide % t == 0)

    def fixed(shape):
        return pl.BlockSpec(shape, lambda j, place: (0, 0))

    outs = [
        jax.ShapeDtypeStruct((tokens, wide), F32),
        jax.ShapeDtypeStruct((tokens, depth), BF16),
    ]
    return pl.pallas_call(
        functools.partial(mixer_in_kernel, count),
        grid_spec=pltpu.PrefetchScalarGridSpec(
            num_scalar_prefetch=1,
            grid=(wide // tile,),
            in_specs=[
                fixed((1, depth)),
                pl.BlockSpec((depth, tile), lambda j, place: (0, j)),
            ]
            + [pl.BlockSpec(memory_space=pl.ANY)] * (2 * count - 1),
            out_specs=[
                pl.BlockSpec((tokens, tile), lambda j, place: (0, j)),
                fixed((tokens, depth)),
            ],
            scratch_shapes=[
                pltpu.VMEM((tokens, depth), BF16),
                pltpu.SemaphoreType.DMA((count,)),
            ],
        ),
        out_shape=outs,
        compiler_params=pltpu.CompilerParams(vmem_limit_bytes=VMEM_LIMIT),
        cost_estimate=dense_cost(2 * tokens * depth * wide, weight, *outs),
        name="mixer_in",
    )(place, gain, weight, own, *ups, *downs)


def ffn_kernel(
    own_ref,
    other_ref,
    act_grad_ref,
    gate_ref,
    up_ref,
    activated_ref,
    grad_gate_ref,
    grad_up_ref,
    rows_ref,
):
    @pl.when(pl.program_id(0) == 0)
    def _():
        rows_ref[: own_ref.shape[0], :] = own_ref[...]
        rows_ref[own_ref.shape[0] :, :] = other_ref[...]

    rows = rows_ref[...]
    gate = mul(rows, gate_ref[...], 1, 0)
    up = mul(rows, up_ref[...], 1, 0)
    grad = act_grad_ref[...]
    sigmoid = jax.nn.sigmoid(gate)
    silu = gate * sigmoid
    activated_ref[...] = (silu * up).astype(BF16)
    grad_gate_ref[...] = (grad * up * (sigmoid * (1.0 + gate * (1.0 - sigmoid)))).astype(BF16)
    grad_up_ref[...] = (grad * silu).astype(BF16)


def ffn_inner(own, other, act_grad, weights):
    tokens, depth = 2 * own.shape[0], own.shape[1]
    units = act_grad.shape[1]
    tile = 256
    tiles = units // tile
    out = jax.ShapeDtypeStruct((tokens, units), BF16)
    by_unit = pl.BlockSpec((tokens, tile), lambda j: (0, j))
    return pl.pallas_call(
        ffn_kernel,
        grid=(tiles,),
        in_specs=[
            pl.BlockSpec(own.shape, lambda j: (0, 0)),
            pl.BlockSpec(own.shape, lambda j: (0, 0)),
            by_unit,
            pl.BlockSpec((depth, tile), lambda j: (0, tiles + j)),
            pl.BlockSpec((depth, tile), lambda j: (0, 2 * tiles + j)),
        ],
        out_specs=[by_unit] * 3 + [pl.BlockSpec((tokens, depth), lambda j: (0, 0))],
        out_shape=[out] * 3 + [jax.ShapeDtypeStruct((tokens, depth), BF16)],
        compiler_params=pltpu.CompilerParams(vmem_limit_bytes=VMEM_LIMIT),
        cost_estimate=dense_cost(4 * tokens * depth * units, weights, out, out, out),
        name="ffn_inner",
    )(own, other, act_grad, weights, weights)


def ffn_back_kernel(count, *refs):
    own_ref, other_ref = refs[-2:]
    total = mul(refs[0][...], refs[count][...], 1, 1)
    for i in range(1, count):
        total = total + mul(refs[i][...], refs[count + i][...], 1, 1)
    half = total.shape[0] // 2
    own_ref[...] = total[:half]
    other_ref[...] = total[half:].astype(BF16)


def ffn_back(grads, weights, columns):
    tokens, units = grads[0].shape
    depth = weights.shape[0]
    tile = 256
    half = pl.BlockSpec((tokens // 2, tile), lambda j: (0, j))
    return pl.pallas_call(
        functools.partial(ffn_back_kernel, len(grads)),
        grid=(depth // tile,),
        in_specs=[pl.BlockSpec((tokens, units), lambda j: (0, 0)) for _ in grads]
        + [pl.BlockSpec((tile, units), lambda j, c=c: (j, c)) for c in columns],
        out_specs=[half, half],
        out_shape=[
            jax.ShapeDtypeStruct((tokens // 2, depth), F32),
            jax.ShapeDtypeStruct((tokens // 2, depth), BF16),
        ],
        compiler_params=pltpu.CompilerParams(vmem_limit_bytes=VMEM_LIMIT),
        cost_estimate=dense_cost(2 * len(grads) * tokens * depth * units, weights),
        name="ffn_back",
    )(*grads, *[weights for _ in columns])


def joint_kernel(count, place_ref, w_ref, *refs):
    parts = refs[: 2 * count - 1]
    out_ref, rows_ref, semaphores = refs[2 * count - 1 :]

    @pl.when(pl.program_id(0) == 0)
    def _():
        fetch_hops(count, place_ref[0], parts, rows_ref, semaphores)

    out_ref[...] = mul(rows_ref[...], w_ref[...], 1, 0)


def joint(place, own, ups, downs, weight):
    size, depth = own.shape
    count = len(ups) + 1
    tokens, wide = size * count, weight.shape[1]
    tile = min(wide, 512)
    outs = [
        jax.ShapeDtypeStruct((tokens, wide), F32),
        jax.ShapeDtypeStruct((tokens, depth), BF16),
    ]
    return pl.pallas_call(
        functools.partial(joint_kernel, count),
        grid_spec=pltpu.PrefetchScalarGridSpec(
            num_scalar_prefetch=1,
            grid=(wide // tile,),
            in_specs=[pl.BlockSpec((depth, tile), lambda j, place: (0, j))]
            + [pl.BlockSpec(memory_space=pl.ANY)] * (2 * count - 1),
            out_specs=[
                pl.BlockSpec((tokens, tile), lambda j, place: (0, j)),
                pl.BlockSpec((tokens, depth), lambda j, place: (0, 0)),
            ],
            scratch_shapes=[pltpu.SemaphoreType.DMA((count,))],
        ),
        out_shape=outs,
        compiler_params=pltpu.CompilerParams(vmem_limit_bytes=VMEM_LIMIT),
        cost_estimate=dense_cost(2 * tokens * depth * wide, weight, *outs),
        name="joint",
    )(place, weight, own, *ups, *downs)


def mixer_out_kernel(grad_ref, w_ref, normed_ref, gain_ref, sum_ref, own_ref, *other_refs):
    total = mul(grad_ref[...], w_ref[:, : grad_ref.shape[1]], 1, 1)
    size = own_ref.shape[0]
    own_ref[...] = total[:size]
    for hop, ref in enumerate(other_refs, 1):
        ref[...] = total[hop * size : (hop + 1) * size].astype(BF16)
    sums = jnp.sum(total * normed_ref[...].astype(F32), axis=0, keepdims=True) / gain_ref[...]
    sum_ref[...] = jnp.broadcast_to(sums, sum_ref.shape)


def mixer_out(grad, weights, normed, gain, size):
    tokens, wide = grad.shape
    depth = weights.shape[0]
    tile = 256
    outs = [jax.ShapeDtypeStruct((8, depth), F32), jax.ShapeDtypeStruct((size, depth), F32)]
    outs += [jax.ShapeDtypeStruct((size, depth), BF16)] * (tokens // size - 1)
    return pl.pallas_call(
        mixer_out_kernel,
        grid=(depth // tile,),
        in_specs=[
            pl.BlockSpec((tokens, wide), lambda j: (0, 0)),
            pl.BlockSpec((tile, weights.shape[1]), lambda j: (j, 0)),
            pl.BlockSpec((tokens, tile), lambda j: (0, j)),
            pl.BlockSpec((1, tile), lambda j: (0, j)),
        ],
        out_specs=[pl.BlockSpec((o.shape[0], tile), lambda j: (0, j)) for o in outs],
        out_shape=outs,
        compiler_params=pltpu.CompilerParams(vmem_limit_bytes=VMEM_LIMIT),
        cost_estimate=dense_cost(2 * tokens * depth * wide, grad, weights, normed, *outs),
        name="mixer_out",
    )(grad, weights, normed, gain)


def outer_kernel(pairs, rider_at, *refs):
    out_ref = refs[-1]
    at = 0
    for left, right, start, wide in pairs:
        value = mul(refs[left][...], refs[right][:, start : start + wide], 0, 0)
        out_ref[:, at : at + wide] = value.astype(BF16)
        at += wide
    if rider_at is not None:
        riders = refs[-2][...]
        rows = riders.shape[0]
        for k in range(out_ref.shape[0] // rows):
            block = out_ref[k * rows : (k + 1) * rows, rider_at : rider_at + LANES]
            out_ref[k * rows : (k + 1) * rows, rider_at : rider_at + LANES] = block + riders


def weight_grads(pairs, riders=None, rider_at=None):
    operands = []

    def position(array):
        for i, held in enumerate(operands):
            if held is array:
                return i
        operands.append(array)
        return len(operands) - 1

    lefts = [position(left) for left, _, _, _ in pairs]
    n_left = len(operands)
    rights = [position(right) for _, right, _, _ in pairs]
    plan = [(l, r, p[2], p[3]) for l, r, p in zip(lefts, rights, pairs)]
    tokens, depth = operands[0].shape
    wide = sum(p[3] for p in pairs)
    tile = 256
    operands += [] if riders is None else [riders]
    specs = [pl.BlockSpec((a.shape[0], tile), lambda j: (0, j)) for a in operands[:n_left]] + [
        pl.BlockSpec(a.shape, lambda j: (0, 0)) for a in operands[n_left:]
    ]
    out = jax.ShapeDtypeStruct((depth, wide), BF16)
    return pl.pallas_call(
        functools.partial(outer_kernel, plan, rider_at),
        grid=(depth // tile,),
        in_specs=specs,
        out_specs=pl.BlockSpec((tile, wide), lambda j: (j, 0)),
        out_shape=out,
        compiler_params=pltpu.CompilerParams(vmem_limit_bytes=VMEM_LIMIT),
        cost_estimate=dense_cost(2 * tokens * depth * wide, out, *operands),
        name="weight_grads",
    )(*operands)


def unpack_kernel(places, q_heads, heads, gain_columns, count, place_ref, *refs):
    arrays = 2 * count - 1
    groups = [refs[i : i + arrays] for i in range(0, len(refs) - 4, arrays)]
    mix_ref, attn_ref, ssm_ref, extra_ref = refs[-4:]
    place = place_ref[0]
    q_wide, z_wide = q_heads * HEAD_SIZE, heads * MIXER_HEAD_SIZE
    group = QUERY_HEADS // KEY_VALUE_HEADS
    key_at = QUERY_HEADS * HEAD_SIZE
    kv_wide = KEY_VALUE_HEADS * HEAD_SIZE
    z_at = key_at + 2 * kv_wide
    x_at = z_at + MIXER_HEADS * MIXER_HEAD_SIZE
    b_at = x_at + MIXER_HEADS * MIXER_HEAD_SIZE
    step = mix_ref.shape[0]
    lane = lax.broadcasted_iota(jnp.int32, (step, LANES), 1)
    head_lane = heads + gain_columns
    head_at = MIXER_HEADS + gain_columns
    shared = jnp.zeros((step, 2 * STATE_SIZE), F32)
    extra = jnp.zeros((step, LANES), F32)
    mix_ref[:, key_at : key_at + 2 * kv_wide] = jnp.zeros((step, 2 * kv_wide), F32)

    for hop in range(count):
        source = lax.rem(place - hop + count, count)

        def of(name, hop=hop):
            group, start, wide = places[name]
            parts = groups[group]
            if hop == 0:
                return parts[0][:, start : start + wide].astype(F32)
            up = parts[hop][:, start : start + wide].astype(F32)
            down = parts[2 * count - 1 - hop][:, start : start + wide].astype(F32)
            return jnp.where(place >= hop, up, down)

        def put(ref, start, value):
            ref[:, pl.ds(pl.multiple_of(start, LANES), value.shape[1])] = value

        put(mix_ref, source * q_wide, of("q"))
        put(mix_ref, z_at + source * z_wide, of("z"))
        put(mix_ref, x_at + source * z_wide, of("x"))
        put(attn_ref, source * q_wide, of("attn"))
        put(ssm_ref, source * z_wide, of("ssm"))
        shared = shared + of("bc")
        which = lax.div(source * q_heads, group)
        for name, base in (("k", key_at), ("v", key_at + kv_wide)):
            at = pl.ds(pl.multiple_of(base + which * HEAD_SIZE, LANES), HEAD_SIZE)
            mix_ref[:, at] += of(name)
        small = of("dt")
        own = jnp.where(lane < heads, small, 0.0)
        gains = jnp.where((lane >= heads) & (lane < head_lane), small, 0.0)
        column = jnp.where(lane == head_lane, small, 0.0)
        extra = (
            extra
            + pltpu.roll(own, source * heads, 1)
            + pltpu.roll(gains, MIXER_HEADS - heads, 1)
            + pltpu.roll(column, head_at - head_lane + source, 1)
        )
    mix_ref[:, b_at:] = shared
    extra_ref[...] = extra


def unpack_mixer(place, groups, places, q_heads, heads, gain_columns):
    count = len(groups[0][1]) + 1
    rows = groups[0][0].shape[0]
    step = min(rows, 128)
    widths = (
        QUERY_HEADS * HEAD_SIZE
        + 2 * KEY_VALUE_HEADS * HEAD_SIZE
        + 2 * MIXER_HEADS * MIXER_HEAD_SIZE
        + 2 * STATE_SIZE,
        QUERY_HEADS * HEAD_SIZE,
        MIXER_HEADS * MIXER_HEAD_SIZE,
        LANES,
    )
    operands = [part for own, ups, downs in groups for part in (own, *ups, *downs)]

    def spec(columns):
        return pl.BlockSpec((step, columns), lambda i, place: (i, 0))

    return pl.pallas_call(
        functools.partial(unpack_kernel, places, q_heads, heads, gain_columns, count),
        grid_spec=pltpu.PrefetchScalarGridSpec(
            num_scalar_prefetch=1,
            grid=(rows // step,),
            in_specs=[spec(o.shape[1]) for o in operands],
            out_specs=[spec(w) for w in widths],
        ),
        out_shape=[jax.ShapeDtypeStruct((rows, w), F32) for w in widths],
        compiler_params=pltpu.CompilerParams(vmem_limit_bytes=VMEM_LIMIT),
        cost_estimate=pl.CostEstimate(
            flops=100_000_000, bytes_accessed=26_000_000, transcendentals=0
        ),
        name="unpack_mixer",
    )(place, *operands)


def unpack_ffn_kernel(count, place_ref, *refs):
    arrays = 2 * count - 1
    groups = (refs[:arrays], refs[arrays : 2 * arrays])
    outs = refs[2 * arrays :]
    place = place_ref[0]
    chunk = groups[0][0].shape[0]
    half = outs[0].shape[1] // 2
    quarter = half // 2
    pieces = (
        (0, 0, 0, half, 0),
        (1, 0, half, quarter, 0),
        (1, 1, 0, quarter, quarter),
        (2, 1, quarter, half, 0),
    )
    for hop in range(count):
        source = lax.rem(place - hop + count, count)
        row = pl.multiple_of(lax.div(source, 2) * chunk, chunk)
        side = lax.rem(source, 2) * half
        for out, group, start, wide, offset in pieces:
            parts = groups[group]
            value = parts[0][:, start : start + wide] if hop == 0 else None
            if hop:
                up = parts[hop][:, start : start + wide]
                down = parts[arrays - hop][:, start : start + wide]
                value = jnp.where(place >= hop, up.astype(F32), down.astype(F32))
            column = pl.multiple_of(side + offset, LANES)
            outs[out][pl.ds(row, chunk), pl.ds(column, wide)] = value.astype(F32)


def unpack_ffn(place, groups, units):
    count = len(groups[0][1]) + 1
    rows = groups[0][0].shape[0] * (count // 2)
    operands = [part for own, ups, downs in groups for part in (own, *ups, *downs)]

    def fixed(shape):
        return pl.BlockSpec(shape, lambda i, place: (0, 0))

    return pl.pallas_call(
        functools.partial(unpack_ffn_kernel, count),
        grid_spec=pltpu.PrefetchScalarGridSpec(
            num_scalar_prefetch=1,
            grid=(1,),
            in_specs=[fixed(o.shape) for o in operands],
            out_specs=[fixed((rows, units))] * 3,
        ),
        out_shape=[jax.ShapeDtypeStruct((rows, units), F32)] * 3,
        compiler_params=pltpu.CompilerParams(vmem_limit_bytes=VMEM_LIMIT),
        cost_estimate=pl.CostEstimate(
            flops=100_000_000, bytes_accessed=22_000_000, transcendentals=0
        ),
        name="unpack_ffn",
    )(place, *operands)


def per_device(
    hidden_in,
    w_mix,
    w_dt,
    w_attn_out,
    w_ssm_out,
    w_gate,
    w_up,
    w_down,
    norm_gains,
    dt_bias,
    a_log,
    skip_scale,
    cotangent,
):
    w_mix, w_dt, w_attn_out, w_ssm_out = w_mix[0], w_dt[0], w_attn_out[0], w_ssm_out[0]
    w_gate, w_up, w_down = w_gate[0], w_up[0], w_down[0]
    gain_mix, gain_ffn = norm_gains[0, 0], norm_gains[0, 1]
    count, place = lax.axis_size("ctx"), lax.axis_index("ctx")
    piece, width = hidden_in.shape[1], hidden_in.shape[2]
    tokens = piece * count
    rows = w_mix.shape[0]
    hidden_units = w_gate.shape[1]
    q_heads = QUERY_HEADS // count
    group = QUERY_HEADS // KEY_VALUE_HEADS
    kv_head = (place * q_heads) // group
    heads = MIXER_HEADS // count
    q_wide, z_wide = q_heads * HEAD_SIZE, heads * MIXER_HEAD_SIZE
    key_at = QUERY_HEADS * HEAD_SIZE
    value_at = key_at + KEY_VALUE_HEADS * HEAD_SIZE
    z_at = value_at + KEY_VALUE_HEADS * HEAD_SIZE
    x_at = z_at + MIXER_HEADS * MIXER_HEAD_SIZE
    b_at = x_at + MIXER_HEADS * MIXER_HEAD_SIZE
    names = ("q", "k", "v", "z", "x", "b", "c", "dt")
    sizes = (q_wide, HEAD_SIZE, HEAD_SIZE, z_wide, z_wide, STATE_SIZE, STATE_SIZE, LANES)
    cuts, mix_wide = {}, 0
    for name, size in zip(names, sizes):
        cuts[name] = mix_wide
        mix_wide += size

    half = place % 2
    half_units = hidden_units // 2
    own_dt = lax.dynamic_slice(w_dt, (0, place * heads), (rows, heads))
    own_dt = jnp.pad(own_dt, ((0, 0), (0, LANES - heads)))
    here = jnp.reshape(place, (1,)).astype(jnp.int32)
    mix_starts = (
        (place * q_wide, q_wide),
        (key_at + kv_head * HEAD_SIZE, HEAD_SIZE),
        (value_at + kv_head * HEAD_SIZE, HEAD_SIZE),
        (z_at + place * z_wide, z_wide),
        (x_at + place * z_wide, z_wide),
        (b_at + 0 * place, 2 * STATE_SIZE),
    )
    from_half = (half * half_units, half_units)
    (mixer_own,) = pack_columns(
        (w_mix, own_dt, w_attn_out, w_ssm_out),
        (
            [(0,) + cut for cut in mix_starts]
            + [(1, 0 * place, LANES), (2, place * q_wide, q_wide), (3, place * z_wide, z_wide)],
        ),
    )
    (ffn_own,) = pack_columns(
        (w_gate, w_up, w_down), ([(2,) + from_half, (0,) + from_half, (1,) + from_half],)
    )
    w_mixer, w_ffn = gather_rows(mixer_own), gather_rows(ffn_own)
    w_out = w_mixer[:, mix_wide:]
    w_down_half = w_ffn[:, :half_units]

    blocks = tokens // piece

    hidden_own = hidden_in.reshape(piece, width)
    hidden_ups, hidden_downs = finish(line_gather(hidden_own))
    mixed, normed = mixer_in(
        here, hidden_own, hidden_ups, hidden_downs, gain_mix[None, :], w_mixer, mix_wide
    )
    own = [lax.dynamic_slice_in_dim(p[0], place * heads, heads) for p in (dt_bias, a_log, skip_scale)]
    tables = mixer_tables(tokens, piece, heads, *own)
    branch_in, states, keys, values = mixer_forward(
        here, mixed, tables, cuts, q_heads, heads, blocks
    )
    cot_own = cotangent.reshape(piece, width)
    cot_swap = swap_pair(after(cot_own, hidden_ups[-1], hidden_downs[-1]))
    branch_in, cot_swap = lax.optimization_barrier((branch_in, cot_swap))
    cot_pair = jnp.concatenate([cot_own, cot_swap], axis=0)
    halves, ready = [], branch_in
    for half_rows in (w_out[: width // 2], w_out[width // 2 :]):
        terms = [None] * count

        def branch_term(rows_in, hop, half_rows=half_rows):
            return dot(rows_in[hop * piece : (hop + 1) * piece], half_rows, 1, 1)

        for hop in (1, count - 1):
            terms[hop] = branch_term(ready, hop)
        branch_line = Chain(line_sum(terms))
        flight = Flight(branch_line)
        late_in = ready = after(branch_in, *flight.values)
        for hop in range(count):
            if terms[hop] is None:
                terms[hop] = branch_term(late_in, hop)
        halves.append((branch_line, flight))
    for branch_line, flight in halves:
        flight.land()
    for branch_line, _ in halves:
        while live(branch_line):
            advance(branch_line)
    branch = jnp.concatenate([branch_line.result for branch_line, _ in halves], axis=1)
    middle = hidden_own.astype(F32) + branch
    grad_act = dot(cot_pair, w_down_half, 1, 0)

    inverse_ffn = inverse_rms(middle)
    normed_ffn = (middle * inverse_ffn * gain_ffn).astype(BF16)
    normed_swap, grad_act = lax.optimization_barrier((swap_pair(normed_ffn), grad_act))
    activated, grad_gate, grad_up, normed_pair = ffn_inner(
        normed_ffn, normed_swap, grad_act, w_ffn
    )
    grad_normed_own, grad_normed_other = ffn_back((grad_gate, grad_up), w_ffn, (1, 2))
    grad_swap = swap_pair(grad_normed_other)
    activated, grad_gate, grad_up = lax.optimization_barrier(
        (activated, grad_gate, grad_up, grad_normed_other)
    )[:3]
    quarter = half_units // 2
    grad_w_first = weight_grads(
        ((normed_pair, grad_gate, 0, half_units), (normed_pair, grad_up, 0, quarter))
    )
    grad_swap, grad_w_first = lax.optimization_barrier((grad_swap, grad_w_first))
    grad_w_first = scatter_rows(grad_w_first)
    grad_normed_ffn = grad_normed_own + grad_swap.astype(F32)

    grad_middle = cot_own.astype(F32) + rms_pull(middle, inverse_ffn, gain_ffn, grad_normed_ffn)
    grad_gain_ffn = jnp.sum(grad_normed_ffn * middle * inverse_ffn, axis=0)
    branch_own = grad_middle.astype(BF16)
    branch_line = Chain(line_gather(branch_own))
    late_activated, late_up = lax.optimization_barrier((activated, grad_up, branch_own))[:2]
    grad_w_second = weight_grads(
        ((normed_pair, late_up, quarter, quarter), (cot_pair, late_activated, 0, half_units))
    )
    (grad_w_second,) = advance(branch_line, beside=(grad_w_second,))
    out_half, out_other = ffn_back((after(activated, grad_w_second),), w_ffn, (0,))
    grad_w_second = scatter_rows(grad_w_second)
    out_half, out_other = advance(branch_line, beside=(out_half, out_other))
    while branch_line.sends is not None:
        advance(branch_line)
    grad_joint, grad_branch = joint(here, branch_own, *branch_line.result, w_out)
    out_swap = swap_pair(after(out_other, *branch_line.result[0]))
    first = Chain(parity_gather(grad_w_first))

    grad_mixed, head_part = mixer_backward(
        here, mixed, grad_joint, states, keys, values, tables, cuts, q_heads, heads, blocks
    )
    grad_mixed, head_part, out_swap = advance(first, beside=(grad_mixed, head_part, out_swap))
    gain_rows, *dn_parts = mixer_out(grad_mixed, w_mixer, normed, gain_mix[None, :], piece)
    gain_rows, *dn_parts = advance(first, beside=(gain_rows, *dn_parts))

    gain_columns = 2 * width // rows
    riders = jnp.concatenate(
        [
            jnp.zeros((rows, heads), F32),
            jnp.stack([gain_rows[0], grad_gain_ffn]).reshape(rows, gain_columns),
            jnp.pad(head_part[:3, :heads].reshape(3 * heads), (0, rows - 3 * heads))[:, None],
            jnp.zeros((rows, LANES - heads - gain_columns - 1), F32),
        ],
        axis=1,
    )
    grad_w_mixer = weight_grads(
        ((normed, grad_mixed, 0, mix_wide), (grad_branch, branch_in, 0, q_wide + z_wide)),
        riders.astype(BF16),
        cuts["dt"],
    )
    normed_sum = Chain(line_sum(dn_parts))
    (grad_w_mixer,) = advance(first, normed_sum, beside=(grad_w_mixer,))
    grad_w_mixer = scatter_rows(after(grad_w_mixer, grad_w_second))
    second = Chain(parity_gather(grad_w_second))
    advance(*live(second, first))
    while live(normed_sum):
        advance(*live(second, first, normed_sum))
    mixer = Chain(line_gather(after(grad_w_mixer, normed_sum.result)))
    while live(second, first):
        advance(*live(mixer, second, first))

    sealed = lax.optimization_barrier(
        (first.result, second.result, tuple(value for value, _ in mixer.sends))
    )
    outs = tuple(unpack_ffn(here, sealed[:2], hidden_units))
    outs = advance(*live(mixer), beside=outs)
    sealed = lax.optimization_barrier(
        (normed_sum.result, out_swap, tuple(value for value, _ in mixer.sends))
    )
    hidden_out = (middle + (out_half + sealed[1].astype(F32))).astype(BF16)
    hidden_f32 = hidden_own.astype(F32)
    grad_hidden = grad_middle + rms_pull(
        hidden_f32, inverse_rms(hidden_f32), gain_mix, sealed[0]
    )
    hidden_out, grad_hidden = advance(mixer, beside=(hidden_out, grad_hidden))
    while live(mixer):
        advance(mixer)
    out_gate, out_up, out_down = outs

    places = {name: (0, cuts[name], size) for name, size in zip(names, sizes)}
    places["bc"] = (0, cuts["b"], 2 * STATE_SIZE)
    places["attn"] = (0, mix_wide, q_wide)
    places["ssm"] = (0, mix_wide + q_wide, z_wide)
    out_mix, out_attn, out_ssm, extra = unpack_mixer(
        here, ((grad_w_mixer,) + mixer.result,), places, q_heads, heads, gain_columns
    )
    head_at = MIXER_HEADS + gain_columns
    gain_sums = extra[:, MIXER_HEADS:head_at].reshape(norm_gains.shape)
    head_sums = extra[: 3 * heads, head_at : head_at + count].reshape(3, heads, count)
    head_sums = jnp.swapaxes(head_sums, 1, 2).reshape(3, MIXER_HEADS)

    return (
        hidden_out.reshape(hidden_in.shape),
        grad_hidden.reshape(hidden_in.shape),
        out_mix[None],
        extra[None, :, :MIXER_HEADS],
        out_attn[None],
        out_ssm[None],
        out_gate[None],
        out_up[None],
        out_down[None],
        gain_sums,
        head_sums[0][None],
        head_sums[1][None],
        head_sums[2][None],
    )


def solution(mesh):
    split, rows = P("fsdp", "ctx", None), P(None, "fsdp", None)
    return jax.shard_map(
        per_device,
        mesh=mesh,
        in_specs=(split,) + (rows,) * 7 + (P(),) * 4 + (split,),
        out_specs=(split, split) + (rows,) * 7 + (P(),) * 4,
        check_vma=False,
    )
```

```python
import functools
import math

import jax
import jax.numpy as jnp
from jax import lax
from jax.experimental import pallas as pl
from jax.experimental.pallas import tpu as pltpu
from jax.sharding import PartitionSpec as P

QUERY_HEADS = 8
KEY_VALUE_HEADS = 2
HEAD_SIZE = 128
MIXER_HEADS = 48
MIXER_HEAD_SIZE = 64
STATE_SIZE = 256
LANES = 128

EPSILON = 1e-05
THETA = 10000.0
SCALE = 1.0 / math.sqrt(HEAD_SIZE)
VMEM_LIMIT = 56 * 1024 * 1024
BF16 = jnp.bfloat16
F32 = jnp.float32


def swap_pair(value):
    count = lax.axis_size("ctx")
    return lax.ppermute(value, "ctx", [(i, i ^ 1) for i in range(count)])


def after(value, *earlier):
    return lax.optimization_barrier((value,) + earlier)[0]


class Chain:
    def __init__(self, steps):
        self.steps, self.sends, self.result = steps, next(steps), None

    def take(self, got):
        try:
            self.sends = self.steps.send(got)
        except StopIteration as stop:
            self.sends, self.result = None, stop.value


class Flight:
    def __init__(self, *chains):
        self.chains = chains
        sends = [send for chain in chains for send in chain.sends]
        self.values = lax.optimization_barrier(tuple(value for value, _ in sends))
        self.got = tuple(
            lax.ppermute(v, "ctx", pairs) for v, (_, pairs) in zip(self.values, sends)
        )

    def land(self, beside=()):
        sealed = lax.optimization_barrier(self.got + tuple(beside))
        got = sealed[: len(self.got)]
        for chain in self.chains:
            count = len(chain.sends)
            chain.take(got[:count])
            got = got[count:]
        return sealed[len(self.got) :]


def advance(*chains, beside=()):
    return Flight(*chains).land(beside)


def live(*chains):
    return [chain for chain in chains if chain.sends is not None]


def finish(steps):
    chain = Chain(steps)
    while chain.sends is not None:
        advance(chain)
    return chain.result


def line_gather(value):
    count = lax.axis_size("ctx")
    up = down = value
    ups, downs = [], []
    for hop in range(1, count):
        up, down = yield [
            (up, [(i, i + 1) for i in range(hop - 1, count - 1)]),
            (down, [(i + 1, i) for i in range(count - hop)]),
        ]
        ups.append(up)
        downs.append(down)
    return ups, downs


def in_hops(value, ups, downs):
    count, place = lax.axis_size("ctx"), lax.axis_index("ctx")
    return [value] + [
        jnp.where(place >= hop, ups[hop - 1], downs[count - hop - 1]) for hop in range(1, count)
    ]


def gather_ctx(value):
    return in_hops(value, *finish(line_gather(value)))


def line_sum(parts):
    count = len(parts)
    up = down = 0.0
    for hop in range(1, count):
        up, down = yield [
            ((parts[hop] + up).astype(BF16), [(i, i + 1) for i in range(hop)]),
            (
                (parts[count - hop] + down).astype(BF16),
                [(i, i - 1) for i in range(count - hop, count)],
            ),
        ]
        up, down = up.astype(F32), down.astype(F32)
    return parts[0] + up + down


def parity_sum(grad):
    count = lax.axis_size("ctx")
    members, member = count // 2, lax.axis_index("ctx") // 2
    chunk = grad.shape[0] // members
    got = yield [
        (
            lax.dynamic_slice_in_dim(grad, ((member + hop) % members) * chunk, chunk, 0),
            [(i, (i + 2 * hop) % count) for i in range(count)],
        )
        for hop in range(1, members)
    ]
    total = lax.dynamic_slice_in_dim(grad, member * chunk, chunk, 0).astype(F32)
    for block in got:
        total = total + block.astype(F32)
    return total.astype(BF16)


def parity_gather(grad):
    total = yield from parity_sum(grad)
    ups, downs = yield from line_gather(total)
    return total, ups, downs


def gather_rows(value):
    return lax.all_gather(value, "fsdp", axis=0, tiled=True)


def scatter_rows(value):
    return lax.psum_scatter(value, "fsdp", scatter_dimension=0, tiled=True)


def dot(left, right, left_dim, right_dim):
    return lax.dot_general(
        left, right, (((left_dim,), (right_dim,)), ((), ())), preferred_element_type=F32
    )


def inverse_rms(rows):
    return lax.rsqrt(jnp.mean(rows * rows, axis=-1, keepdims=True) + EPSILON)


def rms_pull(rows, inverse, gain, grad):
    scaled = grad * gain
    return inverse * (scaled - rows * inverse * inverse * jnp.mean(rows * scaled, -1, keepdims=True))


def lanes_split(value, terms):
    parts = []
    for _ in range(terms):
        part = value.astype(BF16)
        parts.append(part)
        value = value - part.astype(F32)
    return parts


def near_exact(left, right, dims, terms, split_right):
    total = None
    for part in lanes_split(right if split_right else left, terms):
        pair = (left, part) if split_right else (part, right)
        one = lax.dot_general(*pair, (dims, ((), ())), preferred_element_type=F32)
        total = one if total is None else total + one
    return total


def mul(left, right, left_dim, right_dim):
    return lax.dot_general(
        left, right, (((left_dim,), (right_dim,)), ((), ())), preferred_element_type=F32
    )


def turn(vectors, cosine, sine):
    return vectors * cosine + pltpu.roll(vectors, HEAD_SIZE // 2, 1) * sine


def softplus(value):
    return jnp.maximum(value, 0.0) + jnp.log1p(jnp.exp(-jnp.abs(value)))


def block_terms(mixed, cuts, tri, params, spread):
    size = mixed.shape[0]
    dt_in = mixed[:, cuts["dt"] : cuts["dt"] + LANES] + params[0:1, :]
    step = softplus(dt_in)
    rate = params[1:2, :]
    level = near_exact(tri, step * rate, ((1,), (0,)), 3, True)
    last = level[size - 1 : size, :]
    enter = jnp.exp(level)
    leave = jnp.exp(last - level)
    wide = near_exact(
        jnp.concatenate([enter, step, leave * step], axis=0), spread, ((1,), (0,)), 2, False
    )
    return dict(
        dt_in=dt_in,
        step=step,
        rate=rate,
        level=level,
        last=last,
        leave=leave,
        enter_wide=wide[:size],
        step_wide=wide[size : 2 * size],
        tail_wide=wide[2 * size :],
    )


def fading_of(level, level_t, head, causal):
    gap = level[:, head : head + 1] - level_t[head : head + 1, :]
    return jnp.exp(jnp.where(causal, gap, -1e30))


def square_causal(size):
    row = lax.broadcasted_iota(jnp.int32, (size, size), 0)
    col = lax.broadcasted_iota(jnp.int32, (size, size), 1)
    return row >= col


def stacked_heads(value, at, count):
    return jnp.concatenate(
        [value[:, at + h * HEAD_SIZE : at + (h + 1) * HEAD_SIZE] for h in range(count)], axis=0
    )


def unstacked(value, count):
    size = value.shape[0] // count
    return jnp.concatenate([value[h * size : (h + 1) * size] for h in range(count)], axis=1)


def visible_keys(q_heads, size, block):
    shape = (q_heads * size, (block + 1) * size)
    row = lax.broadcasted_iota(jnp.int32, shape, 0)
    col = lax.broadcasted_iota(jnp.int32, shape, 1)
    return (row % size) + block * size >= col


def mixer_forward_kernel(
    cuts,
    q_heads,
    heads,
    blocks,
    place_ref,
    mixed_ref,
    cos_ref,
    sin_ref,
    tri_ref,
    params_ref,
    spread_ref,
    skip_ref,
    out_ref,
    state_ref,
    keys_ref,
    values_ref,
    carry,
):
    block = pl.program_id(0)
    size = mixed_ref.shape[0]
    q_wide, z_wide = q_heads * HEAD_SIZE, heads * MIXER_HEAD_SIZE

    @pl.when(block == 0)
    def _():
        carry[...] = jnp.zeros_like(carry)

    mixed = mixed_ref
    cosine, sine = cos_ref[...], sin_ref[...]
    here = pl.ds(pl.multiple_of(block * size, size), size)
    keys_ref[here, :] = turn(
        mixed[:, cuts["k"] : cuts["k"] + HEAD_SIZE], cosine, sine
    ).astype(BF16)
    values_ref[here, :] = mixed[:, cuts["v"] : cuts["v"] + HEAD_SIZE].astype(BF16)
    queries = jnp.concatenate(
        [
            turn(mixed[:, h * HEAD_SIZE : (h + 1) * HEAD_SIZE], cosine, sine)
            for h in range(q_heads)
        ],
        axis=0,
    ).astype(BF16)

    for at in range(blocks):

        @pl.when(block == at)
        def _(at=at):
            span = (at + 1) * size
            raw = mul(queries, keys_ref[:span, :], 1, 1) * SCALE
            logits = jnp.where(visible_keys(q_heads, size, at), raw, -1e30)
            weights = jnp.exp(logits - jnp.max(logits, axis=-1, keepdims=True))
            total = jnp.sum(weights, axis=-1, keepdims=True)
            attended = mul(weights.astype(BF16), values_ref[:span, :], 1, 0) / total
            out_ref[:, :q_wide] = unstacked(attended, q_heads).astype(BF16)

    terms = block_terms(mixed, cuts, tri_ref[...], params_ref, spread_ref[...])
    x = mixed[:, cuts["x"] : cuts["x"] + z_wide]
    b_rows = mixed[:, cuts["b"] : cuts["b"] + STATE_SIZE].astype(BF16)
    c_rows = mixed[:, cuts["c"] : cuts["c"] + STATE_SIZE].astype(BF16)
    causal = square_causal(size)
    pairing = mul(c_rows, b_rows, 1, 1)
    level = terms["level"]
    level_t = level.T
    x_step = (x * terms["step_wide"]).astype(BF16)
    first = lax.broadcasted_iota(jnp.int32, (size, LANES), 1) < MIXER_HEAD_SIZE
    inside = []
    for pair in range(heads // 2):
        both = x_step[:, pair * LANES : (pair + 1) * LANES]
        sides = []
        for head in (2 * pair, 2 * pair + 1):
            mixing = (fading_of(level, level_t, head, causal) * pairing).astype(BF16)
            sides.append(mul(mixing, both, 1, 0))
        inside.append(jnp.where(first, sides[0], sides[1]))
    state = carry[...]
    state_ref[0] = state
    full = (
        jnp.concatenate(inside, axis=1)
        + terms["enter_wide"] * mul(c_rows, state.astype(BF16), 1, 0)
        + skip_ref[...] * x
    )
    z = mixed[:, cuts["z"] : cuts["z"] + z_wide]
    out_ref[:, q_wide:] = (full * z * jax.nn.sigmoid(z)).astype(BF16)
    fresh = mul(b_rows, (x * terms["tail_wide"]).astype(BF16), 0, 0)
    carry[...] = terms["enter_wide"][size - 1 : size, :] * state + fresh


def mixer_backward_kernel(
    cuts,
    q_heads,
    heads,
    blocks,
    place_ref,
    mixed_ref,
    joint_ref,
    state_ref,
    keys_ref,
    values_ref,
    cos_ref,
    sin_ref,
    tri_ref,
    params_ref,
    spread_ref,
    skip_ref,
    out_ref,
    head_ref,
    grad_keys,
    grad_values,
    carry,
):
    block = blocks - 1 - pl.program_id(0)
    size = mixed_ref.shape[0]
    q_wide, z_wide = q_heads * HEAD_SIZE, heads * MIXER_HEAD_SIZE

    @pl.when(block == blocks - 1)
    def _():
        carry[...] = jnp.zeros_like(carry)
        grad_keys[...] = jnp.zeros_like(grad_keys)
        grad_values[...] = jnp.zeros_like(grad_values)
        head_ref[...] = jnp.zeros_like(head_ref)

    mixed, joint = mixed_ref, joint_ref
    cosine, sine = cos_ref[...], sin_ref[...]
    queries = jnp.concatenate(
        [
            turn(mixed[:, h * HEAD_SIZE : (h + 1) * HEAD_SIZE], cosine, sine)
            for h in range(q_heads)
        ],
        axis=0,
    ).astype(BF16)
    grad_out = stacked_heads(joint, 0, q_heads).astype(BF16)

    for at in range(blocks):

        @pl.when(block == at)
        def _(at=at):
            span = (at + 1) * size
            keys, values = keys_ref[:span, :], values_ref[:span, :]
            raw = mul(queries, keys, 1, 1) * SCALE
            logits = jnp.where(visible_keys(q_heads, size, at), raw, -1e30)
            weights = jnp.exp(logits - jnp.max(logits, axis=-1, keepdims=True))
            probs = weights / jnp.sum(weights, axis=-1, keepdims=True)
            grad_probs = mul(grad_out, values, 1, 1)
            delta = jnp.sum(probs * grad_probs, axis=-1, keepdims=True)
            grad_raw = (probs * (grad_probs - delta) * SCALE).astype(BF16)
            grad_queries = mul(grad_raw, keys, 1, 0)
            for h in range(q_heads):
                out_ref[:, h * HEAD_SIZE : (h + 1) * HEAD_SIZE] = turn(
                    grad_queries[h * size : (h + 1) * size], cosine, -sine
                ).astype(BF16)
            grad_keys[:span, :] += mul(grad_raw, queries, 0, 0)
            grad_values[:span, :] += mul(probs.astype(BF16), grad_out, 0, 0)

    here = pl.ds(pl.multiple_of(block * size, size), size)
    out_ref[:, cuts["k"] : cuts["k"] + HEAD_SIZE] = turn(
        grad_keys[here, :], cosine, -sine
    ).astype(BF16)
    out_ref[:, cuts["v"] : cuts["v"] + HEAD_SIZE] = grad_values[here, :].astype(BF16)

    tri, spread = tri_ref[...], spread_ref[...]
    terms = block_terms(mixed, cuts, tri, params_ref, spread)
    x = mixed[:, cuts["x"] : cuts["x"] + z_wide]
    z = mixed[:, cuts["z"] : cuts["z"] + z_wide]
    b_rows = mixed[:, cuts["b"] : cuts["b"] + STATE_SIZE].astype(BF16)
    c_rows = mixed[:, cuts["c"] : cuts["c"] + STATE_SIZE].astype(BF16)
    skip = skip_ref[...]
    causal = square_causal(size)
    pairing = mul(c_rows, b_rows, 1, 1)
    level = terms["level"]
    level_t = level.T
    enter_wide, step_wide, tail_wide = (
        terms["enter_wide"],
        terms["step_wide"],
        terms["tail_wide"],
    )
    x_step = (x * step_wide).astype(BF16)
    grad_gated = joint[:, q_wide:]
    sigmoid = jax.nn.sigmoid(z)
    grad_y = grad_gated * z * sigmoid
    grad_y16 = grad_y.astype(BF16)
    first = lax.broadcasted_iota(jnp.int32, (size, LANES), 1) < MIXER_HEAD_SIZE
    inside, grad_x_step = [], []
    grad_pairing = jnp.zeros((size, size), F32)
    none = jnp.zeros((size, LANES), BF16)
    for pair in range(heads // 2):
        lanes = slice(pair * LANES, (pair + 1) * LANES)
        both, grad_both = x_step[:, lanes], grad_y16[:, lanes]
        ys, xs = [], []
        for side, head in enumerate((2 * pair, 2 * pair + 1)):
            fading = fading_of(level, level_t, head, causal)
            mixing = (fading * pairing).astype(BF16)
            ys.append(mul(mixing, both, 1, 0))
            xs.append(mul(mixing, grad_both, 0, 0))
            alone = jnp.where(first == (side == 0), grad_both, none)
            grad_pairing = grad_pairing + fading * mul(alone, both, 1, 1)
        inside.append(jnp.where(first, ys[0], ys[1]))
        grad_x_step.append(jnp.where(first, xs[0], xs[1]))
    inside = jnp.concatenate(inside, axis=1)
    grad_x_step = jnp.concatenate(grad_x_step, axis=1)
    state = state_ref[0]
    state16 = state.astype(BF16)
    adjoint = carry[...]
    adjoint16 = adjoint.astype(BF16)
    outer = enter_wide * mul(c_rows, state16, 1, 0)
    full = inside + outer + skip * x
    grad_z = grad_gated * full * (sigmoid * (1.0 + z * (1.0 - sigmoid)))
    out_ref[:, cuts["z"] : cuts["z"] + z_wide] = grad_z.astype(BF16)
    entered = (enter_wide * grad_y).astype(BF16)
    pairing16 = grad_pairing.astype(BF16)
    grad_c = mul(entered, state16, 1, 1) + mul(pairing16, b_rows, 1, 0)
    grad_b = mul((x * tail_wide).astype(BF16), adjoint16, 1, 1) + mul(pairing16, c_rows, 0, 0)
    out_ref[:, cuts["b"] : cuts["b"] + STATE_SIZE] = grad_b.astype(BF16)
    out_ref[:, cuts["c"] : cuts["c"] + STATE_SIZE] = grad_c.astype(BF16)
    pushed = mul(b_rows, adjoint16, 1, 0)
    grad_x = step_wide * grad_x_step + tail_wide * pushed + skip * grad_y
    out_ref[:, cuts["x"] : cuts["x"] + z_wide] = grad_x.astype(BF16)

    def by_head(value):
        return near_exact(value, spread, ((1,), (1,)), 2, False)

    row_part = by_head(grad_y16.astype(F32) * inside + grad_y * outer)
    col_part = by_head(x_step.astype(F32) * grad_x_step)
    step_part = by_head(x * grad_x_step)
    tail_part = by_head(x * pushed)
    sums = jnp.concatenate(
        [
            jnp.sum(state * adjoint, axis=0, keepdims=True),
            jnp.sum(grad_y * x, axis=0, keepdims=True),
            jnp.zeros((6, z_wide), F32),
        ],
        axis=0,
    )
    sums = by_head(sums)
    step, leave, last = terms["step"], terms["leave"], terms["last"]
    moved = leave * step * tail_part
    grad_level = row_part - col_part - moved
    at_last = jnp.sum(moved, axis=0, keepdims=True) + jnp.exp(last) * sums[0:1, :]
    row = lax.broadcasted_iota(jnp.int32, (size, LANES), 0)
    grad_level = grad_level + jnp.where(row == size - 1, at_last, 0.0)
    grad_log = near_exact(tri, grad_level, ((0,), (0,)), 3, True)
    grad_step = step_part + leave * tail_part + grad_log * terms["rate"]
    grad_dt = grad_step * jax.nn.sigmoid(terms["dt_in"])
    lane = lax.broadcasted_iota(jnp.int32, (size, LANES), 1)
    grad_dt = jnp.where(lane < heads, grad_dt, 0.0)
    out_ref[:, cuts["dt"] : cuts["dt"] + LANES] = grad_dt.astype(BF16)
    head_ref[...] += jnp.concatenate(
        [
            jnp.sum(grad_dt, axis=0, keepdims=True),
            jnp.sum(grad_log * step, axis=0, keepdims=True) * terms["rate"],
            sums[1:2, :],
            jnp.zeros((5, LANES), F32),
        ],
        axis=0,
    )
    carry[...] = enter_wide[size - 1 : size, :] * adjoint + mul(c_rows, entered, 0, 0)


def mixer_tables(tokens, size, heads, bias, log_rate, skip):
    half = HEAD_SIZE // 2
    positions = jnp.arange(tokens, dtype=F32)
    frequency = THETA ** (-jnp.arange(half, dtype=F32) / half)
    angles = positions[:, None] * frequency[None, :]
    cosine, sine = jnp.cos(angles), jnp.sin(angles)
    order = jnp.arange(size)
    tri = (order[:, None] >= order[None, :]).astype(BF16)
    z_wide = heads * MIXER_HEAD_SIZE
    owner = jnp.arange(z_wide) // MIXER_HEAD_SIZE
    spread = (jnp.arange(LANES)[:, None] == owner[None, :]).astype(BF16)
    params = jnp.zeros((8, LANES), F32)
    params = params.at[0, :heads].set(bias).at[1, :heads].set(-jnp.exp(log_rate))
    return (
        jnp.concatenate([cosine, cosine], axis=1),
        jnp.concatenate([-sine, sine], axis=1),
        tri,
        params,
        spread,
        jnp.repeat(skip, MIXER_HEAD_SIZE)[None, :],
    )


def whole(shape):
    return pl.BlockSpec(shape, lambda i, place: (0,) * len(shape))


def mixer_forward(place, mixed, tables, cuts, q_heads, heads, blocks):
    tokens, wide = mixed.shape
    size = tokens // blocks
    cosine, sine, tri, params, spread, skip = tables
    z_wide = heads * MIXER_HEAD_SIZE
    out_wide = q_heads * HEAD_SIZE + z_wide

    def by_hop(width):
        return pl.BlockSpec(
            (size, width), lambda i, place: (lax.rem(place[0] - i + blocks, blocks), 0)
        )

    in_order = pl.BlockSpec((size, HEAD_SIZE), lambda i, place: (i, 0))
    return pl.pallas_call(
        functools.partial(mixer_forward_kernel, cuts, q_heads, heads, blocks),
        grid_spec=pltpu.PrefetchScalarGridSpec(
            num_scalar_prefetch=1,
            grid=(blocks,),
            in_specs=[
                by_hop(wide),
                in_order,
                in_order,
                whole(tri.shape),
                whole(params.shape),
                whole(spread.shape),
                whole(skip.shape),
            ],
            out_specs=[
                by_hop(out_wide),
                pl.BlockSpec((1, STATE_SIZE, z_wide), lambda i, place: (i, 0, 0)),
                whole((tokens, HEAD_SIZE)),
                whole((tokens, HEAD_SIZE)),
            ],
            scratch_shapes=[pltpu.VMEM((STATE_SIZE, z_wide), F32)],
        ),
        out_shape=[
            jax.ShapeDtypeStruct((tokens, out_wide), BF16),
            jax.ShapeDtypeStruct((blocks, STATE_SIZE, z_wide), F32),
            jax.ShapeDtypeStruct((tokens, HEAD_SIZE), BF16),
            jax.ShapeDtypeStruct((tokens, HEAD_SIZE), BF16),
        ],
        compiler_params=pltpu.CompilerParams(vmem_limit_bytes=VMEM_LIMIT),
        cost_estimate=pl.CostEstimate(
            flops=8_000_000_000, bytes_accessed=20_000_000, transcendentals=0
        ),
        name="mixer_forward",
    )(place, mixed, cosine, sine, tri, params, spread, skip)


def mixer_backward(place, mixed, joint, states, keys, values, tables, cuts, q_heads, heads, blocks):
    tokens, wide = mixed.shape
    size = tokens // blocks
    cosine, sine, tri, params, spread, skip = tables
    z_wide = heads * MIXER_HEAD_SIZE

    def by_hop(width):
        return pl.BlockSpec(
            (size, width), lambda i, place: (lax.rem(place[0] + i + 1, blocks), 0)
        )

    in_order = pl.BlockSpec((size, HEAD_SIZE), lambda i, place: (blocks - 1 - i, 0))
    return pl.pallas_call(
        functools.partial(mixer_backward_kernel, cuts, q_heads, heads, blocks),
        grid_spec=pltpu.PrefetchScalarGridSpec(
            num_scalar_prefetch=1,
            grid=(blocks,),
            in_specs=[
                by_hop(wide),
                by_hop(joint.shape[1]),
                pl.BlockSpec((1, STATE_SIZE, z_wide), lambda i, place: (blocks - 1 - i, 0, 0)),
                whole(keys.shape),
                whole(values.shape),
                in_order,
                in_order,
                whole(tri.shape),
                whole(params.shape),
                whole(spread.shape),
                whole(skip.shape),
            ],
            out_specs=[by_hop(wide), whole((8, LANES))],
            scratch_shapes=[
                pltpu.VMEM((tokens, HEAD_SIZE), F32),
                pltpu.VMEM((tokens, HEAD_SIZE), F32),
                pltpu.VMEM((STATE_SIZE, z_wide), F32),
            ],
        ),
        out_shape=[
            jax.ShapeDtypeStruct((tokens, wide), BF16),
            jax.ShapeDtypeStruct((8, LANES), F32),
        ],
        compiler_params=pltpu.CompilerParams(vmem_limit_bytes=VMEM_LIMIT),
        cost_estimate=pl.CostEstimate(
            flops=20_000_000_000, bytes_accessed=30_000_000, transcendentals=0
        ),
        name="mixer_backward",
    )(place, mixed, joint, states, keys, values, cosine, sine, tri, params, spread, skip)


def pack_kernel(cuts, starts_ref, *refs):
    sources = refs[: max(c[0] for out in cuts for c in out) + 1]
    outs = refs[len(sources) : len(sources) + len(cuts)]
    semaphores = refs[-1]
    copies, at = [], 0
    for out, ref in zip(cuts, outs):
        column = 0
        for source, wide in out:
            start = pl.multiple_of(starts_ref[at], LANES)
            copies.append(
                pltpu.make_async_copy(
                    sources[source].at[:, pl.ds(start, wide)],
                    ref.at[:, pl.ds(column, wide)],
                    semaphores.at[at],
                )
            )
            column += wide
            at += 1
    for copy in copies:
        copy.start()
    for copy in copies:
        copy.wait()


def pack_columns(sources, cuts):
    starts = jnp.stack([start for out in cuts for _, start, _ in out]).astype(jnp.int32)
    rows = sources[0].shape[0]
    anywhere = pl.BlockSpec(memory_space=pl.ANY)
    return pl.pallas_call(
        functools.partial(pack_kernel, [[(s, w) for s, _, w in out] for out in cuts]),
        grid_spec=pltpu.PrefetchScalarGridSpec(
            num_scalar_prefetch=1,
            grid=(1,),
            in_specs=[anywhere] * len(sources),
            out_specs=[
                pl.BlockSpec((rows, sum(w for _, _, w in out)), lambda i, starts: (0, 0))
                for out in cuts
            ],
            scratch_shapes=[pltpu.SemaphoreType.DMA((starts.shape[0],))],
        ),
        out_shape=[
            jax.ShapeDtypeStruct((rows, sum(w for _, _, w in out)), BF16) for out in cuts
        ],
        compiler_params=pltpu.CompilerParams(vmem_limit_bytes=VMEM_LIMIT),
        cost_estimate=pl.CostEstimate(
            flops=0, bytes_accessed=20_000_000, transcendentals=0
        ),
        name="pack_columns",
    )(starts, *sources)


def dense_cost(flops, *arrays):
    return pl.CostEstimate(
        flops=flops,
        bytes_accessed=sum(math.prod(a.shape) * a.dtype.itemsize for a in arrays),
        transcendentals=0,
    )


def fetch_hops(count, place, parts, target, semaphores):
    size = parts[0].shape[0]

    def copy(source, hop):
        return pltpu.make_async_copy(
            source, target.at[hop * size : (hop + 1) * size, :], semaphores.at[hop]
        )

    copy(parts[0], 0).start()
    for hop in range(1, count):

        @pl.when(place >= hop)
        def _(hop=hop):
            copy(parts[hop], hop).start()

        @pl.when(place < hop)
        def _(hop=hop):
            copy(parts[2 * count - 1 - hop], hop).start()

    for hop in range(count):
        copy(parts[0], hop).wait()


def mixer_in_kernel(count, place_ref, gain_ref, w_ref, *refs):
    parts = refs[: 2 * count - 1]
    out_ref, normed_ref, raw, semaphores = refs[2 * count - 1 :]
    size = parts[0].shape[0]

    @pl.when(pl.program_id(0) == 0)
    def _():
        fetch_hops(count, place_ref[0], parts, raw, semaphores)
        for hop in range(count):
            at = slice(hop * size, (hop + 1) * size)
            rows = raw[at, :].astype(F32)
            scaled = rows * lax.rsqrt(jnp.mean(rows * rows, axis=-1, keepdims=True) + EPSILON)
            normed_ref[at, :] = (scaled * gain_ref[...]).astype(BF16)

    out_ref[...] = mul(normed_ref[...], w_ref[...], 1, 0)


def mixer_in(place, own, ups, downs, gain, weight, wide):
    size, depth = own.shape
    count = len(ups) + 1
    tokens = size * count
    tile = max(t for t in range(LANES, 1025, LANES) if wide % t == 0)

    def fixed(shape):
        return pl.BlockSpec(shape, lambda j, place: (0, 0))

    outs = [
        jax.ShapeDtypeStruct((tokens, wide), F32),
        jax.ShapeDtypeStruct((tokens, depth), BF16),
    ]
    return pl.pallas_call(
        functools.partial(mixer_in_kernel, count),
        grid_spec=pltpu.PrefetchScalarGridSpec(
            num_scalar_prefetch=1,
            grid=(wide // tile,),
            in_specs=[
                fixed((1, depth)),
                pl.BlockSpec((depth, tile), lambda j, place: (0, j)),
            ]
            + [pl.BlockSpec(memory_space=pl.ANY)] * (2 * count - 1),
            out_specs=[
                pl.BlockSpec((tokens, tile), lambda j, place: (0, j)),
                fixed((tokens, depth)),
            ],
            scratch_shapes=[
                pltpu.VMEM((tokens, depth), BF16),
                pltpu.SemaphoreType.DMA((count,)),
            ],
        ),
        out_shape=outs,
        compiler_params=pltpu.CompilerParams(vmem_limit_bytes=VMEM_LIMIT),
        cost_estimate=dense_cost(2 * tokens * depth * wide, weight, *outs),
        name="mixer_in",
    )(place, gain, weight, own, *ups, *downs)


def ffn_kernel(
    own_ref,
    other_ref,
    act_grad_ref,
    gate_ref,
    up_ref,
    activated_ref,
    grad_gate_ref,
    grad_up_ref,
    rows_ref,
):
    @pl.when(pl.program_id(0) == 0)
    def _():
        rows_ref[: own_ref.shape[0], :] = own_ref[...]
        rows_ref[own_ref.shape[0] :, :] = other_ref[...]

    rows = rows_ref[...]
    gate = mul(rows, gate_ref[...], 1, 0)
    up = mul(rows, up_ref[...], 1, 0)
    grad = act_grad_ref[...]
    sigmoid = jax.nn.sigmoid(gate)
    silu = gate * sigmoid
    activated_ref[...] = (silu * up).astype(BF16)
    grad_gate_ref[...] = (grad * up * (sigmoid * (1.0 + gate * (1.0 - sigmoid)))).astype(BF16)
    grad_up_ref[...] = (grad * silu).astype(BF16)


def ffn_inner(own, other, act_grad, weights):
    tokens, depth = 2 * own.shape[0], own.shape[1]
    units = act_grad.shape[1]
    tile = 256
    tiles = units // tile
    out = jax.ShapeDtypeStruct((tokens, units), BF16)
    by_unit = pl.BlockSpec((tokens, tile), lambda j: (0, j))
    return pl.pallas_call(
        ffn_kernel,
        grid=(tiles,),
        in_specs=[
            pl.BlockSpec(own.shape, lambda j: (0, 0)),
            pl.BlockSpec(own.shape, lambda j: (0, 0)),
            by_unit,
            pl.BlockSpec((depth, tile), lambda j: (0, tiles + j)),
            pl.BlockSpec((depth, tile), lambda j: (0, 2 * tiles + j)),
        ],
        out_specs=[by_unit] * 3 + [pl.BlockSpec((tokens, depth), lambda j: (0, 0))],
        out_shape=[out] * 3 + [jax.ShapeDtypeStruct((tokens, depth), BF16)],
        compiler_params=pltpu.CompilerParams(vmem_limit_bytes=VMEM_LIMIT),
        cost_estimate=dense_cost(4 * tokens * depth * units, weights, out, out, out),
        name="ffn_inner",
    )(own, other, act_grad, weights, weights)


def ffn_back_kernel(count, *refs):
    own_ref, other_ref = refs[-2:]
    total = mul(refs[0][...], refs[count][...], 1, 1)
    for i in range(1, count):
        total = total + mul(refs[i][...], refs[count + i][...], 1, 1)
    half = total.shape[0] // 2
    own_ref[...] = total[:half]
    other_ref[...] = total[half:].astype(BF16)


def ffn_back(grads, weights, columns):
    tokens, units = grads[0].shape
    depth = weights.shape[0]
    tile = 256
    half = pl.BlockSpec((tokens // 2, tile), lambda j: (0, j))
    return pl.pallas_call(
        functools.partial(ffn_back_kernel, len(grads)),
        grid=(depth // tile,),
        in_specs=[pl.BlockSpec((tokens, units), lambda j: (0, 0)) for _ in grads]
        + [pl.BlockSpec((tile, units), lambda j, c=c: (j, c)) for c in columns],
        out_specs=[half, half],
        out_shape=[
            jax.ShapeDtypeStruct((tokens // 2, depth), F32),
            jax.ShapeDtypeStruct((tokens // 2, depth), BF16),
        ],
        compiler_params=pltpu.CompilerParams(vmem_limit_bytes=VMEM_LIMIT),
        cost_estimate=dense_cost(2 * len(grads) * tokens * depth * units, weights),
        name="ffn_back",
    )(*grads, *[weights for _ in columns])


def joint_kernel(count, place_ref, w_ref, *refs):
    parts = refs[: 2 * count - 1]
    out_ref, rows_ref, semaphores = refs[2 * count - 1 :]

    @pl.when(pl.program_id(0) == 0)
    def _():
        fetch_hops(count, place_ref[0], parts, rows_ref, semaphores)

    out_ref[...] = mul(rows_ref[...], w_ref[...], 1, 0)


def joint(place, own, ups, downs, weight):
    size, depth = own.shape
    count = len(ups) + 1
    tokens, wide = size * count, weight.shape[1]
    tile = min(wide, 512)
    outs = [
        jax.ShapeDtypeStruct((tokens, wide), F32),
        jax.ShapeDtypeStruct((tokens, depth), BF16),
    ]
    return pl.pallas_call(
        functools.partial(joint_kernel, count),
        grid_spec=pltpu.PrefetchScalarGridSpec(
            num_scalar_prefetch=1,
            grid=(wide // tile,),
            in_specs=[pl.BlockSpec((depth, tile), lambda j, place: (0, j))]
            + [pl.BlockSpec(memory_space=pl.ANY)] * (2 * count - 1),
            out_specs=[
                pl.BlockSpec((tokens, tile), lambda j, place: (0, j)),
                pl.BlockSpec((tokens, depth), lambda j, place: (0, 0)),
            ],
            scratch_shapes=[pltpu.SemaphoreType.DMA((count,))],
        ),
        out_shape=outs,
        compiler_params=pltpu.CompilerParams(vmem_limit_bytes=VMEM_LIMIT),
        cost_estimate=dense_cost(2 * tokens * depth * wide, weight, *outs),
        name="joint",
    )(place, weight, own, *ups, *downs)


def mixer_out_kernel(grad_ref, w_ref, normed_ref, gain_ref, sum_ref, own_ref, *other_refs):
    total = mul(grad_ref[...], w_ref[:, : grad_ref.shape[1]], 1, 1)
    size = own_ref.shape[0]
    own_ref[...] = total[:size]
    for hop, ref in enumerate(other_refs, 1):
        ref[...] = total[hop * size : (hop + 1) * size].astype(BF16)
    sums = jnp.sum(total * normed_ref[...].astype(F32), axis=0, keepdims=True) / gain_ref[...]
    sum_ref[...] = jnp.broadcast_to(sums, sum_ref.shape)


def mixer_out(grad, weights, normed, gain, size):
    tokens, wide = grad.shape
    depth = weights.shape[0]
    tile = 256
    outs = [jax.ShapeDtypeStruct((8, depth), F32), jax.ShapeDtypeStruct((size, depth), F32)]
    outs += [jax.ShapeDtypeStruct((size, depth), BF16)] * (tokens // size - 1)
    return pl.pallas_call(
        mixer_out_kernel,
        grid=(depth // tile,),
        in_specs=[
            pl.BlockSpec((tokens, wide), lambda j: (0, 0)),
            pl.BlockSpec((tile, weights.shape[1]), lambda j: (j, 0)),
            pl.BlockSpec((tokens, tile), lambda j: (0, j)),
            pl.BlockSpec((1, tile), lambda j: (0, j)),
        ],
        out_specs=[pl.BlockSpec((o.shape[0], tile), lambda j: (0, j)) for o in outs],
        out_shape=outs,
        compiler_params=pltpu.CompilerParams(vmem_limit_bytes=VMEM_LIMIT),
        cost_estimate=dense_cost(2 * tokens * depth * wide, grad, weights, normed, *outs),
        name="mixer_out",
    )(grad, weights, normed, gain)


def outer_kernel(pairs, rider_at, *refs):
    out_ref = refs[-1]
    at = 0
    for left, right, start, wide in pairs:
        value = mul(refs[left][...], refs[right][:, start : start + wide], 0, 0)
        out_ref[:, at : at + wide] = value.astype(BF16)
        at += wide
    if rider_at is not None:
        riders = refs[-2][...]
        rows = riders.shape[0]
        for k in range(out_ref.shape[0] // rows):
            block = out_ref[k * rows : (k + 1) * rows, rider_at : rider_at + LANES]
            out_ref[k * rows : (k + 1) * rows, rider_at : rider_at + LANES] = block + riders


def weight_grads(pairs, riders=None, rider_at=None):
    operands = []

    def position(array):
        for i, held in enumerate(operands):
            if held is array:
                return i
        operands.append(array)
        return len(operands) - 1

    lefts = [position(left) for left, _, _, _ in pairs]
    n_left = len(operands)
    rights = [position(right) for _, right, _, _ in pairs]
    plan = [(l, r, p[2], p[3]) for l, r, p in zip(lefts, rights, pairs)]
    tokens, depth = operands[0].shape
    wide = sum(p[3] for p in pairs)
    tile = 256
    operands += [] if riders is None else [riders]
    specs = [pl.BlockSpec((a.shape[0], tile), lambda j: (0, j)) for a in operands[:n_left]] + [
        pl.BlockSpec(a.shape, lambda j: (0, 0)) for a in operands[n_left:]
    ]
    out = jax.ShapeDtypeStruct((depth, wide), BF16)
    return pl.pallas_call(
        functools.partial(outer_kernel, plan, rider_at),
        grid=(depth // tile,),
        in_specs=specs,
        out_specs=pl.BlockSpec((tile, wide), lambda j: (j, 0)),
        out_shape=out,
        compiler_params=pltpu.CompilerParams(vmem_limit_bytes=VMEM_LIMIT),
        cost_estimate=dense_cost(2 * tokens * depth * wide, out, *operands),
        name="weight_grads",
    )(*operands)


def unpack_kernel(places, q_heads, heads, gain_columns, count, place_ref, *refs):
    arrays = 2 * count - 1
    groups = [refs[i : i + arrays] for i in range(0, len(refs) - 4, arrays)]
    mix_ref, attn_ref, ssm_ref, extra_ref = refs[-4:]
    place = place_ref[0]
    q_wide, z_wide = q_heads * HEAD_SIZE, heads * MIXER_HEAD_SIZE
    group = QUERY_HEADS // KEY_VALUE_HEADS
    key_at = QUERY_HEADS * HEAD_SIZE
    kv_wide = KEY_VALUE_HEADS * HEAD_SIZE
    z_at = key_at + 2 * kv_wide
    x_at = z_at + MIXER_HEADS * MIXER_HEAD_SIZE
    b_at = x_at + MIXER_HEADS * MIXER_HEAD_SIZE
    step = mix_ref.shape[0]
    lane = lax.broadcasted_iota(jnp.int32, (step, LANES), 1)
    head_lane = heads + gain_columns
    head_at = MIXER_HEADS + gain_columns
    shared = jnp.zeros((step, 2 * STATE_SIZE), F32)
    extra = jnp.zeros((step, LANES), F32)
    mix_ref[:, key_at : key_at + 2 * kv_wide] = jnp.zeros((step, 2 * kv_wide), F32)

    for hop in range(count):
        source = lax.rem(place - hop + count, count)

        def of(name, hop=hop):
            group, start, wide = places[name]
            parts = groups[group]
            if hop == 0:
                return parts[0][:, start : start + wide].astype(F32)
            up = parts[hop][:, start : start + wide].astype(F32)
            down = parts[2 * count - 1 - hop][:, start : start + wide].astype(F32)
            return jnp.where(place >= hop, up, down)

        def put(ref, start, value):
            ref[:, pl.ds(pl.multiple_of(start, LANES), value.shape[1])] = value

        put(mix_ref, source * q_wide, of("q"))
        put(mix_ref, z_at + source * z_wide, of("z"))
        put(mix_ref, x_at + source * z_wide, of("x"))
        put(attn_ref, source * q_wide, of("attn"))
        put(ssm_ref, source * z_wide, of("ssm"))
        shared = shared + of("bc")
        which = lax.div(source * q_heads, group)
        for name, base in (("k", key_at), ("v", key_at + kv_wide)):
            at = pl.ds(pl.multiple_of(base + which * HEAD_SIZE, LANES), HEAD_SIZE)
            mix_ref[:, at] += of(name)
        small = of("dt")
        own = jnp.where(lane < heads, small, 0.0)
        gains = jnp.where((lane >= heads) & (lane < head_lane), small, 0.0)
        column = jnp.where(lane == head_lane, small, 0.0)
        extra = (
            extra
            + pltpu.roll(own, source * heads, 1)
            + pltpu.roll(gains, MIXER_HEADS - heads, 1)
            + pltpu.roll(column, head_at - head_lane + source, 1)
        )
    mix_ref[:, b_at:] = shared
    extra_ref[...] = extra


def unpack_mixer(place, groups, places, q_heads, heads, gain_columns):
    count = len(groups[0][1]) + 1
    rows = groups[0][0].shape[0]
    step = min(rows, 128)
    widths = (
        QUERY_HEADS * HEAD_SIZE
        + 2 * KEY_VALUE_HEADS * HEAD_SIZE
        + 2 * MIXER_HEADS * MIXER_HEAD_SIZE
        + 2 * STATE_SIZE,
        QUERY_HEADS * HEAD_SIZE,
        MIXER_HEADS * MIXER_HEAD_SIZE,
        LANES,
    )
    operands = [part for own, ups, downs in groups for part in (own, *ups, *downs)]

    def spec(columns):
        return pl.BlockSpec((step, columns), lambda i, place: (i, 0))

    return pl.pallas_call(
        functools.partial(unpack_kernel, places, q_heads, heads, gain_columns, count),
        grid_spec=pltpu.PrefetchScalarGridSpec(
            num_scalar_prefetch=1,
            grid=(rows // step,),
            in_specs=[spec(o.shape[1]) for o in operands],
            out_specs=[spec(w) for w in widths],
        ),
        out_shape=[jax.ShapeDtypeStruct((rows, w), F32) for w in widths],
        compiler_params=pltpu.CompilerParams(vmem_limit_bytes=VMEM_LIMIT),
        cost_estimate=pl.CostEstimate(
            flops=100_000_000, bytes_accessed=26_000_000, transcendentals=0
        ),
        name="unpack_mixer",
    )(place, *operands)


def unpack_ffn_kernel(count, place_ref, *refs):
    arrays = 2 * count - 1
    groups = (refs[:arrays], refs[arrays : 2 * arrays])
    outs = refs[2 * arrays :]
    place = place_ref[0]
    chunk = groups[0][0].shape[0]
    half = outs[0].shape[1] // 2
    quarter = half // 2
    pieces = (
        (0, 0, 0, half, 0),
        (1, 0, half, quarter, 0),
        (1, 1, 0, quarter, quarter),
        (2, 1, quarter, half, 0),
    )
    for hop in range(count):
        source = lax.rem(place - hop + count, count)
        row = pl.multiple_of(lax.div(source, 2) * chunk, chunk)
        side = lax.rem(source, 2) * half
        for out, group, start, wide, offset in pieces:
            parts = groups[group]
            value = parts[0][:, start : start + wide] if hop == 0 else None
            if hop:
                up = parts[hop][:, start : start + wide]
                down = parts[arrays - hop][:, start : start + wide]
                value = jnp.where(place >= hop, up.astype(F32), down.astype(F32))
            column = pl.multiple_of(side + offset, LANES)
            outs[out][pl.ds(row, chunk), pl.ds(column, wide)] = value.astype(F32)


def unpack_ffn(place, groups, units):
    count = len(groups[0][1]) + 1
    rows = groups[0][0].shape[0] * (count // 2)
    operands = [part for own, ups, downs in groups for part in (own, *ups, *downs)]

    def fixed(shape):
        return pl.BlockSpec(shape, lambda i, place: (0, 0))

    return pl.pallas_call(
        functools.partial(unpack_ffn_kernel, count),
        grid_spec=pltpu.PrefetchScalarGridSpec(
            num_scalar_prefetch=1,
            grid=(1,),
            in_specs=[fixed(o.shape) for o in operands],
            out_specs=[fixed((rows, units))] * 3,
        ),
        out_shape=[jax.ShapeDtypeStruct((rows, units), F32)] * 3,
        compiler_params=pltpu.CompilerParams(vmem_limit_bytes=VMEM_LIMIT),
        cost_estimate=pl.CostEstimate(
            flops=100_000_000, bytes_accessed=22_000_000, transcendentals=0
        ),
        name="unpack_ffn",
    )(place, *operands)


def norm_back_kernel(grad_ref, swap_ref, rows_ref, gain_ref, base_ref, out_ref, low_ref, sum_ref):
    grad = grad_ref[...] + swap_ref[...].astype(F32)
    rows = rows_ref[...]
    inverse = lax.rsqrt(jnp.mean(rows * rows, axis=-1, keepdims=True) + EPSILON)
    unit = rows * inverse
    scaled = grad * gain_ref[...]
    out = base_ref[...].astype(F32) + inverse * (
        scaled - unit * jnp.mean(unit * scaled, axis=-1, keepdims=True)
    )
    out_ref[...] = out
    low_ref[...] = out.astype(BF16)

    @pl.when(pl.program_id(0) == 0)
    def _():
        sum_ref[...] = jnp.zeros_like(sum_ref)

    sum_ref[...] += jnp.broadcast_to(jnp.sum(grad * unit, axis=0, keepdims=True), sum_ref.shape)


def norm_back(grad, swap, rows, gain, base):
    size, depth = rows.shape
    step = min(size, 64)
    tile = pl.BlockSpec((step, depth), lambda i: (i, 0))
    fixed = lambda i: (0, 0)
    outs = [
        jax.ShapeDtypeStruct((size, depth), F32),
        jax.ShapeDtypeStruct((size, depth), BF16),
        jax.ShapeDtypeStruct((8, depth), F32),
    ]
    return pl.pallas_call(
        norm_back_kernel,
        grid=(size // step,),
        in_specs=[tile, tile, tile, pl.BlockSpec((1, depth), fixed), tile],
        out_specs=[tile, tile, pl.BlockSpec((8, depth), fixed)],
        out_shape=outs,
        compiler_params=pltpu.CompilerParams(vmem_limit_bytes=VMEM_LIMIT),
        cost_estimate=dense_cost(20 * size * depth, grad, swap, rows, *outs),
        name="norm_back",
    )(grad, swap, rows, gain, base)


def per_device(
    hidden_in,
    w_mix,
    w_dt,
    w_attn_out,
    w_ssm_out,
    w_gate,
    w_up,
    w_down,
    norm_gains,
    dt_bias,
    a_log,
    skip_scale,
    cotangent,
):
    w_mix, w_dt, w_attn_out, w_ssm_out = w_mix[0], w_dt[0], w_attn_out[0], w_ssm_out[0]
    w_gate, w_up, w_down = w_gate[0], w_up[0], w_down[0]
    gain_mix, gain_ffn = norm_gains[0, 0], norm_gains[0, 1]
    count, place = lax.axis_size("ctx"), lax.axis_index("ctx")
    piece, width = hidden_in.shape[1], hidden_in.shape[2]
    tokens = piece * count
    rows = w_mix.shape[0]
    hidden_units = w_gate.shape[1]
    q_heads = QUERY_HEADS // count
    group = QUERY_HEADS // KEY_VALUE_HEADS
    kv_head = (place * q_heads) // group
    heads = MIXER_HEADS // count
    q_wide, z_wide = q_heads * HEAD_SIZE, heads * MIXER_HEAD_SIZE
    key_at = QUERY_HEADS * HEAD_SIZE
    value_at = key_at + KEY_VALUE_HEADS * HEAD_SIZE
    z_at = value_at + KEY_VALUE_HEADS * HEAD_SIZE
    x_at = z_at + MIXER_HEADS * MIXER_HEAD_SIZE
    b_at = x_at + MIXER_HEADS * MIXER_HEAD_SIZE
    names = ("q", "k", "v", "z", "x", "b", "c", "dt")
    sizes = (q_wide, HEAD_SIZE, HEAD_SIZE, z_wide, z_wide, STATE_SIZE, STATE_SIZE, LANES)
    cuts, mix_wide = {}, 0
    for name, size in zip(names, sizes):
        cuts[name] = mix_wide
        mix_wide += size

    half = place % 2
    half_units = hidden_units // 2
    own_dt = lax.dynamic_slice(w_dt, (0, place * heads), (rows, heads))
    own_dt = jnp.pad(own_dt, ((0, 0), (0, LANES - heads)))
    here = jnp.reshape(place, (1,)).astype(jnp.int32)
    mix_starts = (
        (place * q_wide, q_wide),
        (key_at + kv_head * HEAD_SIZE, HEAD_SIZE),
        (value_at + kv_head * HEAD_SIZE, HEAD_SIZE),
        (z_at + place * z_wide, z_wide),
        (x_at + place * z_wide, z_wide),
        (b_at + 0 * place, 2 * STATE_SIZE),
    )
    from_half = (half * half_units, half_units)
    (mixer_own,) = pack_columns(
        (w_mix, own_dt, w_attn_out, w_ssm_out),
        (
            [(0,) + cut for cut in mix_starts]
            + [(1, 0 * place, LANES), (2, place * q_wide, q_wide), (3, place * z_wide, z_wide)],
        ),
    )
    hidden_own = hidden_in.reshape(piece, width)
    hidden_line = Chain(line_gather(hidden_own))
    advance(hidden_line)
    late_down = after(w_down, *[value for value, _ in hidden_line.sends])
    (ffn_own,) = pack_columns(
        (w_gate, w_up, late_down), ([(2,) + from_half, (0,) + from_half, (1,) + from_half],)
    )
    (ffn_own,) = advance(hidden_line, beside=(ffn_own,))
    w_mixer, w_ffn = gather_rows(mixer_own), gather_rows(ffn_own)
    w_out = w_mixer[:, mix_wide:]
    w_down_half = w_ffn[:, :half_units]

    blocks = tokens // piece

    while live(hidden_line):
        advance(hidden_line)
    hidden_ups, hidden_downs = hidden_line.result
    mixed, normed = mixer_in(
        here, hidden_own, hidden_ups, hidden_downs, gain_mix[None, :], w_mixer, mix_wide
    )
    own = [lax.dynamic_slice_in_dim(p[0], place * heads, heads) for p in (dt_bias, a_log, skip_scale)]
    tables = mixer_tables(tokens, piece, heads, *own)
    branch_in, states, keys, values = mixer_forward(
        here, mixed, tables, cuts, q_heads, heads, blocks
    )
    cot_own = cotangent.reshape(piece, width)
    cot_swap = swap_pair(after(cot_own, hidden_ups[-1], hidden_downs[-1]))
    branch_in, cot_swap = lax.optimization_barrier((branch_in, cot_swap))
    cot_pair = jnp.concatenate([cot_own, cot_swap], axis=0)
    halves, ready = [], branch_in
    for half_rows in (w_out[: width // 2], w_out[width // 2 :]):
        terms = [None] * count

        def branch_term(rows_in, hop, half_rows=half_rows):
            return dot(rows_in[hop * piece : (hop + 1) * piece], half_rows, 1, 1)

        for hop in (1, count - 1):
            terms[hop] = branch_term(ready, hop)
        branch_line = Chain(line_sum(terms))
        flight = Flight(branch_line)
        late_in = ready = after(branch_in, *flight.values)
        for hop in range(count):
            if terms[hop] is None:
                terms[hop] = branch_term(late_in, hop)
        halves.append((branch_line, flight))
    for branch_line, flight in halves:
        flight.land()
    for branch_line, _ in halves:
        while live(branch_line):
            advance(branch_line)
    branch = jnp.concatenate([branch_line.result for branch_line, _ in halves], axis=1)
    middle = hidden_own.astype(F32) + branch
    grad_act = dot(cot_pair, w_down_half, 1, 0)

    inverse_ffn = inverse_rms(middle)
    normed_ffn = (middle * inverse_ffn * gain_ffn).astype(BF16)
    normed_swap, grad_act = lax.optimization_barrier((swap_pair(normed_ffn), grad_act))
    activated, grad_gate, grad_up, normed_pair = ffn_inner(
        normed_ffn, normed_swap, grad_act, w_ffn
    )
    grad_normed_own, grad_normed_other = ffn_back((grad_gate, grad_up), w_ffn, (1, 2))
    grad_swap = swap_pair(grad_normed_other)
    activated, grad_gate, grad_up = lax.optimization_barrier(
        (activated, grad_gate, grad_up, grad_normed_other)
    )[:3]
    quarter = half_units // 2
    grad_w_first = weight_grads(
        ((normed_pair, grad_gate, 0, half_units), (normed_pair, grad_up, 0, quarter))
    )
    grad_swap, grad_w_first = lax.optimization_barrier((grad_swap, grad_w_first))
    grad_w_first = scatter_rows(grad_w_first)

    grad_middle, branch_own, gain_ffn_rows = norm_back(
        grad_normed_own, grad_swap, middle, gain_ffn[None, :], cot_own
    )
    branch_line = Chain(line_gather(branch_own))
    late_activated, late_up = lax.optimization_barrier((activated, grad_up, branch_own))[:2]
    grad_w_second = weight_grads(
        ((normed_pair, late_up, quarter, quarter), (cot_pair, late_activated, 0, half_units))
    )
    (grad_w_second,) = advance(branch_line, beside=(grad_w_second,))
    out_half, out_other = ffn_back((after(activated, grad_w_second),), w_ffn, (0,))
    grad_w_second = scatter_rows(grad_w_second)
    out_half, out_other = advance(branch_line, beside=(out_half, out_other))
    while branch_line.sends is not None:
        advance(branch_line)
    grad_joint, grad_branch = joint(here, branch_own, *branch_line.result, w_out)
    out_swap = swap_pair(after(out_other, *branch_line.result[0]))
    first = Chain(parity_gather(grad_w_first))

    grad_mixed, head_part = mixer_backward(
        here, mixed, grad_joint, states, keys, values, tables, cuts, q_heads, heads, blocks
    )
    grad_mixed, head_part, out_swap = advance(first, beside=(grad_mixed, head_part, out_swap))
    gain_rows, *dn_parts = mixer_out(grad_mixed, w_mixer, normed, gain_mix[None, :], piece)
    gain_rows, *dn_parts = advance(first, beside=(gain_rows, *dn_parts))

    gain_columns = 2 * width // rows
    riders = jnp.concatenate(
        [
            jnp.zeros((rows, heads), F32),
            jnp.stack([gain_rows[0], gain_ffn_rows[0]]).reshape(rows, gain_columns),
            jnp.pad(head_part[:3, :heads].reshape(3 * heads), (0, rows - 3 * heads))[:, None],
            jnp.zeros((rows, LANES - heads - gain_columns - 1), F32),
        ],
        axis=1,
    )
    grad_w_mixer = weight_grads(
        ((normed, grad_mixed, 0, mix_wide), (grad_branch, branch_in, 0, q_wide + z_wide)),
        riders.astype(BF16),
        cuts["dt"],
    )
    normed_sum = Chain(line_sum(dn_parts))
    (grad_w_mixer,) = advance(first, normed_sum, beside=(grad_w_mixer,))
    grad_w_mixer = scatter_rows(after(grad_w_mixer, grad_w_second))
    second = Chain(parity_gather(grad_w_second))
    advance(*live(second, first))
    while live(normed_sum):
        advance(*live(second, first, normed_sum))
    mixer = Chain(line_gather(after(grad_w_mixer, normed_sum.result)))
    while live(second, first):
        advance(*live(mixer, second, first))

    sealed = lax.optimization_barrier(
        (first.result, second.result, tuple(value for value, _ in mixer.sends))
    )
    outs = tuple(unpack_ffn(here, sealed[:2], hidden_units))
    outs = advance(*live(mixer), beside=outs)
    sealed = lax.optimization_barrier(
        (normed_sum.result, out_swap, tuple(value for value, _ in mixer.sends))
    )
    hidden_out = (middle + (out_half + sealed[1].astype(F32))).astype(BF16)
    hidden_f32 = hidden_own.astype(F32)
    grad_hidden = grad_middle + rms_pull(
        hidden_f32, inverse_rms(hidden_f32), gain_mix, sealed[0]
    )
    hidden_out, grad_hidden = advance(mixer, beside=(hidden_out, grad_hidden))
    while live(mixer):
        advance(mixer)
    out_gate, out_up, out_down = outs

    places = {name: (0, cuts[name], size) for name, size in zip(names, sizes)}
    places["bc"] = (0, cuts["b"], 2 * STATE_SIZE)
    places["attn"] = (0, mix_wide, q_wide)
    places["ssm"] = (0, mix_wide + q_wide, z_wide)
    out_mix, out_attn, out_ssm, extra = unpack_mixer(
        here, ((grad_w_mixer,) + mixer.result,), places, q_heads, heads, gain_columns
    )
    head_at = MIXER_HEADS + gain_columns
    gain_sums = extra[:, MIXER_HEADS:head_at].reshape(norm_gains.shape)
    head_sums = extra[: 3 * heads, head_at : head_at + count].reshape(3, heads, count)
    head_sums = jnp.swapaxes(head_sums, 1, 2).reshape(3, MIXER_HEADS)

    return (
        hidden_out.reshape(hidden_in.shape),
        grad_hidden.reshape(hidden_in.shape),
        out_mix[None],
        extra[None, :, :MIXER_HEADS],
        out_attn[None],
        out_ssm[None],
        out_gate[None],
        out_up[None],
        out_down[None],
        gain_sums,
        head_sums[0][None],
        head_sums[1][None],
        head_sums[2][None],
    )


def solution(mesh):
    split, rows = P("fsdp", "ctx", None), P(None, "fsdp", None)
    return jax.shard_map(
        per_device,
        mesh=mesh,
        in_specs=(split,) + (rows,) * 7 + (P(),) * 4 + (split,),
        out_specs=(split, split) + (rows,) * 7 + (P(),) * 4,
        check_vma=False,
    )
```

```python
import functools
import math

import jax
import jax.numpy as jnp
from jax import lax
from jax.experimental import pallas as pl
from jax.experimental.pallas import tpu as pltpu
from jax.sharding import PartitionSpec as P

QUERY_HEADS = 8
KEY_VALUE_HEADS = 2
HEAD_SIZE = 128
MIXER_HEADS = 48
MIXER_HEAD_SIZE = 64
STATE_SIZE = 256
LANES = 128

EPSILON = 1e-05
THETA = 10000.0
SCALE = 1.0 / math.sqrt(HEAD_SIZE)
VMEM_LIMIT = 56 * 1024 * 1024
BF16 = jnp.bfloat16
F32 = jnp.float32


def swap_pair(value):
    count = lax.axis_size("ctx")
    return lax.ppermute(value, "ctx", [(i, i ^ 1) for i in range(count)])


def after(value, *earlier):
    return lax.optimization_barrier((value,) + earlier)[0]


class Chain:
    def __init__(self, steps):
        self.steps, self.sends, self.result = steps, next(steps), None

    def take(self, got):
        try:
            self.sends = self.steps.send(got)
        except StopIteration as stop:
            self.sends, self.result = None, stop.value


class Flight:
    def __init__(self, *chains):
        self.chains = chains
        sends = [send for chain in chains for send in chain.sends]
        self.values = lax.optimization_barrier(tuple(value for value, _ in sends))
        self.got = tuple(
            lax.ppermute(v, "ctx", pairs) for v, (_, pairs) in zip(self.values, sends)
        )

    def land(self, beside=()):
        sealed = lax.optimization_barrier(self.got + tuple(beside))
        got = sealed[: len(self.got)]
        for chain in self.chains:
            count = len(chain.sends)
            chain.take(got[:count])
            got = got[count:]
        return sealed[len(self.got) :]


def advance(*chains, beside=()):
    return Flight(*chains).land(beside)


def live(*chains):
    return [chain for chain in chains if chain.sends is not None]


def finish(steps):
    chain = Chain(steps)
    while chain.sends is not None:
        advance(chain)
    return chain.result


def line_gather(value):
    count = lax.axis_size("ctx")
    up = down = value
    ups, downs = [], []
    for hop in range(1, count):
        up, down = yield [
            (up, [(i, i + 1) for i in range(hop - 1, count - 1)]),
            (down, [(i + 1, i) for i in range(count - hop)]),
        ]
        ups.append(up)
        downs.append(down)
    return ups, downs


def in_hops(value, ups, downs):
    count, place = lax.axis_size("ctx"), lax.axis_index("ctx")
    return [value] + [
        jnp.where(place >= hop, ups[hop - 1], downs[count - hop - 1]) for hop in range(1, count)
    ]


def gather_ctx(value):
    return in_hops(value, *finish(line_gather(value)))


def line_sum(parts):
    count = len(parts)
    up = down = 0.0
    for hop in range(1, count):
        up, down = yield [
            ((parts[hop] + up).astype(BF16), [(i, i + 1) for i in range(hop)]),
            (
                (parts[count - hop] + down).astype(BF16),
                [(i, i - 1) for i in range(count - hop, count)],
            ),
        ]
        up, down = up.astype(F32), down.astype(F32)
    return parts[0] + up + down


def parity_sum(grad):
    count = lax.axis_size("ctx")
    members, member = count // 2, lax.axis_index("ctx") // 2
    chunk = grad.shape[0] // members
    got = yield [
        (
            lax.dynamic_slice_in_dim(grad, ((member + hop) % members) * chunk, chunk, 0),
            [(i, (i + 2 * hop) % count) for i in range(count)],
        )
        for hop in range(1, members)
    ]
    total = lax.dynamic_slice_in_dim(grad, member * chunk, chunk, 0).astype(F32)
    for block in got:
        total = total + block.astype(F32)
    return total.astype(BF16)


def parity_gather(grad):
    total = yield from parity_sum(grad)
    ups, downs = yield from line_gather(total)
    return total, ups, downs


def gather_rows(value):
    return lax.all_gather(value, "fsdp", axis=0, tiled=True)


def scatter_rows(value):
    return lax.psum_scatter(value, "fsdp", scatter_dimension=0, tiled=True)


def dot(left, right, left_dim, right_dim):
    return lax.dot_general(
        left, right, (((left_dim,), (right_dim,)), ((), ())), preferred_element_type=F32
    )


def inverse_rms(rows):
    return lax.rsqrt(jnp.mean(rows * rows, axis=-1, keepdims=True) + EPSILON)


def rms_pull(rows, inverse, gain, grad):
    scaled = grad * gain
    return inverse * (scaled - rows * inverse * inverse * jnp.mean(rows * scaled, -1, keepdims=True))


def lanes_split(value, terms):
    parts = []
    for _ in range(terms):
        part = value.astype(BF16)
        parts.append(part)
        value = value - part.astype(F32)
    return parts


def near_exact(left, right, dims, terms, split_right):
    total = None
    for part in lanes_split(right if split_right else left, terms):
        pair = (left, part) if split_right else (part, right)
        one = lax.dot_general(*pair, (dims, ((), ())), preferred_element_type=F32)
        total = one if total is None else total + one
    return total


def mul(left, right, left_dim, right_dim):
    return lax.dot_general(
        left, right, (((left_dim,), (right_dim,)), ((), ())), preferred_element_type=F32
    )


def turn(vectors, cosine, sine):
    return vectors * cosine + pltpu.roll(vectors, HEAD_SIZE // 2, 1) * sine


def softplus(value):
    return jnp.maximum(value, 0.0) + jnp.log1p(jnp.exp(-jnp.abs(value)))


def block_terms(mixed, cuts, tri, params, spread):
    size = mixed.shape[0]
    dt_in = mixed[:, cuts["dt"] : cuts["dt"] + LANES] + params[0:1, :]
    step = softplus(dt_in)
    rate = params[1:2, :]
    level = near_exact(tri, step * rate, ((1,), (0,)), 3, True)
    last = level[size - 1 : size, :]
    enter = jnp.exp(level)
    leave = jnp.exp(last - level)
    wide = near_exact(
        jnp.concatenate([enter, step, leave * step], axis=0), spread, ((1,), (0,)), 2, False
    )
    return dict(
        dt_in=dt_in,
        step=step,
        rate=rate,
        level=level,
        last=last,
        leave=leave,
        enter_wide=wide[:size],
        step_wide=wide[size : 2 * size],
        tail_wide=wide[2 * size :],
    )


def fading_of(level, level_t, head, causal):
    gap = level[:, head : head + 1] - level_t[head : head + 1, :]
    return jnp.exp(jnp.where(causal, gap, -1e30))


def square_causal(size):
    row = lax.broadcasted_iota(jnp.int32, (size, size), 0)
    col = lax.broadcasted_iota(jnp.int32, (size, size), 1)
    return row >= col


def stacked_heads(value, at, count):
    return jnp.concatenate(
        [value[:, at + h * HEAD_SIZE : at + (h + 1) * HEAD_SIZE] for h in range(count)], axis=0
    )


def unstacked(value, count):
    size = value.shape[0] // count
    return jnp.concatenate([value[h * size : (h + 1) * size] for h in range(count)], axis=1)


def visible_keys(q_heads, size, block):
    shape = (q_heads * size, (block + 1) * size)
    row = lax.broadcasted_iota(jnp.int32, shape, 0)
    col = lax.broadcasted_iota(jnp.int32, shape, 1)
    return (row % size) + block * size >= col


def mixer_forward_kernel(
    cuts,
    q_heads,
    heads,
    blocks,
    place_ref,
    mixed_ref,
    cos_ref,
    sin_ref,
    tri_ref,
    params_ref,
    spread_ref,
    skip_ref,
    out_ref,
    state_ref,
    keys_ref,
    values_ref,
    carry,
):
    block = pl.program_id(0)
    size = mixed_ref.shape[0]
    q_wide, z_wide = q_heads * HEAD_SIZE, heads * MIXER_HEAD_SIZE

    @pl.when(block == 0)
    def _():
        carry[...] = jnp.zeros_like(carry)

    mixed = mixed_ref
    cosine, sine = cos_ref[...], sin_ref[...]
    here = pl.ds(pl.multiple_of(block * size, size), size)
    keys_ref[here, :] = turn(
        mixed[:, cuts["k"] : cuts["k"] + HEAD_SIZE], cosine, sine
    ).astype(BF16)
    values_ref[here, :] = mixed[:, cuts["v"] : cuts["v"] + HEAD_SIZE].astype(BF16)
    queries = jnp.concatenate(
        [
            turn(mixed[:, h * HEAD_SIZE : (h + 1) * HEAD_SIZE], cosine, sine)
            for h in range(q_heads)
        ],
        axis=0,
    ).astype(BF16)

    for at in range(blocks):

        @pl.when(block == at)
        def _(at=at):
            span = (at + 1) * size
            raw = mul(queries, keys_ref[:span, :], 1, 1) * SCALE
            logits = jnp.where(visible_keys(q_heads, size, at), raw, -1e30)
            weights = jnp.exp(logits - jnp.max(logits, axis=-1, keepdims=True))
            total = jnp.sum(weights, axis=-1, keepdims=True)
            attended = mul(weights.astype(BF16), values_ref[:span, :], 1, 0) / total
            out_ref[:, :q_wide] = unstacked(attended, q_heads).astype(BF16)

    terms = block_terms(mixed, cuts, tri_ref[...], params_ref, spread_ref[...])
    x = mixed[:, cuts["x"] : cuts["x"] + z_wide]
    b_rows = mixed[:, cuts["b"] : cuts["b"] + STATE_SIZE].astype(BF16)
    c_rows = mixed[:, cuts["c"] : cuts["c"] + STATE_SIZE].astype(BF16)
    causal = square_causal(size)
    pairing = mul(c_rows, b_rows, 1, 1)
    level = terms["level"]
    level_t = level.T
    x_step = (x * terms["step_wide"]).astype(BF16)
    first = lax.broadcasted_iota(jnp.int32, (size, LANES), 1) < MIXER_HEAD_SIZE
    inside = []
    for pair in range(heads // 2):
        both = x_step[:, pair * LANES : (pair + 1) * LANES]
        sides = []
        for head in (2 * pair, 2 * pair + 1):
            mixing = (fading_of(level, level_t, head, causal) * pairing).astype(BF16)
            sides.append(mul(mixing, both, 1, 0))
        inside.append(jnp.where(first, sides[0], sides[1]))
    state = carry[...]
    state_ref[0] = state
    full = (
        jnp.concatenate(inside, axis=1)
        + terms["enter_wide"] * mul(c_rows, state.astype(BF16), 1, 0)
        + skip_ref[...] * x
    )
    z = mixed[:, cuts["z"] : cuts["z"] + z_wide]
    out_ref[:, q_wide:] = (full * z * jax.nn.sigmoid(z)).astype(BF16)
    fresh = mul(b_rows, (x * terms["tail_wide"]).astype(BF16), 0, 0)
    carry[...] = terms["enter_wide"][size - 1 : size, :] * state + fresh


def mixer_backward_kernel(
    cuts,
    q_heads,
    heads,
    blocks,
    place_ref,
    mixed_ref,
    joint_ref,
    state_ref,
    keys_ref,
    values_ref,
    cos_ref,
    sin_ref,
    tri_ref,
    params_ref,
    spread_ref,
    skip_ref,
    out_ref,
    head_ref,
    grad_keys,
    grad_values,
    carry,
):
    block = blocks - 1 - pl.program_id(0)
    size = mixed_ref.shape[0]
    q_wide, z_wide = q_heads * HEAD_SIZE, heads * MIXER_HEAD_SIZE

    @pl.when(block == blocks - 1)
    def _():
        carry[...] = jnp.zeros_like(carry)
        grad_keys[...] = jnp.zeros_like(grad_keys)
        grad_values[...] = jnp.zeros_like(grad_values)
        head_ref[...] = jnp.zeros_like(head_ref)

    mixed, joint = mixed_ref, joint_ref
    cosine, sine = cos_ref[...], sin_ref[...]
    queries = jnp.concatenate(
        [
            turn(mixed[:, h * HEAD_SIZE : (h + 1) * HEAD_SIZE], cosine, sine)
            for h in range(q_heads)
        ],
        axis=0,
    ).astype(BF16)
    grad_out = stacked_heads(joint, 0, q_heads).astype(BF16)

    for at in range(blocks):

        @pl.when(block == at)
        def _(at=at):
            span = (at + 1) * size
            keys, values = keys_ref[:span, :], values_ref[:span, :]
            raw = mul(queries, keys, 1, 1) * SCALE
            logits = jnp.where(visible_keys(q_heads, size, at), raw, -1e30)
            weights = jnp.exp(logits - jnp.max(logits, axis=-1, keepdims=True))
            probs = weights * (1.0 / jnp.sum(weights, axis=-1, keepdims=True))
            grad_probs = mul(grad_out, values, 1, 1)
            delta = jnp.sum(probs * grad_probs, axis=-1, keepdims=True)
            grad_raw = (probs * (grad_probs - delta) * SCALE).astype(BF16)
            grad_queries = mul(grad_raw, keys, 1, 0)
            for h in range(q_heads):
                out_ref[:, h * HEAD_SIZE : (h + 1) * HEAD_SIZE] = turn(
                    grad_queries[h * size : (h + 1) * size], cosine, -sine
                ).astype(BF16)
            grad_keys[:span, :] += mul(grad_raw, queries, 0, 0)
            grad_values[:span, :] += mul(probs.astype(BF16), grad_out, 0, 0)

    here = pl.ds(pl.multiple_of(block * size, size), size)
    out_ref[:, cuts["k"] : cuts["k"] + HEAD_SIZE] = turn(
        grad_keys[here, :], cosine, -sine
    ).astype(BF16)
    out_ref[:, cuts["v"] : cuts["v"] + HEAD_SIZE] = grad_values[here, :].astype(BF16)

    tri, spread = tri_ref[...], spread_ref[...]
    terms = block_terms(mixed, cuts, tri, params_ref, spread)
    x = mixed[:, cuts["x"] : cuts["x"] + z_wide]
    z = mixed[:, cuts["z"] : cuts["z"] + z_wide]
    b_rows = mixed[:, cuts["b"] : cuts["b"] + STATE_SIZE].astype(BF16)
    c_rows = mixed[:, cuts["c"] : cuts["c"] + STATE_SIZE].astype(BF16)
    skip = skip_ref[...]
    causal = square_causal(size)
    pairing = mul(c_rows, b_rows, 1, 1)
    level = terms["level"]
    level_t = level.T
    enter_wide, step_wide, tail_wide = (
        terms["enter_wide"],
        terms["step_wide"],
        terms["tail_wide"],
    )
    x_step = (x * step_wide).astype(BF16)
    grad_gated = joint[:, q_wide:]
    sigmoid = jax.nn.sigmoid(z)
    grad_y = grad_gated * z * sigmoid
    grad_y16 = grad_y.astype(BF16)
    first = lax.broadcasted_iota(jnp.int32, (size, LANES), 1) < MIXER_HEAD_SIZE
    inside, grad_x_step = [], []
    grad_pairing = jnp.zeros((size, size), F32)
    none = jnp.zeros((size, LANES), BF16)
    for pair in range(heads // 2):
        lanes = slice(pair * LANES, (pair + 1) * LANES)
        both, grad_both = x_step[:, lanes], grad_y16[:, lanes]
        ys, xs = [], []
        for side, head in enumerate((2 * pair, 2 * pair + 1)):
            fading = fading_of(level, level_t, head, causal)
            mixing = (fading * pairing).astype(BF16)
            ys.append(mul(mixing, both, 1, 0))
            xs.append(mul(mixing, grad_both, 0, 0))
            alone = jnp.where(first == (side == 0), grad_both, none)
            grad_pairing = grad_pairing + fading * mul(alone, both, 1, 1)
        inside.append(jnp.where(first, ys[0], ys[1]))
        grad_x_step.append(jnp.where(first, xs[0], xs[1]))
    inside = jnp.concatenate(inside, axis=1)
    grad_x_step = jnp.concatenate(grad_x_step, axis=1)
    state = state_ref[0]
    state16 = state.astype(BF16)
    adjoint = carry[...]
    adjoint16 = adjoint.astype(BF16)
    outer = enter_wide * mul(c_rows, state16, 1, 0)
    full = inside + outer + skip * x
    grad_z = grad_gated * full * (sigmoid * (1.0 + z * (1.0 - sigmoid)))
    out_ref[:, cuts["z"] : cuts["z"] + z_wide] = grad_z.astype(BF16)
    entered = (enter_wide * grad_y).astype(BF16)
    pairing16 = grad_pairing.astype(BF16)
    grad_c = mul(entered, state16, 1, 1) + mul(pairing16, b_rows, 1, 0)
    grad_b = mul((x * tail_wide).astype(BF16), adjoint16, 1, 1) + mul(pairing16, c_rows, 0, 0)
    out_ref[:, cuts["b"] : cuts["b"] + STATE_SIZE] = grad_b.astype(BF16)
    out_ref[:, cuts["c"] : cuts["c"] + STATE_SIZE] = grad_c.astype(BF16)
    pushed = mul(b_rows, adjoint16, 1, 0)
    grad_x = step_wide * grad_x_step + tail_wide * pushed + skip * grad_y
    out_ref[:, cuts["x"] : cuts["x"] + z_wide] = grad_x.astype(BF16)

    def by_head(value):
        return near_exact(value, spread, ((1,), (1,)), 2, False)

    row_part = by_head(grad_y16.astype(F32) * inside + grad_y * outer)
    col_part = by_head(x_step.astype(F32) * grad_x_step)
    step_part = by_head(x * grad_x_step)
    tail_part = by_head(x * pushed)
    sums = jnp.concatenate(
        [
            jnp.sum(state * adjoint, axis=0, keepdims=True),
            jnp.sum(grad_y * x, axis=0, keepdims=True),
            jnp.zeros((6, z_wide), F32),
        ],
        axis=0,
    )
    sums = by_head(sums)
    step, leave, last = terms["step"], terms["leave"], terms["last"]
    moved = leave * step * tail_part
    grad_level = row_part - col_part - moved
    at_last = jnp.sum(moved, axis=0, keepdims=True) + jnp.exp(last) * sums[0:1, :]
    row = lax.broadcasted_iota(jnp.int32, (size, LANES), 0)
    grad_level = grad_level + jnp.where(row == size - 1, at_last, 0.0)
    grad_log = near_exact(tri, grad_level, ((0,), (0,)), 3, True)
    grad_step = step_part + leave * tail_part + grad_log * terms["rate"]
    grad_dt = grad_step * jax.nn.sigmoid(terms["dt_in"])
    lane = lax.broadcasted_iota(jnp.int32, (size, LANES), 1)
    grad_dt = jnp.where(lane < heads, grad_dt, 0.0)
    out_ref[:, cuts["dt"] : cuts["dt"] + LANES] = grad_dt.astype(BF16)
    head_ref[...] += jnp.concatenate(
        [
            jnp.sum(grad_dt, axis=0, keepdims=True),
            jnp.sum(grad_log * step, axis=0, keepdims=True) * terms["rate"],
            sums[1:2, :],
            jnp.zeros((5, LANES), F32),
        ],
        axis=0,
    )
    carry[...] = enter_wide[size - 1 : size, :] * adjoint + mul(c_rows, entered, 0, 0)


def mixer_tables(tokens, size, heads, bias, log_rate, skip):
    half = HEAD_SIZE // 2
    positions = jnp.arange(tokens, dtype=F32)
    frequency = THETA ** (-jnp.arange(half, dtype=F32) / half)
    angles = positions[:, None] * frequency[None, :]
    cosine, sine = jnp.cos(angles), jnp.sin(angles)
    order = jnp.arange(size)
    tri = (order[:, None] >= order[None, :]).astype(BF16)
    z_wide = heads * MIXER_HEAD_SIZE
    owner = jnp.arange(z_wide) // MIXER_HEAD_SIZE
    spread = (jnp.arange(LANES)[:, None] == owner[None, :]).astype(BF16)
    params = jnp.zeros((8, LANES), F32)
    params = params.at[0, :heads].set(bias).at[1, :heads].set(-jnp.exp(log_rate))
    return (
        jnp.concatenate([cosine, cosine], axis=1),
        jnp.concatenate([-sine, sine], axis=1),
        tri,
        params,
        spread,
        jnp.repeat(skip, MIXER_HEAD_SIZE)[None, :],
    )


def whole(shape):
    return pl.BlockSpec(shape, lambda i, place: (0,) * len(shape))


def mixer_forward(place, mixed, tables, cuts, q_heads, heads, blocks):
    tokens, wide = mixed.shape
    size = tokens // blocks
    cosine, sine, tri, params, spread, skip = tables
    z_wide = heads * MIXER_HEAD_SIZE
    out_wide = q_heads * HEAD_SIZE + z_wide

    def by_hop(width):
        return pl.BlockSpec(
            (size, width), lambda i, place: (lax.rem(place[0] - i + blocks, blocks), 0)
        )

    in_order = pl.BlockSpec((size, HEAD_SIZE), lambda i, place: (i, 0))
    return pl.pallas_call(
        functools.partial(mixer_forward_kernel, cuts, q_heads, heads, blocks),
        grid_spec=pltpu.PrefetchScalarGridSpec(
            num_scalar_prefetch=1,
            grid=(blocks,),
            in_specs=[
                by_hop(wide),
                in_order,
                in_order,
                whole(tri.shape),
                whole(params.shape),
                whole(spread.shape),
                whole(skip.shape),
            ],
            out_specs=[
                by_hop(out_wide),
                pl.BlockSpec((1, STATE_SIZE, z_wide), lambda i, place: (i, 0, 0)),
                whole((tokens, HEAD_SIZE)),
                whole((tokens, HEAD_SIZE)),
            ],
            scratch_shapes=[pltpu.VMEM((STATE_SIZE, z_wide), F32)],
        ),
        out_shape=[
            jax.ShapeDtypeStruct((tokens, out_wide), BF16),
            jax.ShapeDtypeStruct((blocks, STATE_SIZE, z_wide), F32),
            jax.ShapeDtypeStruct((tokens, HEAD_SIZE), BF16),
            jax.ShapeDtypeStruct((tokens, HEAD_SIZE), BF16),
        ],
        compiler_params=pltpu.CompilerParams(vmem_limit_bytes=VMEM_LIMIT),
        cost_estimate=pl.CostEstimate(
            flops=8_000_000_000, bytes_accessed=20_000_000, transcendentals=0
        ),
        name="mixer_forward",
    )(place, mixed, cosine, sine, tri, params, spread, skip)


def mixer_backward(place, mixed, joint, states, keys, values, tables, cuts, q_heads, heads, blocks):
    tokens, wide = mixed.shape
    size = tokens // blocks
    cosine, sine, tri, params, spread, skip = tables
    z_wide = heads * MIXER_HEAD_SIZE

    def by_hop(width):
        return pl.BlockSpec(
            (size, width), lambda i, place: (lax.rem(place[0] + i + 1, blocks), 0)
        )

    in_order = pl.BlockSpec((size, HEAD_SIZE), lambda i, place: (blocks - 1 - i, 0))
    return pl.pallas_call(
        functools.partial(mixer_backward_kernel, cuts, q_heads, heads, blocks),
        grid_spec=pltpu.PrefetchScalarGridSpec(
            num_scalar_prefetch=1,
            grid=(blocks,),
            in_specs=[
                by_hop(wide),
                by_hop(joint.shape[1]),
                pl.BlockSpec((1, STATE_SIZE, z_wide), lambda i, place: (blocks - 1 - i, 0, 0)),
                whole(keys.shape),
                whole(values.shape),
                in_order,
                in_order,
                whole(tri.shape),
                whole(params.shape),
                whole(spread.shape),
                whole(skip.shape),
            ],
            out_specs=[by_hop(wide), whole((8, LANES))],
            scratch_shapes=[
                pltpu.VMEM((tokens, HEAD_SIZE), F32),
                pltpu.VMEM((tokens, HEAD_SIZE), F32),
                pltpu.VMEM((STATE_SIZE, z_wide), F32),
            ],
        ),
        out_shape=[
            jax.ShapeDtypeStruct((tokens, wide), BF16),
            jax.ShapeDtypeStruct((8, LANES), F32),
        ],
        compiler_params=pltpu.CompilerParams(vmem_limit_bytes=VMEM_LIMIT),
        cost_estimate=pl.CostEstimate(
            flops=20_000_000_000, bytes_accessed=30_000_000, transcendentals=0
        ),
        name="mixer_backward",
    )(place, mixed, joint, states, keys, values, cosine, sine, tri, params, spread, skip)


def pack_kernel(cuts, starts_ref, *refs):
    sources = refs[: max(c[0] for out in cuts for c in out) + 1]
    outs = refs[len(sources) : len(sources) + len(cuts)]
    semaphores = refs[-1]
    copies, at = [], 0
    for out, ref in zip(cuts, outs):
        column = 0
        for source, wide in out:
            start = pl.multiple_of(starts_ref[at], LANES)
            copies.append(
                pltpu.make_async_copy(
                    sources[source].at[:, pl.ds(start, wide)],
                    ref.at[:, pl.ds(column, wide)],
                    semaphores.at[at],
                )
            )
            column += wide
            at += 1
    for copy in copies:
        copy.start()
    for copy in copies:
        copy.wait()


def pack_columns(sources, cuts):
    starts = jnp.stack([start for out in cuts for _, start, _ in out]).astype(jnp.int32)
    rows = sources[0].shape[0]
    anywhere = pl.BlockSpec(memory_space=pl.ANY)
    return pl.pallas_call(
        functools.partial(pack_kernel, [[(s, w) for s, _, w in out] for out in cuts]),
        grid_spec=pltpu.PrefetchScalarGridSpec(
            num_scalar_prefetch=1,
            grid=(1,),
            in_specs=[anywhere] * len(sources),
            out_specs=[
                pl.BlockSpec((rows, sum(w for _, _, w in out)), lambda i, starts: (0, 0))
                for out in cuts
            ],
            scratch_shapes=[pltpu.SemaphoreType.DMA((starts.shape[0],))],
        ),
        out_shape=[
            jax.ShapeDtypeStruct((rows, sum(w for _, _, w in out)), BF16) for out in cuts
        ],
        compiler_params=pltpu.CompilerParams(vmem_limit_bytes=VMEM_LIMIT),
        cost_estimate=pl.CostEstimate(
            flops=0, bytes_accessed=20_000_000, transcendentals=0
        ),
        name="pack_columns",
    )(starts, *sources)


def dense_cost(flops, *arrays):
    return pl.CostEstimate(
        flops=flops,
        bytes_accessed=sum(math.prod(a.shape) * a.dtype.itemsize for a in arrays),
        transcendentals=0,
    )


def fetch_hops(count, place, parts, target, semaphores):
    size = parts[0].shape[0]

    def copy(source, hop):
        return pltpu.make_async_copy(
            source, target.at[hop * size : (hop + 1) * size, :], semaphores.at[hop]
        )

    copy(parts[0], 0).start()
    for hop in range(1, count):

        @pl.when(place >= hop)
        def _(hop=hop):
            copy(parts[hop], hop).start()

        @pl.when(place < hop)
        def _(hop=hop):
            copy(parts[2 * count - 1 - hop], hop).start()

    for hop in range(count):
        copy(parts[0], hop).wait()


def mixer_in_kernel(count, place_ref, gain_ref, w_ref, *refs):
    parts = refs[: 2 * count - 1]
    out_ref, normed_ref, raw, semaphores = refs[2 * count - 1 :]
    size = parts[0].shape[0]

    @pl.when(pl.program_id(0) == 0)
    def _():
        fetch_hops(count, place_ref[0], parts, raw, semaphores)
        for hop in range(count):
            at = slice(hop * size, (hop + 1) * size)
            rows = raw[at, :].astype(F32)
            scaled = rows * lax.rsqrt(jnp.mean(rows * rows, axis=-1, keepdims=True) + EPSILON)
            normed_ref[at, :] = (scaled * gain_ref[...]).astype(BF16)

    out_ref[...] = mul(normed_ref[...], w_ref[...], 1, 0)


def mixer_in(place, own, ups, downs, gain, weight, wide):
    size, depth = own.shape
    count = len(ups) + 1
    tokens = size * count
    tile = max(t for t in range(LANES, 1025, LANES) if wide % t == 0)

    def fixed(shape):
        return pl.BlockSpec(shape, lambda j, place: (0, 0))

    outs = [
        jax.ShapeDtypeStruct((tokens, wide), F32),
        jax.ShapeDtypeStruct((tokens, depth), BF16),
    ]
    return pl.pallas_call(
        functools.partial(mixer_in_kernel, count),
        grid_spec=pltpu.PrefetchScalarGridSpec(
            num_scalar_prefetch=1,
            grid=(wide // tile,),
            in_specs=[
                fixed((1, depth)),
                pl.BlockSpec((depth, tile), lambda j, place: (0, j)),
            ]
            + [pl.BlockSpec(memory_space=pl.ANY)] * (2 * count - 1),
            out_specs=[
                pl.BlockSpec((tokens, tile), lambda j, place: (0, j)),
                fixed((tokens, depth)),
            ],
            scratch_shapes=[
                pltpu.VMEM((tokens, depth), BF16),
                pltpu.SemaphoreType.DMA((count,)),
            ],
        ),
        out_shape=outs,
        compiler_params=pltpu.CompilerParams(vmem_limit_bytes=VMEM_LIMIT),
        cost_estimate=dense_cost(2 * tokens * depth * wide, weight, *outs),
        name="mixer_in",
    )(place, gain, weight, own, *ups, *downs)


def ffn_kernel(
    own_ref,
    other_ref,
    act_grad_ref,
    gate_ref,
    up_ref,
    activated_ref,
    grad_gate_ref,
    grad_up_ref,
    rows_ref,
):
    @pl.when(pl.program_id(0) == 0)
    def _():
        rows_ref[: own_ref.shape[0], :] = own_ref[...]
        rows_ref[own_ref.shape[0] :, :] = other_ref[...]

    rows = rows_ref[...]
    gate = mul(rows, gate_ref[...], 1, 0)
    up = mul(rows, up_ref[...], 1, 0)
    grad = act_grad_ref[...]
    sigmoid = jax.nn.sigmoid(gate)
    silu = gate * sigmoid
    activated_ref[...] = (silu * up).astype(BF16)
    grad_gate_ref[...] = (grad * up * (sigmoid * (1.0 + gate * (1.0 - sigmoid)))).astype(BF16)
    grad_up_ref[...] = (grad * silu).astype(BF16)


def ffn_inner(own, other, act_grad, weights):
    tokens, depth = 2 * own.shape[0], own.shape[1]
    units = act_grad.shape[1]
    tile = 256
    tiles = units // tile
    out = jax.ShapeDtypeStruct((tokens, units), BF16)
    by_unit = pl.BlockSpec((tokens, tile), lambda j: (0, j))
    return pl.pallas_call(
        ffn_kernel,
        grid=(tiles,),
        in_specs=[
            pl.BlockSpec(own.shape, lambda j: (0, 0)),
            pl.BlockSpec(own.shape, lambda j: (0, 0)),
            by_unit,
            pl.BlockSpec((depth, tile), lambda j: (0, tiles + j)),
            pl.BlockSpec((depth, tile), lambda j: (0, 2 * tiles + j)),
        ],
        out_specs=[by_unit] * 3 + [pl.BlockSpec((tokens, depth), lambda j: (0, 0))],
        out_shape=[out] * 3 + [jax.ShapeDtypeStruct((tokens, depth), BF16)],
        compiler_params=pltpu.CompilerParams(vmem_limit_bytes=VMEM_LIMIT),
        cost_estimate=dense_cost(4 * tokens * depth * units, weights, out, out, out),
        name="ffn_inner",
    )(own, other, act_grad, weights, weights)


def ffn_back_kernel(count, *refs):
    own_ref, other_ref = refs[-2:]
    total = mul(refs[0][...], refs[count][...], 1, 1)
    for i in range(1, count):
        total = total + mul(refs[i][...], refs[count + i][...], 1, 1)
    half = total.shape[0] // 2
    own_ref[...] = total[:half]
    other_ref[...] = total[half:].astype(BF16)


def ffn_back(grads, weights, columns):
    tokens, units = grads[0].shape
    depth = weights.shape[0]
    tile = 256
    half = pl.BlockSpec((tokens // 2, tile), lambda j: (0, j))
    return pl.pallas_call(
        functools.partial(ffn_back_kernel, len(grads)),
        grid=(depth // tile,),
        in_specs=[pl.BlockSpec((tokens, units), lambda j: (0, 0)) for _ in grads]
        + [pl.BlockSpec((tile, units), lambda j, c=c: (j, c)) for c in columns],
        out_specs=[half, half],
        out_shape=[
            jax.ShapeDtypeStruct((tokens // 2, depth), F32),
            jax.ShapeDtypeStruct((tokens // 2, depth), BF16),
        ],
        compiler_params=pltpu.CompilerParams(vmem_limit_bytes=VMEM_LIMIT),
        cost_estimate=dense_cost(2 * len(grads) * tokens * depth * units, weights),
        name="ffn_back",
    )(*grads, *[weights for _ in columns])


def joint_kernel(count, place_ref, w_ref, *refs):
    parts = refs[: 2 * count - 1]
    out_ref, rows_ref, semaphores = refs[2 * count - 1 :]

    @pl.when(pl.program_id(0) == 0)
    def _():
        fetch_hops(count, place_ref[0], parts, rows_ref, semaphores)

    out_ref[...] = mul(rows_ref[...], w_ref[...], 1, 0)


def joint(place, own, ups, downs, weight):
    size, depth = own.shape
    count = len(ups) + 1
    tokens, wide = size * count, weight.shape[1]
    tile = min(wide, 512)
    outs = [
        jax.ShapeDtypeStruct((tokens, wide), F32),
        jax.ShapeDtypeStruct((tokens, depth), BF16),
    ]
    return pl.pallas_call(
        functools.partial(joint_kernel, count),
        grid_spec=pltpu.PrefetchScalarGridSpec(
            num_scalar_prefetch=1,
            grid=(wide // tile,),
            in_specs=[pl.BlockSpec((depth, tile), lambda j, place: (0, j))]
            + [pl.BlockSpec(memory_space=pl.ANY)] * (2 * count - 1),
            out_specs=[
                pl.BlockSpec((tokens, tile), lambda j, place: (0, j)),
                pl.BlockSpec((tokens, depth), lambda j, place: (0, 0)),
            ],
            scratch_shapes=[pltpu.SemaphoreType.DMA((count,))],
        ),
        out_shape=outs,
        compiler_params=pltpu.CompilerParams(vmem_limit_bytes=VMEM_LIMIT),
        cost_estimate=dense_cost(2 * tokens * depth * wide, weight, *outs),
        name="joint",
    )(place, weight, own, *ups, *downs)


def mixer_out_kernel(grad_ref, w_ref, normed_ref, gain_ref, sum_ref, own_ref, *other_refs):
    total = mul(grad_ref[...], w_ref[:, : grad_ref.shape[1]], 1, 1)
    size = own_ref.shape[0]
    own_ref[...] = total[:size]
    for hop, ref in enumerate(other_refs, 1):
        ref[...] = total[hop * size : (hop + 1) * size].astype(BF16)
    sums = jnp.sum(total * normed_ref[...].astype(F32), axis=0, keepdims=True) / gain_ref[...]
    sum_ref[...] = jnp.broadcast_to(sums, sum_ref.shape)


def mixer_out(grad, weights, normed, gain, size):
    tokens, wide = grad.shape
    depth = weights.shape[0]
    tile = 256
    outs = [jax.ShapeDtypeStruct((8, depth), F32), jax.ShapeDtypeStruct((size, depth), F32)]
    outs += [jax.ShapeDtypeStruct((size, depth), BF16)] * (tokens // size - 1)
    return pl.pallas_call(
        mixer_out_kernel,
        grid=(depth // tile,),
        in_specs=[
            pl.BlockSpec((tokens, wide), lambda j: (0, 0)),
            pl.BlockSpec((tile, weights.shape[1]), lambda j: (j, 0)),
            pl.BlockSpec((tokens, tile), lambda j: (0, j)),
            pl.BlockSpec((1, tile), lambda j: (0, j)),
        ],
        out_specs=[pl.BlockSpec((o.shape[0], tile), lambda j: (0, j)) for o in outs],
        out_shape=outs,
        compiler_params=pltpu.CompilerParams(vmem_limit_bytes=VMEM_LIMIT),
        cost_estimate=dense_cost(2 * tokens * depth * wide, grad, weights, normed, *outs),
        name="mixer_out",
    )(grad, weights, normed, gain)


def outer_kernel(pairs, rider_at, *refs):
    out_ref = refs[-1]
    at = 0
    for left, right, start, wide in pairs:
        value = mul(refs[left][...], refs[right][:, start : start + wide], 0, 0)
        out_ref[:, at : at + wide] = value.astype(BF16)
        at += wide
    if rider_at is not None:
        riders = refs[-2][...]
        rows = riders.shape[0]
        for k in range(out_ref.shape[0] // rows):
            block = out_ref[k * rows : (k + 1) * rows, rider_at : rider_at + LANES]
            out_ref[k * rows : (k + 1) * rows, rider_at : rider_at + LANES] = block + riders


def weight_grads(pairs, riders=None, rider_at=None):
    operands = []

    def position(array):
        for i, held in enumerate(operands):
            if held is array:
                return i
        operands.append(array)
        return len(operands) - 1

    lefts = [position(left) for left, _, _, _ in pairs]
    n_left = len(operands)
    rights = [position(right) for _, right, _, _ in pairs]
    plan = [(l, r, p[2], p[3]) for l, r, p in zip(lefts, rights, pairs)]
    tokens, depth = operands[0].shape
    wide = sum(p[3] for p in pairs)
    tile = 256
    operands += [] if riders is None else [riders]
    specs = [pl.BlockSpec((a.shape[0], tile), lambda j: (0, j)) for a in operands[:n_left]] + [
        pl.BlockSpec(a.shape, lambda j: (0, 0)) for a in operands[n_left:]
    ]
    out = jax.ShapeDtypeStruct((depth, wide), BF16)
    return pl.pallas_call(
        functools.partial(outer_kernel, plan, rider_at),
        grid=(depth // tile,),
        in_specs=specs,
        out_specs=pl.BlockSpec((tile, wide), lambda j: (j, 0)),
        out_shape=out,
        compiler_params=pltpu.CompilerParams(vmem_limit_bytes=VMEM_LIMIT),
        cost_estimate=dense_cost(2 * tokens * depth * wide, out, *operands),
        name="weight_grads",
    )(*operands)


def unpack_kernel(places, q_heads, heads, gain_columns, count, place_ref, *refs):
    arrays = 2 * count - 1
    groups = [refs[i : i + arrays] for i in range(0, len(refs) - 4, arrays)]
    mix_ref, attn_ref, ssm_ref, extra_ref = refs[-4:]
    place = place_ref[0]
    q_wide, z_wide = q_heads * HEAD_SIZE, heads * MIXER_HEAD_SIZE
    group = QUERY_HEADS // KEY_VALUE_HEADS
    key_at = QUERY_HEADS * HEAD_SIZE
    kv_wide = KEY_VALUE_HEADS * HEAD_SIZE
    z_at = key_at + 2 * kv_wide
    x_at = z_at + MIXER_HEADS * MIXER_HEAD_SIZE
    b_at = x_at + MIXER_HEADS * MIXER_HEAD_SIZE
    step = mix_ref.shape[0]
    lane = lax.broadcasted_iota(jnp.int32, (step, LANES), 1)
    head_lane = heads + gain_columns
    head_at = MIXER_HEADS + gain_columns
    shared = jnp.zeros((step, 2 * STATE_SIZE), F32)
    extra = jnp.zeros((step, LANES), F32)
    mix_ref[:, key_at : key_at + 2 * kv_wide] = jnp.zeros((step, 2 * kv_wide), F32)

    for hop in range(count):
        source = lax.rem(place - hop + count, count)

        def of(name, hop=hop):
            group, start, wide = places[name]
            parts = groups[group]
            if hop == 0:
                return parts[0][:, start : start + wide].astype(F32)
            up = parts[hop][:, start : start + wide].astype(F32)
            down = parts[2 * count - 1 - hop][:, start : start + wide].astype(F32)
            return jnp.where(place >= hop, up, down)

        def put(ref, start, value):
            ref[:, pl.ds(pl.multiple_of(start, LANES), value.shape[1])] = value

        put(mix_ref, source * q_wide, of("q"))
        put(mix_ref, z_at + source * z_wide, of("z"))
        put(mix_ref, x_at + source * z_wide, of("x"))
        put(attn_ref, source * q_wide, of("attn"))
        put(ssm_ref, source * z_wide, of("ssm"))
        shared = shared + of("bc")
        which = lax.div(source * q_heads, group)
        for name, base in (("k", key_at), ("v", key_at + kv_wide)):
            at = pl.ds(pl.multiple_of(base + which * HEAD_SIZE, LANES), HEAD_SIZE)
            mix_ref[:, at] += of(name)
        small = of("dt")
        own = jnp.where(lane < heads, small, 0.0)
        gains = jnp.where((lane >= heads) & (lane < head_lane), small, 0.0)
        column = jnp.where(lane == head_lane, small, 0.0)
        extra = (
            extra
            + pltpu.roll(own, source * heads, 1)
            + pltpu.roll(gains, MIXER_HEADS - heads, 1)
            + pltpu.roll(column, head_at - head_lane + source, 1)
        )
    mix_ref[:, b_at:] = shared
    extra_ref[...] = extra


def unpack_mixer(place, groups, places, q_heads, heads, gain_columns):
    count = len(groups[0][1]) + 1
    rows = groups[0][0].shape[0]
    step = min(rows, 128)
    widths = (
        QUERY_HEADS * HEAD_SIZE
        + 2 * KEY_VALUE_HEADS * HEAD_SIZE
        + 2 * MIXER_HEADS * MIXER_HEAD_SIZE
        + 2 * STATE_SIZE,
        QUERY_HEADS * HEAD_SIZE,
        MIXER_HEADS * MIXER_HEAD_SIZE,
        LANES,
    )
    operands = [part for own, ups, downs in groups for part in (own, *ups, *downs)]

    def spec(columns):
        return pl.BlockSpec((step, columns), lambda i, place: (i, 0))

    return pl.pallas_call(
        functools.partial(unpack_kernel, places, q_heads, heads, gain_columns, count),
        grid_spec=pltpu.PrefetchScalarGridSpec(
            num_scalar_prefetch=1,
            grid=(rows // step,),
            in_specs=[spec(o.shape[1]) for o in operands],
            out_specs=[spec(w) for w in widths],
        ),
        out_shape=[jax.ShapeDtypeStruct((rows, w), F32) for w in widths],
        compiler_params=pltpu.CompilerParams(vmem_limit_bytes=VMEM_LIMIT),
        cost_estimate=pl.CostEstimate(
            flops=100_000_000, bytes_accessed=26_000_000, transcendentals=0
        ),
        name="unpack_mixer",
    )(place, *operands)


def unpack_ffn_kernel(count, place_ref, *refs):
    arrays = 2 * count - 1
    groups = (refs[:arrays], refs[arrays : 2 * arrays])
    outs = refs[2 * arrays :]
    place = place_ref[0]
    chunk = groups[0][0].shape[0]
    half = outs[0].shape[1] // 2
    quarter = half // 2
    pieces = (
        (0, 0, 0, half, 0),
        (1, 0, half, quarter, 0),
        (1, 1, 0, quarter, quarter),
        (2, 1, quarter, half, 0),
    )
    for hop in range(count):
        source = lax.rem(place - hop + count, count)
        row = pl.multiple_of(lax.div(source, 2) * chunk, chunk)
        side = lax.rem(source, 2) * half
        for out, group, start, wide, offset in pieces:
            parts = groups[group]
            value = parts[0][:, start : start + wide] if hop == 0 else None
            if hop:
                up = parts[hop][:, start : start + wide]
                down = parts[arrays - hop][:, start : start + wide]
                value = jnp.where(place >= hop, up.astype(F32), down.astype(F32))
            column = pl.multiple_of(side + offset, LANES)
            outs[out][pl.ds(row, chunk), pl.ds(column, wide)] = value.astype(F32)


def unpack_ffn(place, groups, units):
    count = len(groups[0][1]) + 1
    rows = groups[0][0].shape[0] * (count // 2)
    operands = [part for own, ups, downs in groups for part in (own, *ups, *downs)]

    def fixed(shape):
        return pl.BlockSpec(shape, lambda i, place: (0, 0))

    return pl.pallas_call(
        functools.partial(unpack_ffn_kernel, count),
        grid_spec=pltpu.PrefetchScalarGridSpec(
            num_scalar_prefetch=1,
            grid=(1,),
            in_specs=[fixed(o.shape) for o in operands],
            out_specs=[fixed((rows, units))] * 3,
        ),
        out_shape=[jax.ShapeDtypeStruct((rows, units), F32)] * 3,
        compiler_params=pltpu.CompilerParams(vmem_limit_bytes=VMEM_LIMIT),
        cost_estimate=pl.CostEstimate(
            flops=100_000_000, bytes_accessed=22_000_000, transcendentals=0
        ),
        name="unpack_ffn",
    )(place, *operands)


def norm_back_kernel(grad_ref, swap_ref, rows_ref, gain_ref, base_ref, out_ref, low_ref, sum_ref):
    grad = grad_ref[...] + swap_ref[...].astype(F32)
    rows = rows_ref[...]
    inverse = lax.rsqrt(jnp.mean(rows * rows, axis=-1, keepdims=True) + EPSILON)
    unit = rows * inverse
    scaled = grad * gain_ref[...]
    out = base_ref[...].astype(F32) + inverse * (
        scaled - unit * jnp.mean(unit * scaled, axis=-1, keepdims=True)
    )
    out_ref[...] = out
    low_ref[...] = out.astype(BF16)

    @pl.when(pl.program_id(0) == 0)
    def _():
        sum_ref[...] = jnp.zeros_like(sum_ref)

    sum_ref[...] += jnp.broadcast_to(jnp.sum(grad * unit, axis=0, keepdims=True), sum_ref.shape)


def norm_back(grad, swap, rows, gain, base):
    size, depth = rows.shape
    step = min(size, 64)
    tile = pl.BlockSpec((step, depth), lambda i: (i, 0))
    fixed = lambda i: (0, 0)
    outs = [
        jax.ShapeDtypeStruct((size, depth), F32),
        jax.ShapeDtypeStruct((size, depth), BF16),
        jax.ShapeDtypeStruct((8, depth), F32),
    ]
    return pl.pallas_call(
        norm_back_kernel,
        grid=(size // step,),
        in_specs=[tile, tile, tile, pl.BlockSpec((1, depth), fixed), tile],
        out_specs=[tile, tile, pl.BlockSpec((8, depth), fixed)],
        out_shape=outs,
        compiler_params=pltpu.CompilerParams(vmem_limit_bytes=VMEM_LIMIT),
        cost_estimate=dense_cost(20 * size * depth, grad, swap, rows, *outs),
        name="norm_back",
    )(grad, swap, rows, gain, base)


def per_device(
    hidden_in,
    w_mix,
    w_dt,
    w_attn_out,
    w_ssm_out,
    w_gate,
    w_up,
    w_down,
    norm_gains,
    dt_bias,
    a_log,
    skip_scale,
    cotangent,
):
    w_mix, w_dt, w_attn_out, w_ssm_out = w_mix[0], w_dt[0], w_attn_out[0], w_ssm_out[0]
    w_gate, w_up, w_down = w_gate[0], w_up[0], w_down[0]
    gain_mix, gain_ffn = norm_gains[0, 0], norm_gains[0, 1]
    count, place = lax.axis_size("ctx"), lax.axis_index("ctx")
    piece, width = hidden_in.shape[1], hidden_in.shape[2]
    tokens = piece * count
    rows = w_mix.shape[0]
    hidden_units = w_gate.shape[1]
    q_heads = QUERY_HEADS // count
    group = QUERY_HEADS // KEY_VALUE_HEADS
    kv_head = (place * q_heads) // group
    heads = MIXER_HEADS // count
    q_wide, z_wide = q_heads * HEAD_SIZE, heads * MIXER_HEAD_SIZE
    key_at = QUERY_HEADS * HEAD_SIZE
    value_at = key_at + KEY_VALUE_HEADS * HEAD_SIZE
    z_at = value_at + KEY_VALUE_HEADS * HEAD_SIZE
    x_at = z_at + MIXER_HEADS * MIXER_HEAD_SIZE
    b_at = x_at + MIXER_HEADS * MIXER_HEAD_SIZE
    names = ("q", "k", "v", "z", "x", "b", "c", "dt")
    sizes = (q_wide, HEAD_SIZE, HEAD_SIZE, z_wide, z_wide, STATE_SIZE, STATE_SIZE, LANES)
    cuts, mix_wide = {}, 0
    for name, size in zip(names, sizes):
        cuts[name] = mix_wide
        mix_wide += size

    half = place % 2
    half_units = hidden_units // 2
    own_dt = lax.dynamic_slice(w_dt, (0, place * heads), (rows, heads))
    own_dt = jnp.pad(own_dt, ((0, 0), (0, LANES - heads)))
    here = jnp.reshape(place, (1,)).astype(jnp.int32)
    mix_starts = (
        (place * q_wide, q_wide),
        (key_at + kv_head * HEAD_SIZE, HEAD_SIZE),
        (value_at + kv_head * HEAD_SIZE, HEAD_SIZE),
        (z_at + place * z_wide, z_wide),
        (x_at + place * z_wide, z_wide),
        (b_at + 0 * place, 2 * STATE_SIZE),
    )
    from_half = (half * half_units, half_units)
    (mixer_own,) = pack_columns(
        (w_mix, own_dt, w_attn_out, w_ssm_out),
        (
            [(0,) + cut for cut in mix_starts]
            + [(1, 0 * place, LANES), (2, place * q_wide, q_wide), (3, place * z_wide, z_wide)],
        ),
    )
    hidden_own = hidden_in.reshape(piece, width)
    hidden_line = Chain(line_gather(hidden_own))
    advance(hidden_line)
    late_down = after(w_down, *[value for value, _ in hidden_line.sends])
    (ffn_own,) = pack_columns(
        (w_gate, w_up, late_down), ([(2,) + from_half, (0,) + from_half, (1,) + from_half],)
    )
    (ffn_own,) = advance(hidden_line, beside=(ffn_own,))
    w_mixer, w_ffn = gather_rows(mixer_own), gather_rows(ffn_own)
    w_out = w_mixer[:, mix_wide:]
    w_down_half = w_ffn[:, :half_units]

    blocks = tokens // piece

    while live(hidden_line):
        advance(hidden_line)
    hidden_ups, hidden_downs = hidden_line.result
    mixed, normed = mixer_in(
        here, hidden_own, hidden_ups, hidden_downs, gain_mix[None, :], w_mixer, mix_wide
    )
    own = [lax.dynamic_slice_in_dim(p[0], place * heads, heads) for p in (dt_bias, a_log, skip_scale)]
    tables = mixer_tables(tokens, piece, heads, *own)
    branch_in, states, keys, values = mixer_forward(
        here, mixed, tables, cuts, q_heads, heads, blocks
    )
    cot_own = cotangent.reshape(piece, width)
    cot_swap = swap_pair(after(cot_own, hidden_ups[-1], hidden_downs[-1]))
    branch_in, cot_swap = lax.optimization_barrier((branch_in, cot_swap))
    cot_pair = jnp.concatenate([cot_own, cot_swap], axis=0)
    halves, ready = [], branch_in
    for half_rows in (w_out[: width // 2], w_out[width // 2 :]):
        terms = [None] * count

        def branch_term(rows_in, hop, half_rows=half_rows):
            return dot(rows_in[hop * piece : (hop + 1) * piece], half_rows, 1, 1)

        for hop in (1, count - 1):
            terms[hop] = branch_term(ready, hop)
        branch_line = Chain(line_sum(terms))
        flight = Flight(branch_line)
        late_in = ready = after(branch_in, *flight.values)
        for hop in range(count):
            if terms[hop] is None:
                terms[hop] = branch_term(late_in, hop)
        halves.append((branch_line, flight))
    for branch_line, flight in halves:
        flight.land()
    for branch_line, _ in halves:
        while live(branch_line):
            advance(branch_line)
    branch = jnp.concatenate([branch_line.result for branch_line, _ in halves], axis=1)
    middle = hidden_own.astype(F32) + branch
    grad_act = dot(cot_pair, w_down_half, 1, 0)

    inverse_ffn = inverse_rms(middle)
    normed_ffn = (middle * inverse_ffn * gain_ffn).astype(BF16)
    normed_swap, grad_act = lax.optimization_barrier((swap_pair(normed_ffn), grad_act))
    activated, grad_gate, grad_up, normed_pair = ffn_inner(
        normed_ffn, normed_swap, grad_act, w_ffn
    )
    grad_normed_own, grad_normed_other = ffn_back((grad_gate, grad_up), w_ffn, (1, 2))
    grad_swap = swap_pair(grad_normed_other)
    activated, grad_gate, grad_up = lax.optimization_barrier(
        (activated, grad_gate, grad_up, grad_normed_other)
    )[:3]
    quarter = half_units // 2
    grad_w_first = weight_grads(
        ((normed_pair, grad_gate, 0, half_units), (normed_pair, grad_up, 0, quarter))
    )
    grad_swap, grad_w_first = lax.optimization_barrier((grad_swap, grad_w_first))
    grad_w_first = scatter_rows(grad_w_first)

    grad_middle, branch_own, gain_ffn_rows = norm_back(
        grad_normed_own, grad_swap, middle, gain_ffn[None, :], cot_own
    )
    branch_line = Chain(line_gather(branch_own))
    late_activated, late_up = lax.optimization_barrier((activated, grad_up, branch_own))[:2]
    grad_w_second = weight_grads(
        ((normed_pair, late_up, quarter, quarter), (cot_pair, late_activated, 0, half_units))
    )
    (grad_w_second,) = advance(branch_line, beside=(grad_w_second,))
    out_half, out_other = ffn_back((after(activated, grad_w_second),), w_ffn, (0,))
    grad_w_second = scatter_rows(grad_w_second)
    out_half, out_other = advance(branch_line, beside=(out_half, out_other))
    while branch_line.sends is not None:
        advance(branch_line)
    grad_joint, grad_branch = joint(here, branch_own, *branch_line.result, w_out)
    out_swap = swap_pair(after(out_other, *branch_line.result[0]))
    first = Chain(parity_gather(grad_w_first))

    grad_mixed, head_part = mixer_backward(
        here, mixed, grad_joint, states, keys, values, tables, cuts, q_heads, heads, blocks
    )
    grad_mixed, head_part, out_swap = advance(first, beside=(grad_mixed, head_part, out_swap))
    gain_rows, *dn_parts = mixer_out(grad_mixed, w_mixer, normed, gain_mix[None, :], piece)
    gain_rows, *dn_parts = advance(first, beside=(gain_rows, *dn_parts))

    gain_columns = 2 * width // rows
    riders = jnp.concatenate(
        [
            jnp.zeros((rows, heads), F32),
            jnp.stack([gain_rows[0], gain_ffn_rows[0]]).reshape(rows, gain_columns),
            jnp.pad(head_part[:3, :heads].reshape(3 * heads), (0, rows - 3 * heads))[:, None],
            jnp.zeros((rows, LANES - heads - gain_columns - 1), F32),
        ],
        axis=1,
    )
    grad_w_mixer = weight_grads(
        ((normed, grad_mixed, 0, mix_wide), (grad_branch, branch_in, 0, q_wide + z_wide)),
        riders.astype(BF16),
        cuts["dt"],
    )
    normed_sum = Chain(line_sum(dn_parts))
    (grad_w_mixer,) = advance(first, normed_sum, beside=(grad_w_mixer,))
    grad_w_mixer = scatter_rows(after(grad_w_mixer, grad_w_second))
    second = Chain(parity_gather(grad_w_second))
    advance(*live(second, first))
    while live(normed_sum):
        advance(*live(second, first, normed_sum))
    mixer = Chain(line_gather(after(grad_w_mixer, normed_sum.result)))
    while live(second, first):
        advance(*live(mixer, second, first))

    sealed = lax.optimization_barrier(
        (first.result, second.result, tuple(value for value, _ in mixer.sends))
    )
    outs = tuple(unpack_ffn(here, sealed[:2], hidden_units))
    outs = advance(*live(mixer), beside=outs)
    sealed = lax.optimization_barrier(
        (normed_sum.result, out_swap, tuple(value for value, _ in mixer.sends))
    )
    hidden_out = (middle + (out_half + sealed[1].astype(F32))).astype(BF16)
    hidden_f32 = hidden_own.astype(F32)
    grad_hidden = grad_middle + rms_pull(
        hidden_f32, inverse_rms(hidden_f32), gain_mix, sealed[0]
    )
    hidden_out, grad_hidden = advance(mixer, beside=(hidden_out, grad_hidden))
    while live(mixer):
        advance(mixer)
    out_gate, out_up, out_down = outs

    places = {name: (0, cuts[name], size) for name, size in zip(names, sizes)}
    places["bc"] = (0, cuts["b"], 2 * STATE_SIZE)
    places["attn"] = (0, mix_wide, q_wide)
    places["ssm"] = (0, mix_wide + q_wide, z_wide)
    out_mix, out_attn, out_ssm, extra = unpack_mixer(
        here, ((grad_w_mixer,) + mixer.result,), places, q_heads, heads, gain_columns
    )
    head_at = MIXER_HEADS + gain_columns
    gain_sums = extra[:, MIXER_HEADS:head_at].reshape(norm_gains.shape)
    head_sums = extra[: 3 * heads, head_at : head_at + count].reshape(3, heads, count)
    head_sums = jnp.swapaxes(head_sums, 1, 2).reshape(3, MIXER_HEADS)

    return (
        hidden_out.reshape(hidden_in.shape),
        grad_hidden.reshape(hidden_in.shape),
        out_mix[None],
        extra[None, :, :MIXER_HEADS],
        out_attn[None],
        out_ssm[None],
        out_gate[None],
        out_up[None],
        out_down[None],
        gain_sums,
        head_sums[0][None],
        head_sums[1][None],
        head_sums[2][None],
    )


def solution(mesh):
    split, rows = P("fsdp", "ctx", None), P(None, "fsdp", None)
    return jax.shard_map(
        per_device,
        mesh=mesh,
        in_specs=(split,) + (rows,) * 7 + (P(),) * 4 + (split,),
        out_specs=(split, split) + (rows,) * 7 + (P(),) * 4,
        check_vma=False,
    )
```
